256 devices in a mesh: dp: 16 (over z_lo, x, core), expert: 16 (over z_hi, y).
Axes of the slice: x: 4, y: 4, z: 8 (z_hi: 4, z_lo: 2; z = z_hi * 2 + z_lo), core: 2. Of those that a mesh axis runs over, the one named last changes fastest.
Arguments:
- tokens: bfloat16 [32768, 3584], P(('dp', 'expert')), may hold values from -6 to 6
- out_grad: bfloat16 [32768, 3584], P(('dp', 'expert')), may hold values from -6 to 6
- routes: int32 [32768, 2], P(('dp', 'expert')), may hold values from 0 to 15, all different within a row; in each aligned block of 128 rows (0 to 127, 128 to 255, ...) at most 20 rows name the same one
- probs: bfloat16 [32768, 2], P(('dp', 'expert')), may hold values from 0.099609375 to 1
- swap_flags: int32 [16], replicated, may hold values from 0 to 1, as said below
- up_weight: bfloat16 [16, 1024, 3584], P('expert', 'dp'), may hold values from -4 to 4
- down_weight: bfloat16 [16, 1024, 3584], P('expert', 'dp'), may hold values from -4 to 4
- up_first: float32 [16, 1024, 3584], P('expert', 'dp'), may hold values from -3 to 3
- up_second: float32 [16, 1024, 3584], P('expert', 'dp'), may hold values from 0.02 to 0.3
- down_first: float32 [16, 1024, 3584], P('expert', 'dp'), may hold values from -3 to 3
- down_second: float32 [16, 1024, 3584], P('expert', 'dp'), may hold values from 0.02 to 0.3
Outputs:
- token_grad: bfloat16 [32768, 3584], P(('dp', 'expert'))
- new_up_weight: bfloat16 [16, 1024, 3584], P('expert', 'dp')
- new_down_weight: bfloat16 [16, 1024, 3584], P('expert', 'dp')
- new_up_first: float32 [16, 1024, 3584], P('expert', 'dp')
- new_up_second: float32 [16, 1024, 3584], P('expert', 'dp')
- new_down_first: float32 [16, 1024, 3584], P('expert', 'dp')
- new_down_second: float32 [16, 1024, 3584], P('expert', 'dp')
The draws below stay inside these ranges and needn't reach their ends.
Inputs may be any that keep to these rules, and one draw needn't show every extreme that they name: `routes`: each row names 2 different experts. Within the 128 rows of one device no expert is named by more than 20 rows, a bound that some block reaches. swap_flags[s] equals swap_flags[s XOR (8)]; the slots 16 // 2 - 1 and 15 always trade places.
All inputs are finite; a program needn't handle non-finite values.
Results may differ from the reference program's by a relative error of at most 0.022.
Values may be sent and summed in bfloat16 or wider, within the bound.
No kernel may reach another device: no remote copies, remote signals or barrier semaphores. Data moves between devices by JAX's collectives and lax.ppermute only.
A program may use at most 128 MiB of HBM per device.

```python
import math
import jax
import jax.numpy as jnp
import numpy as np
from jax import lax

D = 3584
F = 1024
TOK_DEV = 128
TOP = 2
ADAM_STEP = 20
EXPERTS = 16
REPLICAS = 16
CAP = 20
TOKENS = 32768


def draw_swap_flags(key, part):
    key = jax.random.fold_in(key, 11)
    half_axis = EXPERTS // 2
    pair_bits = jax.random.randint(key, (half_axis,), 0, 2)
    positions = jnp.arange(half_axis)
    pair_bits = jnp.where(positions == half_axis - 1, 1, pair_bits)
    return jnp.concatenate([pair_bits, pair_bits]).astype(jnp.int32)


def levels(rng, shape, shards, least, high):
    gain = 1.0
    for axis_at, parts in shards:
        steps = jax.random.uniform(jax.random.fold_in(jax.random.fold_in(rng, 6), axis_at), (parts,), jnp.float32, least / len(shards), high / len(shards))
        gain = gain * jnp.repeat(jnp.exp(steps), shape[axis_at] // parts).reshape((-1,) + (1,) * (len(shape) - 1 - axis_at))
    return gain


def shared_out(stream_key, own, number, rows, number_of, top, bound, slope):
    order = jax.random.permutation(stream_key, number_of)
    heavy_load, ordinary = load_shares(number_of, rows * top, bound, slope, True), load_shares(number_of, rows * top, bound, slope, False)
    places = jnp.arange(number_of)

    def named(tallies, rotation):
        used = int((tallies > 0).sum())
        fixed = max(1, used // 4)
        moved = fixed + (places - fixed + rotation * (used - fixed)) % max(1, number_of - fixed)
        return jnp.zeros((number_of,), jnp.int32).at[order[jnp.where(places < fixed, places, moved)]].set(jnp.asarray(tallies, jnp.int32))

    tallies = jnp.where(number % 4 == 0, named(heavy_load, number // 4), named(ordinary, number - number // 4 - 1))
    mixed = jax.random.permutation(jax.random.fold_in(own, 3), number_of)
    source_of, sink = mixed[0:number_of // 2 * 2:2], mixed[1:number_of // 2 * 2:2]
    slack = jnp.minimum(tallies[source_of] - 1, bound - tallies[sink]) // 2
    slack = jnp.where((source_of == order[0]) | (sink == order[0]) | (tallies[sink] == 0), 0, jnp.maximum(slack, 0))
    moved = jax.random.randint(jax.random.fold_in(own, 4), (number_of // 2,), 0, 1 << 20) % (slack + 1)
    tallies = tallies.at[source_of].add(-moved).at[sink].add(moved)
    members = jnp.searchsorted(jnp.cumsum(tallies), jnp.arange(rows * top), side="right").astype(jnp.int32)
    grid = members.reshape(top, rows).T
    grid = grid[jax.random.permutation(jax.random.fold_in(own, 1), rows)]
    rotation = jax.random.randint(jax.random.fold_in(own, 2), (rows, 1), 0, top)
    return jnp.take_along_axis(grid, (jnp.arange(top)[None, :] + rotation) % top, axis=1)


def load_shares(number_of, total, bound, slope, full):
    portions = [(1 << 20) // math.isqrt(standing ** slope) + 1 for standing in range(1, number_of + 1)]
    largest = bound if full else min(bound, max(-(-total // number_of), total * portions[0] // sum(portions)))
    least = 1 if total - largest >= number_of - 1 else 0
    given, surplus = [largest] + [least] * (number_of - 1), total - largest - least * (number_of - 1)
    while surplus > 0:
        movable = [i for i in range(1, number_of) if given[i] < largest] or [i for i in range(1, number_of) if given[i] < bound]
        pool, left = sum([portions[i] for i in movable]), surplus
        for i in movable:
            more = min(bound - given[i], max(1, left * portions[i] // pool), surplus)
            given[i] = given[i] + more
            surplus = surplus - more
    return np.array(given)


def scatter_about(stream_key, dims, deviation, reach, split=(), kind=jnp.bfloat16):
    drawn = deviation * jax.random.normal(stream_key, dims, jnp.float32)
    if split:
        drawn = drawn * levels(stream_key, dims, split, -0.22, 0.18)
    return jnp.clip(drawn, -reach, reach).astype(kind)


def setup_inputs(seed: int = 0) -> dict:
    keys = jax.random.split(jax.random.key(seed), 12)
    tokens = scatter_about(keys[0], (TOKENS, D), 1.0, 6.0, ((0, 256),))
    out_grad = scatter_about(keys[1], (TOKENS, D), 1.0, 6.0, ((0, 256),))
    routes_keys = jax.random.split(jax.random.fold_in(keys[2], 1), TOKENS // TOK_DEV)
    routes_turns = jax.random.permutation(jax.random.fold_in(keys[2], 3), TOKENS // TOK_DEV)
    routes = jax.vmap(lambda own, number: shared_out(jax.random.fold_in(keys[2], 2), own, number, TOK_DEV, EXPERTS, TOP, CAP, 2))(routes_keys, routes_turns).reshape((TOKENS, TOP))
    probs = jnp.clip(0.099609375 + 0.9003906 * jax.random.uniform(keys[3], (TOKENS, TOP), jnp.float32) ** levels(keys[3], (TOKENS, TOP), ((0, 256),), -0.2, 0.2), 0.099609375, 1.0).astype(jnp.bfloat16)
    swap_flags = draw_swap_flags(jax.random.fold_in(keys[11], 71), 0)
    up_weight = scatter_about(keys[5], (EXPERTS, F, D), 1.0, 4.0, ((0, 16), (1, 16)))
    down_weight = scatter_about(keys[6], (EXPERTS, F, D), 1.0, 4.0, ((0, 16), (1, 16)))
    up_first = scatter_about(keys[7], (EXPERTS, F, D), 0.5, 3.0, ((0, 16), (1, 16)), jnp.float32)
    up_second = jnp.clip(jnp.exp(math.log(0.3) - 2.7080503 * jax.random.uniform(keys[8], (EXPERTS, F, D), jnp.float32) ** levels(keys[8], (EXPERTS, F, D), ((0, 16), (1, 16)), -0.2, 0.2)), 0.02, 0.3)
    down_first = scatter_about(keys[9], (EXPERTS, F, D), 0.5, 3.0, ((0, 16), (1, 16)), jnp.float32)
    down_second = jnp.clip(jnp.exp(math.log(0.3) - 2.7080503 * jax.random.uniform(keys[10], (EXPERTS, F, D), jnp.float32) ** levels(keys[10], (EXPERTS, F, D), ((0, 16), (1, 16)), -0.2, 0.2)), 0.02, 0.3)
    return dict(tokens=tokens, out_grad=out_grad, routes=routes, probs=probs, swap_flags=swap_flags, up_weight=up_weight, down_weight=down_weight, up_first=up_first, up_second=up_second, down_first=down_first, down_second=down_second)


beta_first = 0.9
beta_second = 0.95
step_size = 0.05
adam_epsilon = 1e-08

def adam_update(weight, first, second, gradient):
    first_new = beta_first * first + (1.0 - beta_first) * gradient
    second_new = beta_second * second + (1.0 - beta_second) * gradient * gradient
    corr_first = 1.0 - beta_first ** ADAM_STEP
    corr_second = 1.0 - beta_second ** ADAM_STEP
    stepped = weight.astype(jnp.float32) - step_size * (first_new / corr_first) / (jnp.sqrt(second_new / corr_second) + adam_epsilon)
    return (stepped.astype(jnp.bfloat16), first_new, second_new)

def reference(tokens, out_grad, routes, probs, swap_flags, up_weight, down_weight, up_first, up_second, down_first, down_second):
    half_axis = EXPERTS // 2
    expert_ids = jnp.arange(EXPERTS, dtype=jnp.int32)
    new_slot = jnp.where(swap_flags == 1, jnp.bitwise_xor(expert_ids, half_axis), expert_ids).astype(jnp.int32)
    block_rows = TOK_DEV * EXPERTS
    block_pairs = block_rows * TOP
    buffer_rows = EXPERTS * CAP
    inv_model = D ** (-0.5)
    inv_hidden = F ** (-0.5)
    token_blocks = tokens.reshape(REPLICAS, block_rows, D)
    cotan_blocks = out_grad.reshape(REPLICAS, block_rows, D)
    route_blocks = routes.reshape(REPLICAS, block_pairs).astype(jnp.int32)
    prob_blocks = probs.reshape(REPLICAS, block_pairs)

    def one_block(totals, inputs):
        up_total, down_total = totals
        block_tokens, block_cotan, block_routes, block_probs = inputs

        def one_expert(expert):
            order = jnp.argsort((block_routes != expert).astype(jnp.int32), stable=True)[:buffer_rows].astype(jnp.int32)
            valid = block_routes[order] == expert
            token_index = (order // TOP).astype(jnp.int32)
            rows = block_tokens[token_index]
            cotan = block_cotan[token_index]
            row_probs = jnp.where(valid, block_probs[order].astype(jnp.float32), 0.0)
            up_mat = up_weight[expert]
            down_mat = down_weight[expert]
            pre_act = jnp.dot(rows, up_mat.T, preferred_element_type=jnp.float32) * inv_model
            sigmoid_act = jax.nn.sigmoid(pre_act)
            activ = (pre_act * sigmoid_act).astype(jnp.bfloat16)
            back_proj = jnp.dot(cotan, down_mat.T, preferred_element_type=jnp.float32)
            delta = (row_probs[:, None] * back_proj * inv_hidden * sigmoid_act * (1.0 + pre_act * (1.0 - sigmoid_act))).astype(jnp.bfloat16)
            scaled = (row_probs[:, None] * cotan.astype(jnp.float32)).astype(jnp.bfloat16)
            pair_grad = (jnp.dot(delta, up_mat, preferred_element_type=jnp.float32) * inv_model).astype(jnp.bfloat16)
            up_part = (jnp.dot(delta.T, rows, preferred_element_type=jnp.float32) * inv_model).astype(jnp.bfloat16)
            down_part = (jnp.dot(activ.T, scaled, preferred_element_type=jnp.float32) * inv_hidden).astype(jnp.bfloat16)
            return (up_part, down_part, token_index, pair_grad)
        up_parts, down_parts, token_index, pair_grads = lax.map(one_expert, expert_ids)
        grad_block = jnp.zeros((block_rows, D), jnp.float32).at[token_index.reshape(-1)].add(pair_grads.reshape(-1, D).astype(jnp.float32))
        return ((up_total + up_parts.astype(jnp.float32), down_total + down_parts.astype(jnp.float32)), grad_block.astype(jnp.bfloat16))
    start_totals = (jnp.zeros((EXPERTS, F, D), jnp.float32), jnp.zeros((EXPERTS, F, D), jnp.float32))
    totals, grad_blocks = lax.scan(one_block, start_totals, (token_blocks, cotan_blocks, route_blocks, prob_blocks))
    up_grad, down_grad = totals
    token_grad = grad_blocks.reshape(TOKENS, D)
    new_up, up_first_new, up_second_new = adam_update(up_weight, up_first, up_second, up_grad)
    new_down, down_first_new, down_second_new = adam_update(down_weight, down_first, down_second, down_grad)

    def place(array):
        return jnp.take(array, new_slot, axis=0)
    return (token_grad, place(new_up), place(new_down), place(up_first_new), place(up_second_new), place(down_first_new), place(down_second_new))
```

```python
import jax
import jax.numpy as jnp
from jax import lax
from jax.sharding import Mesh
from jax.sharding import PartitionSpec as P

ADAM_STEP = 20


beta_first = 0.9
beta_second = 0.95
step_size = 0.05
adam_epsilon = 1e-08

FAR = "far"
CORE = "core"
EXPERT = "expert"


def partner_2(shard, axis, stride):
    return lax.ppermute(shard, axis, [(i, i ^ 1 << stride) for i in range(lax.axis_size(axis))])


def adam_update(weight, first, second, gradient):
    first_new = beta_first * first + (1.0 - beta_first) * gradient
    second_new = beta_second * second + (1.0 - beta_second) * gradient * gradient
    corr_first = 1.0 - beta_first**ADAM_STEP
    corr_second = 1.0 - beta_second**ADAM_STEP
    stepped = weight.astype(jnp.float32) - step_size * (first_new / corr_first) / (
        jnp.sqrt(second_new / corr_second) + adam_epsilon
    )
    return (stepped.astype(jnp.bfloat16), first_new, second_new)


def on_device(
    tokens,
    out_grad,
    routes,
    probs,
    swap_flags,
    up_weight,
    down_weight,
    up_first,
    up_second,
    down_first,
    down_second,
):
    model_width = tokens.shape[1]
    tok_rows, top_count = routes.shape
    experts = lax.axis_size(EXPERT)
    far = lax.axis_size(FAR)
    half_axis = experts // 2
    swap_bit = half_axis.bit_length() - 1
    capacity = max(2, tok_rows * top_count * 5 // (4 * experts))
    buffer_rows = experts * capacity
    local_hidden = up_weight.shape[1]
    hidden_units = local_hidden * far * lax.axis_size(CORE)
    inv_model = model_width ** (-0.5)
    inv_hidden = hidden_units ** (-0.5)
    contract_last = (((1,), (1,)), ((), ()))
    contract_first = (((0,), (0,)), ((), ()))
    my_index = lax.axis_index(EXPERT)
    expert_ids = jnp.arange(experts, dtype=jnp.int32)
    flag_mine = jnp.sum(jnp.where(expert_ids == my_index, swap_flags, 0))
    new_slot = jnp.where(swap_flags == 1, jnp.bitwise_xor(expert_ids, half_axis), expert_ids)
    swapped = flag_mine == 1

    weights = jnp.concatenate((up_weight[0], down_weight[0]), axis=0)
    weights = jnp.where(swapped, partner_2(weights, EXPERT, swap_bit), weights)
    gathered = lax.all_gather(weights, FAR, axis=0)
    up_half = gathered[:, :local_hidden].reshape(far * local_hidden, model_width)
    down_half = gathered[:, local_hidden:].reshape(far * local_hidden, model_width)

    destination = jnp.sum(
        jnp.where(routes[:, :, None] == expert_ids[None, None, :], new_slot[None, None, :], 0),
        axis=2,
    )
    pair_dest = destination.reshape(-1)
    dest_onehot = (pair_dest[:, None] == expert_ids[None, :]).astype(jnp.int32)
    earlier = jnp.cumsum(dest_onehot, axis=0) - dest_onehot
    position = jnp.sum(earlier * dest_onehot, axis=1)
    buffer_index = pair_dest * capacity + position
    buffer_ids = jnp.arange(buffer_rows, dtype=jnp.int32)
    pair_select = (buffer_ids[:, None] == buffer_index[None, :]).astype(jnp.bfloat16)
    token_select = jnp.sum(pair_select.reshape(buffer_rows, tok_rows, top_count), axis=2)
    prob_select = jnp.sum(
        (pair_select * probs.reshape(1, -1)).reshape(buffer_rows, tok_rows, top_count), axis=2
    )
    send_tokens = jnp.dot(token_select, tokens, preferred_element_type=jnp.float32)
    send_scaled = jnp.dot(prob_select, out_grad, preferred_element_type=jnp.float32)
    send = jnp.concatenate(
        (
            send_tokens.astype(jnp.bfloat16).reshape(experts, capacity, model_width),
            send_scaled.astype(jnp.bfloat16).reshape(experts, capacity, model_width),
        ),
        axis=1,
    )
    got = lax.all_to_all(send, EXPERT, split_axis=0, concat_axis=0, tiled=True)
    other = partner_2(got, CORE, 0)

    def split(block):
        return (
            block[:, :capacity].reshape(buffer_rows, model_width),
            block[:, capacity:].reshape(buffer_rows, model_width),
        )

    def hidden(rows, scaled):
        pre_act = (
            lax.dot_general(rows, up_half, contract_last, preferred_element_type=jnp.float32)
            * inv_model
        )
        back_proj = lax.dot_general(
            scaled, down_half, contract_last, preferred_element_type=jnp.float32
        )
        sigmoid_act = jax.nn.sigmoid(pre_act)
        activ = (pre_act * sigmoid_act).astype(jnp.bfloat16)
        delta = (
            back_proj * inv_hidden * sigmoid_act * (1.0 + pre_act * (1.0 - sigmoid_act))
        ).astype(jnp.bfloat16)
        return activ, delta

    rows_mine, scaled_mine = split(got)
    rows_other, scaled_other = split(other)
    activ_mine, delta_mine = hidden(rows_mine, scaled_mine)
    activ_other, delta_other = hidden(rows_other, scaled_other)
    for_other = (
        jnp.dot(delta_other, up_half, preferred_element_type=jnp.float32) * inv_model
    ).astype(jnp.bfloat16)
    from_other = partner_2(for_other, CORE, 0)
    pair_grad = (
        jnp.dot(delta_mine, up_half, preferred_element_type=jnp.float32) * inv_model
        + from_other.astype(jnp.float32)
    ).astype(jnp.bfloat16)
    half_width = model_width // 2
    returned = lax.all_to_all(
        jnp.concatenate(
            (
                pair_grad[:, :half_width].reshape(experts, capacity, half_width),
                pair_grad[:, half_width:].reshape(experts, capacity, half_width),
            ),
            axis=1,
        ),
        EXPERT,
        split_axis=0,
        concat_axis=0,
        tiled=True,
    )
    token_grad = jnp.concatenate(
        [
            lax.dot_general(
                token_select,
                part.reshape(buffer_rows, half_width),
                contract_first,
                preferred_element_type=jnp.float32,
            ).astype(jnp.bfloat16)
            for part in (returned[:, :capacity], returned[:, capacity:])
        ],
        axis=1,
    )

    def weight_grad(left_mine, right_mine, left_other, right_other, scale):
        total = lax.dot_general(
            left_mine, right_mine, contract_first, preferred_element_type=jnp.float32
        ) + lax.dot_general(
            left_other, right_other, contract_first, preferred_element_type=jnp.float32
        )
        return (total * scale).astype(jnp.bfloat16).reshape(far, local_hidden, model_width)

    up_part = weight_grad(delta_mine, rows_mine, delta_other, rows_other, inv_model)
    down_part = weight_grad(activ_mine, scaled_mine, activ_other, scaled_other, inv_hidden)
    summed = lax.psum_scatter(
        jnp.concatenate((up_part, down_part), axis=1),
        FAR,
        scatter_dimension=0,
        tiled=False,
    ).astype(jnp.float32)

    def moment(array):
        partner = partner_2(array[0].astype(jnp.bfloat16), EXPERT, swap_bit)
        return jnp.where(swapped, partner.astype(jnp.float32), array[0])

    new_up, up_first_new, up_second_new = adam_update(
        weights[:local_hidden], moment(up_first), moment(up_second), summed[:local_hidden]
    )
    new_down, down_first_new, down_second_new = adam_update(
        weights[local_hidden:], moment(down_first), moment(down_second), summed[local_hidden:]
    )
    return (
        token_grad,
        new_up[None],
        new_down[None],
        up_first_new[None],
        up_second_new[None],
        down_first_new[None],
        down_second_new[None],
    )


def solution(mesh):
    dp, expert = (mesh.shape[name] for name in ("dp", "expert"))
    fine = Mesh(mesh.devices.reshape(dp // 2, 2, expert), (FAR, CORE, EXPERT))
    rows = P((FAR, CORE, EXPERT), None)
    slots = P(EXPERT, (FAR, CORE), None)
    return jax.shard_map(
        on_device,
        mesh=fine,
        in_specs=(rows, rows, rows, rows, P()) + (slots,) * 6,
        out_specs=(rows,) + (slots,) * 6,
        check_vma=False,
    )
```

```python
import jax
import jax.numpy as jnp
from jax import lax
from jax.sharding import Mesh
from jax.sharding import PartitionSpec as P

ADAM_STEP = 20


beta_first = 0.9
beta_second = 0.95
step_size = 0.05
adam_epsilon = 1e-08

NEAR = "near"
RING = "ring"
CORE = "core"
EXPERT = "expert"


def partner_2(shard, axis, stride):
    return lax.ppermute(shard, axis, [(i, i ^ 1 << stride) for i in range(lax.axis_size(axis))])


def adam_update(weight, first, second, gradient):
    first_new = beta_first * first + (1.0 - beta_first) * gradient
    second_new = beta_second * second + (1.0 - beta_second) * gradient * gradient
    corr_first = 1.0 - beta_first**ADAM_STEP
    corr_second = 1.0 - beta_second**ADAM_STEP
    stepped = weight.astype(jnp.float32) - step_size * (first_new / corr_first) / (
        jnp.sqrt(second_new / corr_second) + adam_epsilon
    )
    return (stepped.astype(jnp.bfloat16), first_new, second_new)


def on_device(
    tokens,
    out_grad,
    routes,
    probs,
    swap_flags,
    up_weight,
    down_weight,
    up_first,
    up_second,
    down_first,
    down_second,
):
    model_width = tokens.shape[1]
    tok_rows, top_count = routes.shape
    experts = lax.axis_size(EXPERT)
    ring = lax.axis_size(RING)
    near = lax.axis_size(NEAR)
    chips = ring * near
    half_axis = experts // 2
    swap_bit = half_axis.bit_length() - 1
    capacity = max(2, tok_rows * top_count * 5 // (4 * experts))
    buffer_rows = experts * capacity
    local_hidden = up_weight.shape[1]
    hidden_units = local_hidden * chips * lax.axis_size(CORE)
    inv_model = model_width ** (-0.5)
    inv_hidden = hidden_units ** (-0.5)
    contract_last = (((1,), (1,)), ((), ()))
    contract_first = (((0,), (0,)), ((), ()))
    my_index = lax.axis_index(EXPERT)
    expert_ids = jnp.arange(experts, dtype=jnp.int32)
    flag_mine = jnp.sum(jnp.where(expert_ids == my_index, swap_flags, 0))
    new_slot = jnp.where(swap_flags == 1, jnp.bitwise_xor(expert_ids, half_axis), expert_ids)
    swapped = flag_mine == 1

    weights = jnp.concatenate((up_weight[0], down_weight[0]), axis=0)
    weights = jnp.where(swapped, partner_2(weights, EXPERT, swap_bit), weights)
    both = jnp.stack((weights, partner_2(weights, NEAR, 0)), axis=0)
    gathered = lax.all_gather(both, RING, axis=0)
    up_half = gathered[:, :, :local_hidden].reshape(chips * local_hidden, model_width)
    down_half = gathered[:, :, local_hidden:].reshape(chips * local_hidden, model_width)

    destination = jnp.sum(
        jnp.where(routes[:, :, None] == expert_ids[None, None, :], new_slot[None, None, :], 0),
        axis=2,
    )
    pair_dest = destination.reshape(-1)
    dest_onehot = (pair_dest[:, None] == expert_ids[None, :]).astype(jnp.int32)
    earlier = jnp.cumsum(dest_onehot, axis=0) - dest_onehot
    position = jnp.sum(earlier * dest_onehot, axis=1)
    buffer_index = pair_dest * capacity + position
    buffer_ids = jnp.arange(buffer_rows, dtype=jnp.int32)
    pair_select = (buffer_ids[:, None] == buffer_index[None, :]).astype(jnp.bfloat16)
    token_select = jnp.sum(pair_select.reshape(buffer_rows, tok_rows, top_count), axis=2)
    prob_select = jnp.sum(
        (pair_select * probs.reshape(1, -1)).reshape(buffer_rows, tok_rows, top_count), axis=2
    )
    zeros = jnp.zeros((experts, capacity, tok_rows), jnp.bfloat16)
    mixed_select = jnp.concatenate(
        (
            jnp.concatenate((token_select.reshape(zeros.shape), zeros), axis=2),
            jnp.concatenate((zeros, prob_select.reshape(zeros.shape)), axis=2),
        ),
        axis=1,
    ).reshape(2 * buffer_rows, 2 * tok_rows)
    send = (
        jnp.dot(
            mixed_select,
            jnp.concatenate((tokens, out_grad), axis=0),
            preferred_element_type=jnp.float32,
        )
        .astype(jnp.bfloat16)
        .reshape(experts, 2 * capacity, model_width)
    )
    got = lax.all_to_all(send, EXPERT, split_axis=0, concat_axis=0, tiled=True)
    other = partner_2(got, CORE, 0)

    order = jnp.arange(buffer_rows, dtype=jnp.int32)
    place = (order // capacity) * (2 * capacity) + order % capacity
    mixed_ids = jnp.arange(2 * buffer_rows, dtype=jnp.int32)
    pick_rows = (place[:, None] == mixed_ids[None, :]).astype(jnp.bfloat16)
    pick_scaled = (place[:, None] + capacity == mixed_ids[None, :]).astype(jnp.bfloat16)

    def split(block):
        flat = block.reshape(2 * buffer_rows, model_width)
        return tuple(
            jnp.dot(pick, flat, preferred_element_type=jnp.float32).astype(jnp.bfloat16)
            for pick in (pick_rows, pick_scaled)
        )

    def hidden(rows, scaled):
        pre_act = (
            lax.dot_general(rows, up_half, contract_last, preferred_element_type=jnp.float32)
            * inv_model
        )
        back_proj = lax.dot_general(
            scaled, down_half, contract_last, preferred_element_type=jnp.float32
        )
        sigmoid_act = jax.nn.sigmoid(pre_act)
        activ = (pre_act * sigmoid_act).astype(jnp.bfloat16)
        delta = (
            back_proj * inv_hidden * sigmoid_act * (1.0 + pre_act * (1.0 - sigmoid_act))
        ).astype(jnp.bfloat16)
        return activ, delta

    rows_mine, scaled_mine = split(got)
    rows_other, scaled_other = split(other)
    activ_mine, delta_mine = hidden(rows_mine, scaled_mine)
    activ_other, delta_other = hidden(rows_other, scaled_other)
    for_other = (
        jnp.dot(delta_other, up_half, preferred_element_type=jnp.float32) * inv_model
    ).astype(jnp.bfloat16)
    from_other = partner_2(for_other, CORE, 0)
    pair_grad = (
        jnp.dot(delta_mine, up_half, preferred_element_type=jnp.float32) * inv_model
        + from_other.astype(jnp.float32)
    ).astype(jnp.bfloat16)
    half_width = model_width // 2
    returned = lax.all_to_all(
        jnp.concatenate(
            (
                pair_grad[:, :half_width].reshape(experts, capacity, half_width),
                pair_grad[:, half_width:].reshape(experts, capacity, half_width),
            ),
            axis=1,
        ),
        EXPERT,
        split_axis=0,
        concat_axis=0,
        tiled=True,
    )
    token_grad = jnp.concatenate(
        [
            lax.dot_general(
                token_select,
                part.reshape(buffer_rows, half_width),
                contract_first,
                preferred_element_type=jnp.float32,
            ).astype(jnp.bfloat16)
            for part in (returned[:, :capacity], returned[:, capacity:])
        ],
        axis=1,
    )

    def weight_grad(left_mine, right_mine, left_other, right_other, scale):
        total = lax.dot_general(
            left_mine, right_mine, contract_first, preferred_element_type=jnp.float32
        ) + lax.dot_general(
            left_other, right_other, contract_first, preferred_element_type=jnp.float32
        )
        return (total * scale).astype(jnp.bfloat16).reshape(ring, near, local_hidden, model_width)

    up_part = weight_grad(delta_mine, rows_mine, delta_other, rows_other, inv_model)
    down_part = weight_grad(activ_mine, scaled_mine, activ_other, scaled_other, inv_hidden)
    own, beside = lax.psum_scatter(
        jnp.concatenate((up_part, down_part), axis=2), RING, scatter_dimension=0, tiled=False
    )
    summed = own.astype(jnp.float32) + partner_2(beside, NEAR, 0).astype(jnp.float32)
    held, _ = lax.optimization_barrier(
        (
            tuple(
                array[0].astype(jnp.bfloat16)
                for array in (up_first, up_second, down_first, down_second)
            ),
            got,
        )
    )

    def moment(array, rounded):
        partner = partner_2(rounded, EXPERT, swap_bit)
        return jnp.where(swapped, partner.astype(jnp.float32), array[0])

    new_up, up_first_new, up_second_new = adam_update(
        weights[:local_hidden], moment(up_first, held[0]), moment(up_second, held[1]), summed[:local_hidden]
    )
    new_down, down_first_new, down_second_new = adam_update(
        weights[local_hidden:], moment(down_first, held[2]), moment(down_second, held[3]), summed[local_hidden:]
    )
    return (
        token_grad,
        new_up[None],
        new_down[None],
        up_first_new[None],
        up_second_new[None],
        down_first_new[None],
        down_second_new[None],
    )


def solution(mesh):
    dp, expert = (mesh.shape[name] for name in ("dp", "expert"))
    fine = Mesh(mesh.devices.reshape(2, dp // 4, 2, expert), (NEAR, RING, CORE, EXPERT))
    rows = P((NEAR, RING, CORE, EXPERT), None)
    slots = P(EXPERT, (NEAR, RING, CORE), None)
    return jax.shard_map(
        on_device,
        mesh=fine,
        in_specs=(rows, rows, rows, rows, P()) + (slots,) * 6,
        out_specs=(rows,) + (slots,) * 6,
        check_vma=False,
    )
```

```python
import jax
import jax.numpy as jnp
from jax import lax
from jax.sharding import Mesh
from jax.sharding import PartitionSpec as P

ADAM_STEP = 20


beta_first = 0.9
beta_second = 0.95
step_size = 0.05
adam_epsilon = 1e-08

NEAR = "near"
RING = "ring"
CORE = "core"
HIGH = "high"
SIDE = "side"


def partner(array, axis, flip):
    return lax.ppermute(array, axis, [(i, i ^ flip) for i in range(lax.axis_size(axis))])


def shift(array, axis, by):
    size = lax.axis_size(axis)
    return lax.ppermute(array, axis, [(i, (i + by) % size) for i in range(size)])


def gather_high(block):
    half = block.shape[0] // 2
    below = shift(block, HIGH, 1)
    above = shift(block, HIGH, -1)
    return jnp.concatenate(
        (block, below, above, shift(below[:half], HIGH, 1), shift(above[half:], HIGH, -1)), axis=0
    )


def scatter_high(parts):
    own, below, above, far = parts
    half = far.shape[0] // 2
    wide = jnp.float32
    from_below = shift(far[:half].astype(jnp.bfloat16), HIGH, 1).astype(wide)
    from_above = shift(far[half:].astype(jnp.bfloat16), HIGH, -1).astype(wide)
    above = jnp.concatenate((above[:half] + from_below, above[half:]), axis=0)
    below = jnp.concatenate((below[:half], below[half:] + from_above), axis=0)
    return (
        own
        + shift(above.astype(jnp.bfloat16), HIGH, 1).astype(wide)
        + shift(below.astype(jnp.bfloat16), HIGH, -1).astype(wide)
    )


def adam_update(weight, first, second, gradient):
    first_new = beta_first * first + (1.0 - beta_first) * gradient
    second_new = beta_second * second + (1.0 - beta_second) * gradient * gradient
    corr_first = 1.0 - beta_first**ADAM_STEP
    corr_second = 1.0 - beta_second**ADAM_STEP
    stepped = weight.astype(jnp.float32) - step_size * (first_new / corr_first) / (
        jnp.sqrt(second_new / corr_second) + adam_epsilon
    )
    return (stepped.astype(jnp.bfloat16), first_new, second_new)


def on_device(
    tokens,
    out_grad,
    routes,
    probs,
    swap_flags,
    up_weight,
    down_weight,
    up_first,
    up_second,
    down_first,
    down_second,
):
    model_width = tokens.shape[1]
    tok_rows, top_count = routes.shape
    high = lax.axis_size(HIGH)
    side = lax.axis_size(SIDE)
    experts = high * side
    ring = lax.axis_size(RING)
    near = lax.axis_size(NEAR)
    chips = ring * near
    half_axis = experts // 2
    swap_flip = half_axis // side
    capacity = max(2, tok_rows * top_count * 5 // (4 * experts))
    side_rows = high * capacity
    buffer_rows = side * side_rows
    local_hidden = up_weight.shape[1]
    hidden_units = local_hidden * chips * lax.axis_size(CORE)
    inv_model = model_width ** (-0.5)
    inv_hidden = hidden_units ** (-0.5)
    contract_last = (((1,), (1,)), ((), ()))
    contract_first = (((0,), (0,)), ((), ()))
    my_high = lax.axis_index(HIGH)
    my_index = my_high * side + lax.axis_index(SIDE)
    expert_ids = jnp.arange(experts, dtype=jnp.int32)
    flag_mine = jnp.sum(jnp.where(expert_ids == my_index, swap_flags, 0))
    new_slot = jnp.where(swap_flags == 1, jnp.bitwise_xor(expert_ids, half_axis), expert_ids)
    swapped = flag_mine == 1

    destination = jnp.sum(
        jnp.where(routes[:, :, None] == expert_ids[None, None, :], new_slot[None, None, :], 0),
        axis=2,
    )
    pair_dest = destination.reshape(-1)
    dest_onehot = (pair_dest[:, None] == expert_ids[None, :]).astype(jnp.int32)
    earlier = jnp.cumsum(dest_onehot, axis=0) - dest_onehot
    position = jnp.sum(earlier * dest_onehot, axis=1)
    buffer_index = (pair_dest * capacity + position).reshape(tok_rows, top_count)

    plan = jnp.concatenate(
        (buffer_index.astype(jnp.float32).T, probs.astype(jnp.float32).T), axis=0
    )
    plans = lax.all_gather(plan, HIGH, axis=0)
    sources = jnp.stack([(my_high + step) % high for step in (0, high - 1, 1, 2)])
    plans = jnp.take(plans, sources, axis=0)
    local = plans[:, :top_count].astype(jnp.int32) - my_high * (side * capacity)
    valid = (local >= 0) & (local < side * capacity)
    block_ids = jnp.arange(high, dtype=jnp.int32)[:, None, None]
    row = (local // capacity) * side_rows + block_ids * capacity + local % capacity
    row = jnp.where(valid, row, -1)
    buffer_ids = jnp.arange(buffer_rows, dtype=jnp.int32)[:, None, None, None]
    hits = (buffer_ids == row[None]).astype(jnp.bfloat16)
    token_select = jnp.sum(hits, axis=2).reshape(buffer_rows, high * tok_rows)
    prob_select = jnp.sum(
        hits * plans[None, :, top_count:].astype(jnp.bfloat16), axis=2
    ).reshape(buffer_rows, high * tok_rows)

    weights = jnp.concatenate((up_weight[0], down_weight[0]), axis=0)
    weights = jnp.where(swapped, partner(weights, HIGH, swap_flip), weights)
    weights, token_select, prob_select = lax.optimization_barrier(
        (weights, token_select, prob_select)
    )
    both = jnp.stack((weights, partner(weights, NEAR, 1)), axis=0)
    both, tokens, out_grad = lax.optimization_barrier((both, tokens, out_grad))
    gathered = lax.all_gather(both, RING, axis=0)
    up_half = gathered[:, :, :local_hidden].reshape(chips * local_hidden, model_width)
    down_half = gathered[:, :, local_hidden:].reshape(chips * local_hidden, model_width)

    def to_experts(select, block):
        rows = jnp.dot(select, gather_high(block), preferred_element_type=jnp.float32)
        return lax.all_to_all(
            rows.astype(jnp.bfloat16).reshape(side, side_rows, model_width),
            SIDE,
            split_axis=0,
            concat_axis=0,
            tiled=True,
        ).reshape(buffer_rows, model_width)

    rows_mine = to_experts(token_select, tokens)
    scaled_mine = to_experts(prob_select, out_grad)
    rows_other = partner(rows_mine, CORE, 1)
    scaled_other = partner(scaled_mine, CORE, 1)
    moments = (up_first[0], up_second[0], down_first[0], down_second[0])
    held, scaled_mine = lax.optimization_barrier(
        (tuple(array.astype(jnp.bfloat16) for array in moments), scaled_mine)
    )
    arrived = tuple(partner(array, HIGH, swap_flip) for array in held)

    def hidden(rows, scaled):
        pre_act = (
            lax.dot_general(rows, up_half, contract_last, preferred_element_type=jnp.float32)
            * inv_model
        )
        back_proj = lax.dot_general(
            scaled, down_half, contract_last, preferred_element_type=jnp.float32
        )
        sigmoid_act = jax.nn.sigmoid(pre_act)
        activ = (pre_act * sigmoid_act).astype(jnp.bfloat16)
        delta = (
            back_proj * inv_hidden * sigmoid_act * (1.0 + pre_act * (1.0 - sigmoid_act))
        ).astype(jnp.bfloat16)
        return activ, delta

    activ_mine, delta_mine = hidden(rows_mine, scaled_mine)
    activ_other, delta_other = hidden(rows_other, scaled_other)
    for_other = (
        jnp.dot(delta_other, up_half, preferred_element_type=jnp.float32) * inv_model
    ).astype(jnp.bfloat16)
    from_other = partner(for_other, CORE, 1)
    pair_grad = (
        jnp.dot(delta_mine, up_half, preferred_element_type=jnp.float32) * inv_model
        + from_other.astype(jnp.float32)
    ).astype(jnp.bfloat16)
    returned = lax.all_to_all(
        pair_grad.reshape(side, side_rows, model_width),
        SIDE,
        split_axis=0,
        concat_axis=0,
        tiled=True,
    ).reshape(buffer_rows, model_width)
    token_parts = lax.dot_general(
        token_select, returned, contract_first, preferred_element_type=jnp.float32
    ).reshape(high, tok_rows, model_width)
    token_grad = scatter_high(token_parts).astype(jnp.bfloat16)

    def weight_grad(left_mine, right_mine, left_other, right_other, scale):
        total = lax.dot_general(
            left_mine, right_mine, contract_first, preferred_element_type=jnp.float32
        ) + lax.dot_general(
            left_other, right_other, contract_first, preferred_element_type=jnp.float32
        )
        return (total * scale).astype(jnp.bfloat16).reshape(ring, near, local_hidden, model_width)

    up_part = weight_grad(delta_mine, rows_mine, delta_other, rows_other, inv_model)
    down_part = weight_grad(activ_mine, scaled_mine, activ_other, scaled_other, inv_hidden)
    own, beside = lax.psum_scatter(
        jnp.concatenate((up_part, down_part), axis=2), RING, scatter_dimension=0, tiled=False
    )
    summed = own.astype(jnp.float32) + partner(beside, NEAR, 1).astype(jnp.float32)
    moments = tuple(
        jnp.where(swapped, new.astype(jnp.float32), old) for new, old in zip(arrived, moments)
    )
    new_up, up_first_new, up_second_new = adam_update(
        weights[:local_hidden], moments[0], moments[1], summed[:local_hidden]
    )
    new_down, down_first_new, down_second_new = adam_update(
        weights[local_hidden:], moments[2], moments[3], summed[local_hidden:]
    )
    return (
        token_grad,
        new_up[None],
        new_down[None],
        up_first_new[None],
        up_second_new[None],
        down_first_new[None],
        down_second_new[None],
    )


def solution(mesh):
    dp, expert = (mesh.shape[name] for name in ("dp", "expert"))
    fine = Mesh(
        mesh.devices.reshape(2, dp // 4, 2, 4, expert // 4), (NEAR, RING, CORE, HIGH, SIDE)
    )
    rows = P((NEAR, RING, CORE, HIGH, SIDE), None)
    slots = P((HIGH, SIDE), (NEAR, RING, CORE), None)
    return jax.shard_map(
        on_device,
        mesh=fine,
        in_specs=(rows, rows, rows, rows, P()) + (slots,) * 6,
        out_specs=(rows,) + (slots,) * 6,
        check_vma=False,
    )
```

```python
import functools

import jax
import jax.numpy as jnp
from jax import lax
from jax.experimental import pallas as pl
from jax.experimental.pallas import tpu as pltpu
from jax.sharding import Mesh
from jax.sharding import PartitionSpec as P

ADAM_STEP = 20


beta_first = 0.9
beta_second = 0.95
step_size = 0.05
adam_epsilon = 1e-08

NEAR = "near"
RING = "ring"
CORE = "core"
HIGH = "high"
SIDE = "side"
HIGHS = 4


def partner(array, axis, flip):
    return lax.ppermute(array, axis, [(i, i ^ flip) for i in range(lax.axis_size(axis))])


def z_routes():
    routes = []
    for step, crosses in ((1, False), (-1, True), (2, True)):
        pairs = []
        for near in range(2):
            sign = 1 if near == 0 else -1
            for high in range(HIGHS):
                other = (1 - near) if crosses else near
                pairs.append((near * HIGHS + high, other * HIGHS + (high + sign * step) % HIGHS))
        routes.append(pairs)
    return routes


def adam_update(weight, first, second, gradient):
    first_new = beta_first * first + (1.0 - beta_first) * gradient
    second_new = beta_second * second + (1.0 - beta_second) * gradient * gradient
    corr_first = 1.0 - beta_first**ADAM_STEP
    corr_second = 1.0 - beta_second**ADAM_STEP
    stepped = weight.astype(jnp.float32) - step_size * (first_new / corr_first) / (
        jnp.sqrt(second_new / corr_second) + adam_epsilon
    )
    return (stepped.astype(jnp.bfloat16), first_new, second_new)


def dispatch_kernel(
    capacity,
    flags_ref,
    routes_ref,
    probs_ref,
    tokens_ref,
    out_grad_ref,
    token_rows_ref,
    scaled_rows_ref,
    select_ref,
):
    count, tops = routes_ref.shape
    experts = flags_ref.shape[1]
    rows, width = token_rows_ref.shape
    side = experts // HIGHS
    half_axis = experts // 2
    my_high = lax.axis_index(HIGH)
    my_near = lax.axis_index(NEAR)
    ids = lax.broadcasted_iota(jnp.int32, (1, experts), 1)
    slot = jnp.where(flags_ref[...] == 1, jnp.bitwise_xor(ids, half_axis), ids)
    away = lax.shift_right_logical(slot, side.bit_length() - 1) - my_high
    away = jnp.bitwise_and(jnp.where(my_near == 0, away, -away), HIGHS - 1)
    block = jnp.where(away >= 2, 5 - away, away)
    base = jnp.bitwise_and(slot, side - 1) * (HIGHS * capacity) + block * capacity
    base = base.astype(jnp.float32)
    expert_ids = lax.broadcasted_iota(jnp.int32, (count, experts), 1)
    below = (
        lax.broadcasted_iota(jnp.int32, (count, count), 0)
        > lax.broadcasted_iota(jnp.int32, (count, count), 1)
    )
    below = jnp.where(below, 1.0, 0.0).astype(jnp.bfloat16)
    padded = -(-rows // 128) * 128
    row_ids = lax.broadcasted_iota(jnp.int32, (count, padded), 1)
    token_select = jnp.zeros((count, padded), jnp.float32)
    prob_select = jnp.zeros((count, padded), jnp.float32)
    for k in range(tops):
        onehot = jnp.where(routes_ref[:, k : k + 1] == expert_ids, 1.0, 0.0)
        earlier = jnp.dot(below, onehot.astype(jnp.bfloat16), preferred_element_type=jnp.float32)
        row = jnp.sum(onehot * (base + earlier), axis=1, keepdims=True).astype(jnp.int32)
        hit = row_ids == row
        token_select = token_select + jnp.where(hit, 1.0, 0.0)
        prob = probs_ref[:, k : k + 1].astype(jnp.float32)
        prob_select = prob_select + jnp.where(hit, prob, 0.0)
        base = base + jnp.sum(onehot, axis=0, keepdims=True)
    select_ref[...] = token_select[:, :rows].astype(jnp.bfloat16)
    token_pick = token_select.T[:rows].astype(jnp.bfloat16)
    prob_pick = prob_select.T[:rows].astype(jnp.bfloat16)
    piece = 512
    for at in range(0, width, piece):
        cut = slice(at, min(at + piece, width))
        for pick, source, target in (
            (token_pick, tokens_ref, token_rows_ref),
            (prob_pick, out_grad_ref, scaled_rows_ref),
        ):
            target[:, cut] = jnp.dot(
                pick, source[:, cut], preferred_element_type=jnp.float32
            ).astype(jnp.bfloat16)


def dispatch(swap_flags, routes, probs, tokens, out_grad, capacity):
    count, width = tokens.shape
    rows = swap_flags.shape[0] * capacity
    whole = pl.BlockSpec(memory_space=pltpu.VMEM)
    return pl.pallas_call(
        functools.partial(dispatch_kernel, capacity),
        in_specs=[whole] * 5,
        out_specs=[whole] * 3,
        out_shape=[
            jax.ShapeDtypeStruct((rows, width), jnp.bfloat16),
            jax.ShapeDtypeStruct((rows, width), jnp.bfloat16),
            jax.ShapeDtypeStruct((count, rows), jnp.bfloat16),
        ],
        compiler_params=pltpu.CompilerParams(vmem_limit_bytes=24 * 1024 * 1024),
        cost_estimate=pl.CostEstimate(flops=0, bytes_accessed=1024, transcendentals=0),
    )(swap_flags.reshape(1, -1), routes, probs, tokens, out_grad)


def expert_kernel(
    steps,
    inv_model,
    inv_hidden,
    mine_ref,
    other_ref,
    mine_scaled_ref,
    other_scaled_ref,
    weight_ref,
    part_ref,
    pair_ref,
    pair_other_ref,
    pre_ref,
    back_ref,
    delta_ref,
    delta_turned_ref,
    activ_turned_ref,
):
    step = pl.program_id(0)
    chips, both, _ = weight_ref.shape
    local = both // 2
    rows = mine_ref.shape[0]
    contract_last = (((1,), (1,)), ((), ()))
    up = jnp.concatenate([weight_ref[i, :local] for i in range(chips)], axis=0)

    @pl.when(step == 0)
    def _():
        pre_ref[...] = jnp.zeros_like(pre_ref)
        back_ref[...] = jnp.zeros_like(back_ref)

    @pl.when(step < steps)
    def _():
        down = jnp.concatenate([weight_ref[i, local:] for i in range(chips)], axis=0)
        for at, token, scaled in (
            (0, mine_ref, mine_scaled_ref),
            (rows, other_ref, other_scaled_ref),
        ):
            pre_ref[at : at + rows] += lax.dot_general(
                token[...], up, contract_last, preferred_element_type=jnp.float32
            )
            back_ref[at : at + rows] += lax.dot_general(
                scaled[...], down, contract_last, preferred_element_type=jnp.float32
            )

    @pl.when(step == steps - 1)
    def _():
        pre_act = pre_ref[...] * inv_model
        sigmoid_act = 1.0 / (1.0 + jnp.exp(-pre_act))
        delta = (
            back_ref[...] * inv_hidden * sigmoid_act * (1.0 + pre_act * (1.0 - sigmoid_act))
        )
        delta_ref[...] = delta.astype(jnp.bfloat16)
        delta_turned_ref[...] = delta.T.astype(jnp.bfloat16)
        activ_turned_ref[...] = (pre_act * sigmoid_act).T.astype(jnp.bfloat16)

    @pl.when(step >= steps)
    def _():
        for at, turned, mine, other, scale in (
            (0, delta_turned_ref, mine_ref, other_ref, inv_model),
            (local, activ_turned_ref, mine_scaled_ref, other_scaled_ref, inv_hidden),
        ):
            right = jnp.concatenate((mine[...], other[...]), axis=0)
            part = jnp.dot(turned[...], right, preferred_element_type=jnp.float32) * scale
            part = part.astype(jnp.bfloat16)
            for i in range(chips):
                part_ref[i, at : at + local] = part[i * local : (i + 1) * local]
        pair = jnp.dot(delta_ref[...], up, preferred_element_type=jnp.float32) * inv_model
        pair_ref[...] = pair[:rows]
        pair_other_ref[...] = pair[rows:].astype(jnp.bfloat16)


def expert_stage(mine, other, mine_scaled, other_scaled, weights, inv_model, inv_hidden):
    rows, width = mine.shape
    chips, both, _ = weights.shape
    hidden = chips * both // 2
    block = 512
    steps = width // block

    def late(i):
        return jnp.maximum(i - steps, 0)

    row_spec = pl.BlockSpec((rows, block), lambda i: (0, i % steps))
    late_spec = pl.BlockSpec((rows, block), lambda i: (0, late(i)))
    return pl.pallas_call(
        functools.partial(expert_kernel, steps, inv_model, inv_hidden),
        grid=(2 * steps,),
        in_specs=[row_spec] * 4 + [pl.BlockSpec((chips, both, block), lambda i: (0, 0, i % steps))],
        out_specs=[
            pl.BlockSpec((chips, both, block), lambda i: (0, 0, late(i))),
            late_spec,
            late_spec,
        ],
        out_shape=[
            jax.ShapeDtypeStruct(weights.shape, jnp.bfloat16),
            jax.ShapeDtypeStruct((rows, width), jnp.float32),
            jax.ShapeDtypeStruct((rows, width), jnp.bfloat16),
        ],
        scratch_shapes=[
            pltpu.VMEM((2 * rows, hidden), jnp.float32),
            pltpu.VMEM((2 * rows, hidden), jnp.float32),
            pltpu.VMEM((2 * rows, hidden), jnp.bfloat16),
            pltpu.VMEM((hidden, 2 * rows), jnp.bfloat16),
            pltpu.VMEM((hidden, 2 * rows), jnp.bfloat16),
        ],
        compiler_params=pltpu.CompilerParams(
            dimension_semantics=("arbitrary",), vmem_limit_bytes=40 * 1024 * 1024
        ),
        cost_estimate=pl.CostEstimate(flops=0, bytes_accessed=1024, transcendentals=0),
    )(mine, other, mine_scaled, other_scaled, weights)


def on_device(
    tokens,
    out_grad,
    routes,
    probs,
    swap_flags,
    up_weight,
    down_weight,
    up_first,
    up_second,
    down_first,
    down_second,
):
    model_width = tokens.shape[1]
    high = lax.axis_size(HIGH)
    side = lax.axis_size(SIDE)
    experts = high * side
    ring = lax.axis_size(RING)
    near = lax.axis_size(NEAR)
    chips = ring * near
    half_axis = experts // 2
    swap_flip = half_axis // side
    capacity = max(2, routes.size * 5 // (4 * experts))
    side_rows = high * capacity
    high_rows = side * capacity
    buffer_rows = experts * capacity
    local_hidden = up_weight.shape[1]
    hidden_units = local_hidden * chips * lax.axis_size(CORE)
    inv_model = model_width ** (-0.5)
    inv_hidden = hidden_units ** (-0.5)
    my_high = lax.axis_index(HIGH)
    my_index = my_high * side + lax.axis_index(SIDE)
    expert_ids = jnp.arange(experts, dtype=jnp.int32)
    flag_mine = jnp.sum(jnp.where(expert_ids == my_index, swap_flags, 0))
    swapped = flag_mine == 1

    weights = jnp.concatenate((up_weight[0], down_weight[0]), axis=0)
    weights_partner = partner(weights, HIGH, swap_flip)

    send_tokens, send_scaled, token_select = dispatch(
        swap_flags, routes, probs, tokens, out_grad, capacity
    )
    buffer_ids = jnp.arange(buffer_rows, dtype=jnp.int32)
    other_order = (
        (buffer_ids // capacity % high) * side_rows
        + (buffer_ids // side_rows) * capacity
        + buffer_ids % capacity
    )
    regroup = (buffer_ids[None, :] == other_order[:, None]).astype(jnp.bfloat16)

    def along_side(rows):
        return lax.all_to_all(
            rows.reshape(side, side_rows, model_width),
            SIDE,
            split_axis=0,
            concat_axis=0,
            tiled=True,
        ).reshape(buffer_rows, model_width)

    def pick(matrix, rows):
        return jnp.dot(matrix, rows, preferred_element_type=jnp.float32).astype(jnp.bfloat16)

    ways = z_routes()

    def along_high(rows, back):
        blocks = [rows[i * high_rows : (i + 1) * high_rows] for i in range(high)]
        moved = [
            lax.ppermute(
                array, (NEAR, HIGH), [(b, a) for a, b in way] if back else way
            )
            for array, way in zip(blocks[1:], ways)
        ]
        return jnp.concatenate(blocks[:1] + moved, axis=0)

    token_rows = pick(regroup, along_side(send_tokens))
    scaled_rows = pick(regroup, along_side(send_scaled))

    weights = jnp.where(swapped, weights_partner, weights)
    weights, token_rows, scaled_rows = lax.optimization_barrier(
        (weights, token_rows, scaled_rows)
    )
    both = jnp.stack((weights, partner(weights, NEAR, 1)), axis=0)
    gathered = lax.all_gather(both, RING, axis=0).reshape(
        chips, 2 * local_hidden, model_width
    )

    rows_mine = along_high(token_rows, False)
    scaled_mine = along_high(scaled_rows, False)
    rows_other = partner(rows_mine, CORE, 1)
    scaled_other = partner(scaled_mine, CORE, 1)
    moments = (up_first[0], up_second[0], down_first[0], down_second[0])
    held, rows_mine, scaled_mine = lax.optimization_barrier(
        (tuple(array.astype(jnp.bfloat16) for array in moments), rows_mine, scaled_mine)
    )
    arrived = tuple(partner(array, HIGH, swap_flip) for array in held)

    parts, pair_mine, for_other = expert_stage(
        rows_mine, rows_other, scaled_mine, scaled_other, gathered, inv_model, inv_hidden
    )
    from_other = partner(for_other, CORE, 1)
    pair_grad = (pair_mine + from_other.astype(jnp.float32)).astype(jnp.bfloat16)
    arrived, pair_grad = lax.optimization_barrier((arrived, pair_grad))
    returned = along_side(pick(regroup, along_high(pair_grad, True)))
    token_grad = pick(token_select, returned)

    own, beside = lax.psum_scatter(
        parts.reshape(ring, near, 2 * local_hidden, model_width),
        RING,
        scatter_dimension=0,
        tiled=False,
    )
    summed = own.astype(jnp.float32) + partner(beside, NEAR, 1).astype(jnp.float32)
    moments = tuple(
        jnp.where(swapped, new.astype(jnp.float32), old) for new, old in zip(arrived, moments)
    )
    new_up, up_first_new, up_second_new = adam_update(
        weights[:local_hidden], moments[0], moments[1], summed[:local_hidden]
    )
    new_down, down_first_new, down_second_new = adam_update(
        weights[local_hidden:], moments[2], moments[3], summed[local_hidden:]
    )
    return (
        token_grad,
        new_up[None],
        new_down[None],
        up_first_new[None],
        up_second_new[None],
        down_first_new[None],
        down_second_new[None],
    )


def solution(mesh):
    dp, expert = (mesh.shape[name] for name in ("dp", "expert"))
    fine = Mesh(
        mesh.devices.reshape(2, dp // 4, 2, HIGHS, expert // HIGHS),
        (NEAR, RING, CORE, HIGH, SIDE),
    )
    rows = P((NEAR, RING, CORE, HIGH, SIDE), None)
    slots = P((HIGH, SIDE), (NEAR, RING, CORE), None)
    return jax.shard_map(
        on_device,
        mesh=fine,
        in_specs=(rows, rows, rows, rows, P()) + (slots,) * 6,
        out_specs=(rows,) + (slots,) * 6,
        check_vma=False,
    )
```

```python
import functools

import jax
import jax.numpy as jnp
from jax import lax
from jax.experimental import pallas as pl
from jax.experimental.pallas import tpu as pltpu
from jax.sharding import Mesh
from jax.sharding import PartitionSpec as P

ADAM_STEP = 20


beta_first = 0.9
beta_second = 0.95
step_size = 0.05
adam_epsilon = 1e-08

NEAR = "near"
RING = "ring"
CORE = "core"
FAR = "far"
STEP = "step"
HIGH = (FAR, STEP)
SIDE = "side"
HIGHS = 4


def partner(array, axis, flip):
    return lax.ppermute(array, axis, [(i, i ^ flip) for i in range(lax.axis_size(axis))])


def z_routes():
    routes = []
    for step, crosses in ((1, False), (-1, True), (2, True)):
        pairs = []
        for near in range(2):
            sign = 1 if near == 0 else -1
            for high in range(HIGHS):
                other = (1 - near) if crosses else near
                pairs.append((near * HIGHS + high, other * HIGHS + (high + sign * step) % HIGHS))
        routes.append(pairs)
    return routes


def adam_update(weight, first, second, gradient):
    first_new = beta_first * first + (1.0 - beta_first) * gradient
    second_new = beta_second * second + (1.0 - beta_second) * gradient * gradient
    corr_first = 1.0 - beta_first**ADAM_STEP
    corr_second = 1.0 - beta_second**ADAM_STEP
    stepped = weight.astype(jnp.float32) - step_size * (first_new / corr_first) / (
        jnp.sqrt(second_new / corr_second) + adam_epsilon
    )
    return (stepped.astype(jnp.bfloat16), first_new, second_new)


def dispatch_kernel(
    capacity,
    flags_ref,
    routes_ref,
    probs_ref,
    tokens_ref,
    out_grad_ref,
    token_rows_ref,
    scaled_rows_ref,
    select_ref,
):
    count, tops = routes_ref.shape
    experts = flags_ref.shape[1]
    rows, width = token_rows_ref.shape
    side = experts // HIGHS
    half_axis = experts // 2
    my_high = lax.axis_index(HIGH)
    my_near = lax.axis_index(NEAR)
    ids = lax.broadcasted_iota(jnp.int32, (1, experts), 1)
    slot = jnp.where(flags_ref[...] == 1, jnp.bitwise_xor(ids, half_axis), ids)
    away = lax.shift_right_logical(slot, side.bit_length() - 1) - my_high
    away = jnp.bitwise_and(jnp.where(my_near == 0, away, -away), HIGHS - 1)
    block = jnp.where(away >= 2, 5 - away, away)
    base = jnp.bitwise_and(slot, side - 1) * (HIGHS * capacity) + block * capacity
    base = base.astype(jnp.float32)
    expert_ids = lax.broadcasted_iota(jnp.int32, (count, experts), 1)
    below = (
        lax.broadcasted_iota(jnp.int32, (count, count), 0)
        > lax.broadcasted_iota(jnp.int32, (count, count), 1)
    )
    below = jnp.where(below, 1.0, 0.0).astype(jnp.bfloat16)
    padded = -(-rows // 128) * 128
    row_ids = lax.broadcasted_iota(jnp.int32, (count, padded), 1)
    token_select = jnp.zeros((count, padded), jnp.float32)
    prob_select = jnp.zeros((count, padded), jnp.float32)
    for k in range(tops):
        onehot = jnp.where(routes_ref[:, k : k + 1] == expert_ids, 1.0, 0.0)
        earlier = jnp.dot(below, onehot.astype(jnp.bfloat16), preferred_element_type=jnp.float32)
        row = jnp.sum(onehot * (base + earlier), axis=1, keepdims=True).astype(jnp.int32)
        hit = row_ids == row
        token_select = token_select + jnp.where(hit, 1.0, 0.0)
        prob = probs_ref[:, k : k + 1].astype(jnp.float32)
        prob_select = prob_select + jnp.where(hit, prob, 0.0)
        base = base + jnp.sum(onehot, axis=0, keepdims=True)
    select_ref[...] = token_select[:, :rows].astype(jnp.bfloat16)
    token_pick = token_select.T[:rows].astype(jnp.bfloat16)
    prob_pick = prob_select.T[:rows].astype(jnp.bfloat16)
    piece = 512
    for at in range(0, width, piece):
        cut = slice(at, min(at + piece, width))
        for pick, source, target in (
            (token_pick, tokens_ref, token_rows_ref),
            (prob_pick, out_grad_ref, scaled_rows_ref),
        ):
            target[:, cut] = jnp.dot(
                pick, source[:, cut], preferred_element_type=jnp.float32
            ).astype(jnp.bfloat16)


def dispatch(swap_flags, routes, probs, tokens, out_grad, capacity):
    count, width = tokens.shape
    rows = swap_flags.shape[0] * capacity
    whole = pl.BlockSpec(memory_space=pltpu.VMEM)
    return pl.pallas_call(
        functools.partial(dispatch_kernel, capacity),
        in_specs=[whole] * 5,
        out_specs=[whole] * 3,
        out_shape=[
            jax.ShapeDtypeStruct((rows, width), jnp.bfloat16),
            jax.ShapeDtypeStruct((rows, width), jnp.bfloat16),
            jax.ShapeDtypeStruct((count, rows), jnp.bfloat16),
        ],
        compiler_params=pltpu.CompilerParams(vmem_limit_bytes=24 * 1024 * 1024),
        cost_estimate=pl.CostEstimate(flops=0, bytes_accessed=1024, transcendentals=0),
    )(swap_flags.reshape(1, -1), routes, probs, tokens, out_grad)


def expert_kernel(
    steps,
    inv_model,
    inv_hidden,
    mine_ref,
    other_ref,
    mine_scaled_ref,
    other_scaled_ref,
    weight_ref,
    pair_ref,
    pair_other_ref,
    left_ref,
    pre_ref,
    back_ref,
    delta_ref,
):
    step = pl.program_id(0)
    chips, both, _ = weight_ref.shape
    local = both // 2
    rows = mine_ref.shape[0]
    contract_last = (((1,), (1,)), ((), ()))
    up = jnp.concatenate([weight_ref[i, :local] for i in range(chips)], axis=0)

    @pl.when(step == 0)
    def _():
        pre_ref[...] = jnp.zeros_like(pre_ref)
        back_ref[...] = jnp.zeros_like(back_ref)

    @pl.when(step < steps)
    def _():
        down = jnp.concatenate([weight_ref[i, local:] for i in range(chips)], axis=0)
        token = jnp.concatenate((mine_ref[...], other_ref[...]), axis=0)
        pre_ref[...] += lax.dot_general(
            up, token, contract_last, preferred_element_type=jnp.float32
        )
        scaled = jnp.concatenate((mine_scaled_ref[...], other_scaled_ref[...]), axis=0)
        back_ref[...] += lax.dot_general(
            down, scaled, contract_last, preferred_element_type=jnp.float32
        )

    @pl.when(step == steps - 1)
    def _():
        pre_act = pre_ref[...] * inv_model
        sigmoid_act = 1.0 / (1.0 + jnp.exp(-pre_act))
        delta = (
            back_ref[...] * inv_hidden * sigmoid_act * (1.0 + pre_act * (1.0 - sigmoid_act))
        ).astype(jnp.bfloat16)
        left_ref[0] = delta
        left_ref[1] = (pre_act * sigmoid_act).astype(jnp.bfloat16)
        delta_ref[...] = delta.T

    @pl.when(step >= steps)
    def _():
        pair = jnp.dot(delta_ref[...], up, preferred_element_type=jnp.float32) * inv_model
        pair_ref[...] = pair[:rows]
        pair_other_ref[...] = pair[rows:].astype(jnp.bfloat16)


def expert_stage(mine, other, mine_scaled, other_scaled, weights, inv_model, inv_hidden):
    rows, width = mine.shape
    chips, both, _ = weights.shape
    hidden = chips * both // 2
    block = 512
    steps = width // block

    def early(i):
        return jnp.minimum(i, steps - 1)

    def late(i):
        return jnp.maximum(i - steps, 0)

    row_spec = pl.BlockSpec((rows, block), lambda i: (0, early(i)))
    late_spec = pl.BlockSpec((rows, block), lambda i: (0, late(i)))
    return pl.pallas_call(
        functools.partial(expert_kernel, steps, inv_model, inv_hidden),
        grid=(2 * steps,),
        in_specs=[row_spec] * 4 + [pl.BlockSpec((chips, both, block), lambda i: (0, 0, i % steps))],
        out_specs=[
            late_spec,
            late_spec,
            pl.BlockSpec((2, hidden, 2 * rows), lambda i: (0, 0, 0)),
        ],
        out_shape=[
            jax.ShapeDtypeStruct((rows, width), jnp.float32),
            jax.ShapeDtypeStruct((rows, width), jnp.bfloat16),
            jax.ShapeDtypeStruct((2, hidden, 2 * rows), jnp.bfloat16),
        ],
        scratch_shapes=[
            pltpu.VMEM((hidden, 2 * rows), jnp.float32),
            pltpu.VMEM((hidden, 2 * rows), jnp.float32),
            pltpu.VMEM((2 * rows, hidden), jnp.bfloat16),
        ],
        compiler_params=pltpu.CompilerParams(
            dimension_semantics=("arbitrary",), vmem_limit_bytes=40 * 1024 * 1024
        ),
        cost_estimate=pl.CostEstimate(
            flops=12 * rows * hidden * width, bytes_accessed=32 * rows * width, transcendentals=0
        ),
    )(mine, other, mine_scaled, other_scaled, weights)


def weight_kernel(
    inv_model,
    inv_hidden,
    left_ref,
    mine_ref,
    other_ref,
    mine_scaled_ref,
    other_scaled_ref,
    part_ref,
):
    chips, both, _ = part_ref.shape
    local = both // 2
    for kind, mine, other, scale in (
        (0, mine_ref, other_ref, inv_model),
        (1, mine_scaled_ref, other_scaled_ref, inv_hidden),
    ):
        right = jnp.concatenate((mine[...], other[...]), axis=0)
        part = jnp.dot(left_ref[kind], right, preferred_element_type=jnp.float32) * scale
        part = part.astype(jnp.bfloat16)
        for i in range(chips):
            part_ref[i, kind * local : (kind + 1) * local] = part[i * local : (i + 1) * local]


def weight_stage(left, mine, other, mine_scaled, other_scaled, chips, inv_model, inv_hidden):
    rows, width = mine.shape
    both = 2 * left.shape[1] // chips
    block = 512
    row_spec = pl.BlockSpec((rows, block), lambda i: (0, i))
    return pl.pallas_call(
        functools.partial(weight_kernel, inv_model, inv_hidden),
        grid=(width // block,),
        in_specs=[pl.BlockSpec(left.shape, lambda i: (0, 0, 0))] + [row_spec] * 4,
        out_specs=pl.BlockSpec((chips, both, block), lambda i: (0, 0, i)),
        out_shape=jax.ShapeDtypeStruct((chips, both, width), jnp.bfloat16),
        compiler_params=pltpu.CompilerParams(
            dimension_semantics=("arbitrary",), vmem_limit_bytes=40 * 1024 * 1024
        ),
        cost_estimate=pl.CostEstimate(
            flops=8 * rows * left.shape[1] * width,
            bytes_accessed=32 * rows * width,
            transcendentals=0,
        ),
    )(left, mine, other, mine_scaled, other_scaled)


def on_device(
    tokens,
    out_grad,
    routes,
    probs,
    swap_flags,
    up_weight,
    down_weight,
    up_first,
    up_second,
    down_first,
    down_second,
):
    model_width = tokens.shape[1]
    high = lax.axis_size(HIGH)
    side = lax.axis_size(SIDE)
    experts = high * side
    ring = lax.axis_size(RING)
    near = lax.axis_size(NEAR)
    chips = ring * near
    half_axis = experts // 2
    capacity = max(2, routes.size * 5 // (4 * experts))
    side_rows = high * capacity
    high_rows = side * capacity
    buffer_rows = experts * capacity
    local_hidden = up_weight.shape[1]
    hidden_units = local_hidden * chips * lax.axis_size(CORE)
    inv_model = model_width ** (-0.5)
    inv_hidden = hidden_units ** (-0.5)
    my_high = lax.axis_index(HIGH)
    my_index = my_high * side + lax.axis_index(SIDE)
    expert_ids = jnp.arange(experts, dtype=jnp.int32)
    flag_mine = jnp.sum(jnp.where(expert_ids == my_index, swap_flags, 0))
    swapped = flag_mine == 1

    weights = jnp.concatenate((up_weight[0], down_weight[0]), axis=0)
    weights_partner = partner(weights, FAR, 1)

    send_tokens, send_scaled, token_select = dispatch(
        swap_flags, routes, probs, tokens, out_grad, capacity
    )
    buffer_ids = jnp.arange(buffer_rows, dtype=jnp.int32)
    other_order = (
        (buffer_ids // capacity % high) * side_rows
        + (buffer_ids // side_rows) * capacity
        + buffer_ids % capacity
    )
    regroup = (buffer_ids[None, :] == other_order[:, None]).astype(jnp.bfloat16)

    def along_side(rows):
        return lax.all_to_all(
            rows.reshape(side, side_rows, model_width),
            SIDE,
            split_axis=0,
            concat_axis=0,
            tiled=True,
        ).reshape(buffer_rows, model_width)

    def pick(matrix, rows):
        return jnp.dot(matrix, rows, preferred_element_type=jnp.float32).astype(jnp.bfloat16)

    ways = z_routes()

    def along_high(rows, back):
        blocks = [rows[i * high_rows : (i + 1) * high_rows] for i in range(high)]
        moved = [
            lax.ppermute(
                array, (NEAR, *HIGH), [(b, a) for a, b in way] if back else way
            )
            for array, way in zip(blocks[1:], ways)
        ]
        return jnp.concatenate(blocks[:1] + moved, axis=0)

    token_rows = pick(regroup, along_side(send_tokens))
    side_scaled = along_side(send_scaled)
    scaled_rows = pick(regroup, side_scaled)

    weights = jnp.where(swapped, weights_partner, weights)
    weights, _ = lax.optimization_barrier((weights, token_rows))
    both = jnp.stack((weights, partner(weights, NEAR, 1)), axis=0)
    both, _ = lax.optimization_barrier((both, side_scaled))
    gathered = lax.all_gather(both, RING, axis=0).reshape(
        chips, 2 * local_hidden, model_width
    )

    rows_mine = along_high(token_rows, False)
    scaled_mine = along_high(scaled_rows, False)
    rows_other = partner(rows_mine, CORE, 1)
    scaled_other = partner(scaled_mine, CORE, 1)
    moments = (up_first[0], up_second[0], down_first[0], down_second[0])

    rounded = tuple(array.astype(jnp.bfloat16) for array in moments)
    up_held, _ = lax.optimization_barrier((jnp.stack(rounded[:2]), scaled_mine))
    up_pair = lax.all_gather(up_held, FAR, axis=0)
    pair_mine, for_other, left = expert_stage(
        rows_mine, rows_other, scaled_mine, scaled_other, gathered, inv_model, inv_hidden
    )
    parts = weight_stage(
        left, rows_mine, rows_other, scaled_mine, scaled_other, chips, inv_model, inv_hidden
    )
    from_other = partner(for_other, CORE, 1)
    pair_grad = (pair_mine + from_other.astype(jnp.float32)).astype(jnp.bfloat16)
    parts, up_pair, _ = lax.optimization_barrier((parts, up_pair, pair_grad))
    up_arrived = jnp.where(lax.axis_index(FAR) == 0, up_pair[1], up_pair[0])
    back_rows = along_high(pair_grad, True)
    down_held, back_rows = lax.optimization_barrier((rounded[2:], back_rows))
    down_arrived = tuple(partner(array, FAR, 1) for array in down_held)
    returned = along_side(pick(regroup, back_rows))
    token_grad = pick(token_select, returned)

    own, beside = lax.psum_scatter(
        parts.reshape(ring, near, 2 * local_hidden, model_width),
        RING,
        scatter_dimension=0,
        tiled=False,
    )
    down_arrived, beside = lax.optimization_barrier((down_arrived, beside))
    arrived = (up_arrived[0], up_arrived[1], *down_arrived)
    summed = own.astype(jnp.float32) + partner(beside, NEAR, 1).astype(jnp.float32)
    moments = tuple(
        jnp.where(swapped, new.astype(jnp.float32), old) for new, old in zip(arrived, moments)
    )
    new_up, up_first_new, up_second_new = adam_update(
        weights[:local_hidden], moments[0], moments[1], summed[:local_hidden]
    )
    new_down, down_first_new, down_second_new = adam_update(
        weights[local_hidden:], moments[2], moments[3], summed[local_hidden:]
    )
    return (
        token_grad,
        new_up[None],
        new_down[None],
        up_first_new[None],
        up_second_new[None],
        down_first_new[None],
        down_second_new[None],
    )


def solution(mesh):
    dp, expert = (mesh.shape[name] for name in ("dp", "expert"))
    fine = Mesh(
        mesh.devices.reshape(2, dp // 4, 2, 2, HIGHS // 2, expert // HIGHS),
        (NEAR, RING, CORE, *HIGH, SIDE),
    )
    rows = P((NEAR, RING, CORE, *HIGH, SIDE), None)
    slots = P((*HIGH, SIDE), (NEAR, RING, CORE), None)
    return jax.shard_map(
        on_device,
        mesh=fine,
        in_specs=(rows, rows, rows, rows, P()) + (slots,) * 6,
        out_specs=(rows,) + (slots,) * 6,
        check_vma=False,
    )
```

```python
import functools

import jax
import jax.numpy as jnp
from jax import lax
from jax.experimental import pallas as pl
from jax.experimental.pallas import tpu as pltpu
from jax.sharding import Mesh
from jax.sharding import PartitionSpec as P

ADAM_STEP = 20


beta_first = 0.9
beta_second = 0.95
step_size = 0.05
adam_epsilon = 1e-08

NEAR = "near"
RING = "ring"
CORE = "core"
FAR = "far"
STEP = "step"
HIGH = (FAR, STEP)
SIDE = "side"
HIGHS = 4


def partner(array, axis, flip):
    return lax.ppermute(array, axis, [(i, i ^ flip) for i in range(lax.axis_size(axis))])


def z_routes():
    routes = []
    for step, crosses in ((1, False), (-1, True), (2, True)):
        pairs = []
        for near in range(2):
            sign = 1 if near == 0 else -1
            for high in range(HIGHS):
                other = (1 - near) if crosses else near
                pairs.append((near * HIGHS + high, other * HIGHS + (high + sign * step) % HIGHS))
        routes.append(pairs)
    return routes


def adam_update(weight, first, second, gradient):
    first_new = beta_first * first + (1.0 - beta_first) * gradient
    second_new = beta_second * second + (1.0 - beta_second) * gradient * gradient
    corr_first = 1.0 - beta_first**ADAM_STEP
    corr_second = 1.0 - beta_second**ADAM_STEP
    stepped = weight.astype(jnp.float32) - step_size * (first_new / corr_first) / (
        jnp.sqrt(second_new / corr_second) + adam_epsilon
    )
    return (stepped.astype(jnp.bfloat16), first_new, second_new)


def dispatch_kernel(
    capacity,
    flags_ref,
    routes_ref,
    probs_ref,
    tokens_ref,
    out_grad_ref,
    token_rows_ref,
    scaled_rows_ref,
    select_ref,
):
    count, tops = routes_ref.shape
    experts = flags_ref.shape[1]
    rows, width = token_rows_ref.shape
    side = experts // HIGHS
    half_axis = experts // 2
    my_high = lax.axis_index(HIGH)
    my_near = lax.axis_index(NEAR)
    ids = lax.broadcasted_iota(jnp.int32, (1, experts), 1)
    slot = jnp.where(flags_ref[...] == 1, jnp.bitwise_xor(ids, half_axis), ids)
    away = lax.shift_right_logical(slot, side.bit_length() - 1) - my_high
    away = jnp.bitwise_and(jnp.where(my_near == 0, away, -away), HIGHS - 1)
    block = jnp.where(away >= 2, 5 - away, away)
    base = jnp.bitwise_and(slot, side - 1) * (HIGHS * capacity) + block * capacity
    base = base.astype(jnp.float32)
    expert_ids = lax.broadcasted_iota(jnp.int32, (count, experts), 1)
    below = (
        lax.broadcasted_iota(jnp.int32, (count, count), 0)
        > lax.broadcasted_iota(jnp.int32, (count, count), 1)
    )
    below = jnp.where(below, 1.0, 0.0).astype(jnp.bfloat16)
    padded = -(-rows // 128) * 128
    row_ids = lax.broadcasted_iota(jnp.int32, (count, padded), 1)
    token_select = jnp.zeros((count, padded), jnp.float32)
    prob_select = jnp.zeros((count, padded), jnp.float32)
    for k in range(tops):
        onehot = jnp.where(routes_ref[:, k : k + 1] == expert_ids, 1.0, 0.0)
        earlier = jnp.dot(below, onehot.astype(jnp.bfloat16), preferred_element_type=jnp.float32)
        row = jnp.sum(onehot * (base + earlier), axis=1, keepdims=True).astype(jnp.int32)
        hit = row_ids == row
        token_select = token_select + jnp.where(hit, 1.0, 0.0)
        prob = probs_ref[:, k : k + 1].astype(jnp.float32)
        prob_select = prob_select + jnp.where(hit, prob, 0.0)
        base = base + jnp.sum(onehot, axis=0, keepdims=True)
    select_ref[...] = token_select[:, :rows].astype(jnp.bfloat16)
    token_pick = token_select.T[:rows].astype(jnp.bfloat16)
    prob_pick = prob_select.T[:rows].astype(jnp.bfloat16)
    piece = 512
    for at in range(0, width, piece):
        cut = slice(at, min(at + piece, width))
        for pick, source, target in (
            (token_pick, tokens_ref, token_rows_ref),
            (prob_pick, out_grad_ref, scaled_rows_ref),
        ):
            target[:, cut] = jnp.dot(
                pick, source[:, cut], preferred_element_type=jnp.float32
            ).astype(jnp.bfloat16)


def dispatch(swap_flags, routes, probs, tokens, out_grad, capacity):
    count, width = tokens.shape
    rows = swap_flags.shape[0] * capacity
    whole = pl.BlockSpec(memory_space=pltpu.VMEM)
    return pl.pallas_call(
        functools.partial(dispatch_kernel, capacity),
        in_specs=[whole] * 5,
        out_specs=[whole] * 3,
        out_shape=[
            jax.ShapeDtypeStruct((rows, width), jnp.bfloat16),
            jax.ShapeDtypeStruct((rows, width), jnp.bfloat16),
            jax.ShapeDtypeStruct((count, rows), jnp.bfloat16),
        ],
        compiler_params=pltpu.CompilerParams(vmem_limit_bytes=24 * 1024 * 1024),
        cost_estimate=pl.CostEstimate(flops=0, bytes_accessed=1024, transcendentals=0),
    )(swap_flags.reshape(1, -1), routes, probs, tokens, out_grad)


def expert_kernel(
    steps,
    inv_model,
    inv_hidden,
    mine_ref,
    other_ref,
    mine_scaled_ref,
    other_scaled_ref,
    weight_ref,
    pair_ref,
    pair_other_ref,
    left_ref,
    pre_ref,
    back_ref,
    delta_ref,
):
    step = pl.program_id(0)
    chips, both, _ = weight_ref.shape
    local = both // 2
    rows = mine_ref.shape[0]
    contract_last = (((1,), (1,)), ((), ()))
    up = jnp.concatenate([weight_ref[i, :local] for i in range(chips)], axis=0)

    @pl.when(step == 0)
    def _():
        pre_ref[...] = jnp.zeros_like(pre_ref)
        back_ref[...] = jnp.zeros_like(back_ref)

    @pl.when(step < steps)
    def _():
        down = jnp.concatenate([weight_ref[i, local:] for i in range(chips)], axis=0)
        token = jnp.concatenate((mine_ref[...], other_ref[...]), axis=0)
        pre_ref[...] += lax.dot_general(
            up, token, contract_last, preferred_element_type=jnp.float32
        )
        scaled = jnp.concatenate((mine_scaled_ref[...], other_scaled_ref[...]), axis=0)
        back_ref[...] += lax.dot_general(
            down, scaled, contract_last, preferred_element_type=jnp.float32
        )

    @pl.when(step == steps - 1)
    def _():
        pre_act = pre_ref[...] * inv_model
        sigmoid_act = 1.0 / (1.0 + jnp.exp(-pre_act))
        delta = (
            back_ref[...] * inv_hidden * sigmoid_act * (1.0 + pre_act * (1.0 - sigmoid_act))
        ).astype(jnp.bfloat16)
        left_ref[0] = delta
        left_ref[1] = (pre_act * sigmoid_act).astype(jnp.bfloat16)
        delta_ref[...] = delta.T

    @pl.when(step >= steps)
    def _():
        pair = jnp.dot(delta_ref[...], up, preferred_element_type=jnp.float32) * inv_model
        pair_ref[...] = pair[:rows]
        pair_other_ref[...] = pair[rows:].astype(jnp.bfloat16)


def expert_stage(mine, other, mine_scaled, other_scaled, weights, inv_model, inv_hidden):
    rows, width = mine.shape
    chips, both, _ = weights.shape
    hidden = chips * both // 2
    block = 512
    steps = width // block

    def early(i):
        return jnp.minimum(i, steps - 1)

    def late(i):
        return jnp.maximum(i - steps, 0)

    row_spec = pl.BlockSpec((rows, block), lambda i: (0, early(i)))
    late_spec = pl.BlockSpec((rows, block), lambda i: (0, late(i)))
    return pl.pallas_call(
        functools.partial(expert_kernel, steps, inv_model, inv_hidden),
        grid=(2 * steps,),
        in_specs=[row_spec] * 4 + [pl.BlockSpec((chips, both, block), lambda i: (0, 0, i % steps))],
        out_specs=[
            late_spec,
            late_spec,
            pl.BlockSpec((2, hidden, 2 * rows), lambda i: (0, 0, 0)),
        ],
        out_shape=[
            jax.ShapeDtypeStruct((rows, width), jnp.float32),
            jax.ShapeDtypeStruct((rows, width), jnp.bfloat16),
            jax.ShapeDtypeStruct((2, hidden, 2 * rows), jnp.bfloat16),
        ],
        scratch_shapes=[
            pltpu.VMEM((hidden, 2 * rows), jnp.float32),
            pltpu.VMEM((hidden, 2 * rows), jnp.float32),
            pltpu.VMEM((2 * rows, hidden), jnp.bfloat16),
        ],
        compiler_params=pltpu.CompilerParams(
            dimension_semantics=("arbitrary",), vmem_limit_bytes=40 * 1024 * 1024
        ),
        cost_estimate=pl.CostEstimate(
            flops=12 * rows * hidden * width, bytes_accessed=32 * rows * width, transcendentals=0
        ),
    )(mine, other, mine_scaled, other_scaled, weights)


def weight_kernel(
    inv_model,
    inv_hidden,
    left_ref,
    mine_ref,
    other_ref,
    mine_scaled_ref,
    other_scaled_ref,
    part_ref,
):
    chips, both, _ = part_ref.shape
    local = both // 2
    for kind, mine, other, scale in (
        (0, mine_ref, other_ref, inv_model),
        (1, mine_scaled_ref, other_scaled_ref, inv_hidden),
    ):
        right = jnp.concatenate((mine[...], other[...]), axis=0)
        part = jnp.dot(left_ref[kind], right, preferred_element_type=jnp.float32) * scale
        part = part.astype(jnp.bfloat16)
        for i in range(chips):
            part_ref[i, kind * local : (kind + 1) * local] = part[i * local : (i + 1) * local]


def weight_stage(left, mine, other, mine_scaled, other_scaled, chips, inv_model, inv_hidden):
    rows, width = mine.shape
    both = 2 * left.shape[1] // chips
    block = 512
    row_spec = pl.BlockSpec((rows, block), lambda i: (0, i))
    return pl.pallas_call(
        functools.partial(weight_kernel, inv_model, inv_hidden),
        grid=(width // block,),
        in_specs=[pl.BlockSpec(left.shape, lambda i: (0, 0, 0))] + [row_spec] * 4,
        out_specs=pl.BlockSpec((chips, both, block), lambda i: (0, 0, i)),
        out_shape=jax.ShapeDtypeStruct((chips, both, width), jnp.bfloat16),
        compiler_params=pltpu.CompilerParams(
            dimension_semantics=("arbitrary",), vmem_limit_bytes=40 * 1024 * 1024
        ),
        cost_estimate=pl.CostEstimate(flops=0, bytes_accessed=1024, transcendentals=0),
    )(left, mine, other, mine_scaled, other_scaled)


def on_device(
    tokens,
    out_grad,
    routes,
    probs,
    swap_flags,
    up_weight,
    down_weight,
    up_first,
    up_second,
    down_first,
    down_second,
):
    model_width = tokens.shape[1]
    high = lax.axis_size(HIGH)
    side = lax.axis_size(SIDE)
    experts = high * side
    ring = lax.axis_size(RING)
    near = lax.axis_size(NEAR)
    chips = ring * near
    half_axis = experts // 2
    capacity = max(2, routes.size * 5 // (4 * experts))
    side_rows = high * capacity
    high_rows = side * capacity
    buffer_rows = experts * capacity
    local_hidden = up_weight.shape[1]
    hidden_units = local_hidden * chips * lax.axis_size(CORE)
    inv_model = model_width ** (-0.5)
    inv_hidden = hidden_units ** (-0.5)
    my_high = lax.axis_index(HIGH)
    my_index = my_high * side + lax.axis_index(SIDE)
    expert_ids = jnp.arange(experts, dtype=jnp.int32)
    flag_mine = jnp.sum(jnp.where(expert_ids == my_index, swap_flags, 0))
    swapped = flag_mine == 1

    weights = jnp.concatenate((up_weight[0], down_weight[0]), axis=0)
    weights_partner = partner(weights, FAR, 1)

    send_tokens, send_scaled, token_select = dispatch(
        swap_flags, routes, probs, tokens, out_grad, capacity
    )
    buffer_ids = jnp.arange(buffer_rows, dtype=jnp.int32)
    other_order = (
        (buffer_ids // capacity % high) * side_rows
        + (buffer_ids // side_rows) * capacity
        + buffer_ids % capacity
    )
    regroup = (buffer_ids[None, :] == other_order[:, None]).astype(jnp.bfloat16)

    def along_side(rows):
        return lax.all_to_all(
            rows.reshape(side, side_rows, model_width),
            SIDE,
            split_axis=0,
            concat_axis=0,
            tiled=True,
        ).reshape(buffer_rows, model_width)

    def pick(matrix, rows):
        return jnp.dot(matrix, rows, preferred_element_type=jnp.float32).astype(jnp.bfloat16)

    ways = z_routes()

    def along_high(rows, back):
        blocks = [rows[i * high_rows : (i + 1) * high_rows] for i in range(high)]
        moved = [
            lax.ppermute(
                array, (NEAR, *HIGH), [(b, a) for a, b in way] if back else way
            )
            for array, way in zip(blocks[1:], ways)
        ]
        return jnp.concatenate(blocks[:1] + moved, axis=0), moved[-1]

    token_rows = pick(regroup, along_side(send_tokens))
    side_scaled = along_side(send_scaled)
    scaled_rows = pick(regroup, side_scaled)

    rows_mine, farthest = along_high(token_rows, False)

    weights_partner, _ = lax.optimization_barrier((weights_partner, token_rows))
    weights = jnp.where(swapped, weights_partner, weights)
    both = jnp.stack((weights, partner(weights, NEAR, 1)), axis=0)
    both, _, _ = lax.optimization_barrier((both, side_scaled, farthest))
    gathered = lax.all_gather(both, RING, axis=0).reshape(
        chips, 2 * local_hidden, model_width
    )

    scaled_mine, _ = along_high(scaled_rows, False)
    rows_other = partner(rows_mine, CORE, 1)
    scaled_other = partner(scaled_mine, CORE, 1)
    moments = (up_first[0], up_second[0], down_first[0], down_second[0])

    rounded = tuple(array.astype(jnp.bfloat16) for array in moments)
    up_held, _ = lax.optimization_barrier((jnp.stack(rounded[:2]), scaled_mine))
    up_pair = lax.all_gather(up_held, FAR, axis=0)
    pair_mine, for_other, left = expert_stage(
        rows_mine, rows_other, scaled_mine, scaled_other, gathered, inv_model, inv_hidden
    )
    parts = weight_stage(
        left, rows_mine, rows_other, scaled_mine, scaled_other, chips, inv_model, inv_hidden
    )
    from_other = partner(for_other, CORE, 1)
    pair_grad = (pair_mine + from_other.astype(jnp.float32)).astype(jnp.bfloat16)
    up_pair, pair_grad = lax.optimization_barrier((up_pair, pair_grad))
    up_arrived = jnp.where(lax.axis_index(FAR) == 0, up_pair[1], up_pair[0])
    back_rows, _ = along_high(pair_grad, True)
    down_held, back_rows = lax.optimization_barrier((rounded[2:], back_rows))
    down_arrived = tuple(partner(array, FAR, 1) for array in down_held)
    returned = along_side(pick(regroup, back_rows))
    token_grad = pick(token_select, returned)

    own, beside = lax.psum_scatter(
        parts.reshape(ring, near, 2 * local_hidden, model_width),
        RING,
        scatter_dimension=0,
        tiled=False,
    )
    down_arrived, beside = lax.optimization_barrier((down_arrived, beside))
    arrived = (up_arrived[0], up_arrived[1], *down_arrived)
    summed = own.astype(jnp.float32) + partner(beside, NEAR, 1).astype(jnp.float32)
    moments = tuple(
        jnp.where(swapped, new.astype(jnp.float32), old) for new, old in zip(arrived, moments)
    )
    new_up, up_first_new, up_second_new = adam_update(
        weights[:local_hidden], moments[0], moments[1], summed[:local_hidden]
    )
    new_down, down_first_new, down_second_new = adam_update(
        weights[local_hidden:], moments[2], moments[3], summed[local_hidden:]
    )
    return (
        token_grad,
        new_up[None],
        new_down[None],
        up_first_new[None],
        up_second_new[None],
        down_first_new[None],
        down_second_new[None],
    )


def solution(mesh):
    dp, expert = (mesh.shape[name] for name in ("dp", "expert"))
    fine = Mesh(
        mesh.devices.reshape(2, dp // 4, 2, 2, HIGHS // 2, expert // HIGHS),
        (NEAR, RING, CORE, *HIGH, SIDE),
    )
    rows = P((NEAR, RING, CORE, *HIGH, SIDE), None)
    slots = P((*HIGH, SIDE), (NEAR, RING, CORE), None)
    return jax.shard_map(
        on_device,
        mesh=fine,
        in_specs=(rows, rows, rows, rows, P()) + (slots,) * 6,
        out_specs=(rows,) + (slots,) * 6,
        check_vma=False,
    )
```

```python
import functools

import jax
import jax.numpy as jnp
from jax import lax
from jax.experimental import pallas as pl
from jax.experimental.pallas import tpu as pltpu
from jax.sharding import Mesh
from jax.sharding import PartitionSpec as P

ADAM_STEP = 20


beta_first = 0.9
beta_second = 0.95
step_size = 0.05
adam_epsilon = 1e-08

NEAR = "near"
RING = "ring"
CORE = "core"
FAR = "far"
STEP = "step"
HIGH = (FAR, STEP)
SIDE = "side"
HIGHS = 4


def partner(array, axis, flip):
    return lax.ppermute(array, axis, [(i, i ^ flip) for i in range(lax.axis_size(axis))])


def z_routes():
    routes = []
    for step, crosses in ((1, False), (-1, True), (2, True)):
        pairs = []
        for near in range(2):
            sign = 1 if near == 0 else -1
            for high in range(HIGHS):
                other = (1 - near) if crosses else near
                pairs.append((near * HIGHS + high, other * HIGHS + (high + sign * step) % HIGHS))
        routes.append(pairs)
    return routes


def adam_update(weight, first, second, gradient):
    first_new = beta_first * first + (1.0 - beta_first) * gradient
    second_new = beta_second * second + (1.0 - beta_second) * gradient * gradient
    corr_first = 1.0 - beta_first**ADAM_STEP
    corr_second = 1.0 - beta_second**ADAM_STEP
    stepped = weight.astype(jnp.float32) - step_size * (first_new / corr_first) / (
        jnp.sqrt(second_new / corr_second) + adam_epsilon
    )
    return (stepped.astype(jnp.bfloat16), first_new, second_new)


def dispatch_kernel(
    capacity,
    flags_ref,
    routes_ref,
    probs_ref,
    tokens_ref,
    out_grad_ref,
    token_rows_ref,
    scaled_rows_ref,
    select_ref,
):
    tops, count = routes_ref.shape
    experts = flags_ref.shape[0]
    rows, width = token_rows_ref.shape
    side = experts // HIGHS
    half_axis = experts // 2
    my_high = lax.axis_index(FAR) * (HIGHS // 2) + lax.axis_index(STEP)
    my_near = lax.axis_index(NEAR)
    ids = lax.broadcasted_iota(jnp.int32, (experts, 1), 0)
    slot = jnp.where(flags_ref[...] == 1, jnp.bitwise_xor(ids, half_axis), ids)
    away = lax.shift_right_logical(slot, side.bit_length() - 1) - my_high
    away = jnp.bitwise_and(jnp.where(my_near == 0, away, -away), HIGHS - 1)
    block = jnp.where(away >= 2, 5 - away, away)
    base = jnp.bitwise_and(slot, side - 1) * (HIGHS * capacity) + block * capacity
    base = base.astype(jnp.float32)
    expert_ids = lax.broadcasted_iota(jnp.int32, (experts, count), 0)
    before = (
        lax.broadcasted_iota(jnp.int32, (count, count), 0)
        < lax.broadcasted_iota(jnp.int32, (count, count), 1)
    )
    before = jnp.where(before, 1.0, 0.0).astype(jnp.bfloat16)
    row_ids = lax.broadcasted_iota(jnp.int32, (rows, count), 0)
    token_pick = jnp.zeros((rows, count), jnp.float32)
    prob_pick = jnp.zeros((rows, count), jnp.float32)
    for k in range(tops):
        onehot = jnp.where(routes_ref[k : k + 1] == expert_ids, 1.0, 0.0)
        earlier = jnp.dot(onehot.astype(jnp.bfloat16), before, preferred_element_type=jnp.float32)
        row = jnp.sum(onehot * (base + earlier), axis=0, keepdims=True).astype(jnp.int32)
        hit = row_ids == row
        token_pick = token_pick + jnp.where(hit, 1.0, 0.0)
        prob_pick = prob_pick + jnp.where(hit, probs_ref[k : k + 1].astype(jnp.float32), 0.0)
        base = base + jnp.sum(onehot, axis=1, keepdims=True)
    token_pick = token_pick.astype(jnp.bfloat16)
    prob_pick = prob_pick.astype(jnp.bfloat16)
    select_ref[...] = token_pick
    piece = 512
    for at in range(0, width, piece):
        cut = slice(at, min(at + piece, width))
        for pick, source, target in (
            (token_pick, tokens_ref, token_rows_ref),
            (prob_pick, out_grad_ref, scaled_rows_ref),
        ):
            target[:, cut] = jnp.dot(
                pick, source[:, cut], preferred_element_type=jnp.float32
            ).astype(jnp.bfloat16)


def dispatch(swap_flags, routes, probs, tokens, out_grad, capacity):
    count, width = tokens.shape
    rows = swap_flags.shape[0] * capacity
    whole = pl.BlockSpec(memory_space=pltpu.VMEM)
    return pl.pallas_call(
        functools.partial(dispatch_kernel, capacity),
        in_specs=[whole] * 5,
        out_specs=[whole] * 3,
        out_shape=[
            jax.ShapeDtypeStruct((rows, width), jnp.bfloat16),
            jax.ShapeDtypeStruct((rows, width), jnp.bfloat16),
            jax.ShapeDtypeStruct((rows, count), jnp.bfloat16),
        ],
        compiler_params=pltpu.CompilerParams(vmem_limit_bytes=24 * 1024 * 1024),
        cost_estimate=pl.CostEstimate(flops=0, bytes_accessed=1024, transcendentals=0),
    )(swap_flags.reshape(-1, 1), routes.T, probs.T, tokens, out_grad)


def expert_kernel(
    steps,
    inv_model,
    inv_hidden,
    mine_ref,
    other_ref,
    mine_scaled_ref,
    other_scaled_ref,
    weight_ref,
    pair_ref,
    pair_other_ref,
    left_ref,
    pre_ref,
    back_ref,
    delta_ref,
):
    step = pl.program_id(0)
    chips, both, _ = weight_ref.shape
    local = both // 2
    rows = mine_ref.shape[0]
    contract_last = (((1,), (1,)), ((), ()))
    up = jnp.concatenate([weight_ref[i, :local] for i in range(chips)], axis=0)

    @pl.when(step == 0)
    def _():
        pre_ref[...] = jnp.zeros_like(pre_ref)
        back_ref[...] = jnp.zeros_like(back_ref)

    @pl.when(step < steps)
    def _():
        down = jnp.concatenate([weight_ref[i, local:] for i in range(chips)], axis=0)
        token = jnp.concatenate((mine_ref[...], other_ref[...]), axis=0)
        pre_ref[...] += lax.dot_general(
            up, token, contract_last, preferred_element_type=jnp.float32
        )
        scaled = jnp.concatenate((mine_scaled_ref[...], other_scaled_ref[...]), axis=0)
        back_ref[...] += lax.dot_general(
            down, scaled, contract_last, preferred_element_type=jnp.float32
        )

    @pl.when(step == steps - 1)
    def _():
        pre_act = pre_ref[...] * inv_model
        sigmoid_act = 1.0 / (1.0 + jnp.exp(-pre_act))
        delta = (
            back_ref[...] * inv_hidden * sigmoid_act * (1.0 + pre_act * (1.0 - sigmoid_act))
        ).astype(jnp.bfloat16)
        left_ref[0] = delta
        left_ref[1] = (pre_act * sigmoid_act).astype(jnp.bfloat16)
        delta_ref[...] = delta.T

    @pl.when(step >= steps)
    def _():
        pair = jnp.dot(delta_ref[...], up, preferred_element_type=jnp.float32) * inv_model
        pair_ref[...] = pair[:rows]
        pair_other_ref[...] = pair[rows:].astype(jnp.bfloat16)


def expert_stage(mine, other, mine_scaled, other_scaled, weights, inv_model, inv_hidden):
    rows, width = mine.shape
    chips, both, _ = weights.shape
    hidden = chips * both // 2
    block = 512
    steps = width // block

    def early(i):
        return jnp.minimum(i, steps - 1)

    def late(i):
        return jnp.maximum(i - steps, 0)

    row_spec = pl.BlockSpec((rows, block), lambda i: (0, early(i)))
    late_spec = pl.BlockSpec((rows, block), lambda i: (0, late(i)))
    return pl.pallas_call(
        functools.partial(expert_kernel, steps, inv_model, inv_hidden),
        grid=(2 * steps,),
        in_specs=[row_spec] * 4 + [pl.BlockSpec((chips, both, block), lambda i: (0, 0, i % steps))],
        out_specs=[
            late_spec,
            late_spec,
            pl.BlockSpec((2, hidden, 2 * rows), lambda i: (0, 0, 0)),
        ],
        out_shape=[
            jax.ShapeDtypeStruct((rows, width), jnp.float32),
            jax.ShapeDtypeStruct((rows, width), jnp.bfloat16),
            jax.ShapeDtypeStruct((2, hidden, 2 * rows), jnp.bfloat16),
        ],
        scratch_shapes=[
            pltpu.VMEM((hidden, 2 * rows), jnp.float32),
            pltpu.VMEM((hidden, 2 * rows), jnp.float32),
            pltpu.VMEM((2 * rows, hidden), jnp.bfloat16),
        ],
        compiler_params=pltpu.CompilerParams(
            dimension_semantics=("arbitrary",), vmem_limit_bytes=40 * 1024 * 1024
        ),
        cost_estimate=pl.CostEstimate(
            flops=12 * rows * hidden * width, bytes_accessed=32 * rows * width, transcendentals=0
        ),
    )(mine, other, mine_scaled, other_scaled, weights)


def weight_kernel(
    inv_model,
    inv_hidden,
    left_ref,
    mine_ref,
    other_ref,
    mine_scaled_ref,
    other_scaled_ref,
    part_ref,
):
    chips, both, _ = part_ref.shape
    local = both // 2
    for kind, mine, other, scale in (
        (0, mine_ref, other_ref, inv_model),
        (1, mine_scaled_ref, other_scaled_ref, inv_hidden),
    ):
        right = jnp.concatenate((mine[...], other[...]), axis=0)
        part = jnp.dot(left_ref[kind], right, preferred_element_type=jnp.float32) * scale
        part = part.astype(jnp.bfloat16)
        for i in range(chips):
            part_ref[i, kind * local : (kind + 1) * local] = part[i * local : (i + 1) * local]


def weight_stage(left, mine, other, mine_scaled, other_scaled, chips, inv_model, inv_hidden):
    rows, width = mine.shape
    both = 2 * left.shape[1] // chips
    block = 512
    row_spec = pl.BlockSpec((rows, block), lambda i: (0, i))
    return pl.pallas_call(
        functools.partial(weight_kernel, inv_model, inv_hidden),
        grid=(width // block,),
        in_specs=[pl.BlockSpec(left.shape, lambda i: (0, 0, 0))] + [row_spec] * 4,
        out_specs=pl.BlockSpec((chips, both, block), lambda i: (0, 0, i)),
        out_shape=jax.ShapeDtypeStruct((chips, both, width), jnp.bfloat16),
        compiler_params=pltpu.CompilerParams(
            dimension_semantics=("arbitrary",), vmem_limit_bytes=40 * 1024 * 1024
        ),
        cost_estimate=pl.CostEstimate(flops=0, bytes_accessed=1024, transcendentals=0),
    )(left, mine, other, mine_scaled, other_scaled)


def on_device(
    tokens,
    out_grad,
    routes,
    probs,
    swap_flags,
    up_weight,
    down_weight,
    up_first,
    up_second,
    down_first,
    down_second,
):
    model_width = tokens.shape[1]
    high = lax.axis_size(HIGH)
    side = lax.axis_size(SIDE)
    experts = high * side
    ring = lax.axis_size(RING)
    near = lax.axis_size(NEAR)
    chips = ring * near
    half_axis = experts // 2
    capacity = max(2, routes.size * 5 // (4 * experts))
    side_rows = high * capacity
    high_rows = side * capacity
    buffer_rows = experts * capacity
    local_hidden = up_weight.shape[1]
    hidden_units = local_hidden * chips * lax.axis_size(CORE)
    inv_model = model_width ** (-0.5)
    inv_hidden = hidden_units ** (-0.5)
    my_high = lax.axis_index(HIGH)
    my_index = my_high * side + lax.axis_index(SIDE)
    expert_ids = jnp.arange(experts, dtype=jnp.int32)
    flag_mine = jnp.sum(jnp.where(expert_ids == my_index, swap_flags, 0))
    swapped = flag_mine == 1

    weights = jnp.concatenate((up_weight[0], down_weight[0]), axis=0)
    weights_partner = partner(weights, FAR, 1)

    send_tokens, send_scaled, token_select = dispatch(
        swap_flags, routes, probs, tokens, out_grad, capacity
    )
    buffer_ids = jnp.arange(buffer_rows, dtype=jnp.int32)
    other_order = (
        (buffer_ids // capacity % high) * side_rows
        + (buffer_ids // side_rows) * capacity
        + buffer_ids % capacity
    )
    regroup = (buffer_ids[None, :] == other_order[:, None]).astype(jnp.bfloat16)

    def along_side(rows):
        return lax.all_to_all(
            rows.reshape(side, side_rows, model_width),
            SIDE,
            split_axis=0,
            concat_axis=0,
            tiled=True,
        ).reshape(buffer_rows, model_width)

    def pick(matrix, rows):
        return jnp.dot(matrix, rows, preferred_element_type=jnp.float32).astype(jnp.bfloat16)

    ways = z_routes()

    def along_high(rows, back):
        blocks = [rows[i * high_rows : (i + 1) * high_rows] for i in range(high)]
        moved = [
            lax.ppermute(
                array, (NEAR, *HIGH), [(b, a) for a, b in way] if back else way
            )
            for array, way in zip(blocks[1:], ways)
        ]
        return jnp.concatenate(blocks[:1] + moved, axis=0), moved[-1]

    token_rows = pick(regroup, along_side(send_tokens))
    side_scaled = along_side(send_scaled)
    scaled_rows = pick(regroup, side_scaled)

    rows_mine, farthest = along_high(token_rows, False)

    weights = jnp.where(swapped, weights_partner, weights)
    weights, _ = lax.optimization_barrier((weights, token_rows))
    both = jnp.stack((weights, partner(weights, NEAR, 1)), axis=0)
    both, _, _ = lax.optimization_barrier((both, side_scaled, farthest))
    gathered = lax.all_gather(both, RING, axis=0).reshape(
        chips, 2 * local_hidden, model_width
    )

    scaled_mine, _ = along_high(scaled_rows, False)
    rows_other = partner(rows_mine, CORE, 1)
    scaled_other = partner(scaled_mine, CORE, 1)
    moments = (up_first[0], up_second[0], down_first[0], down_second[0])

    rounded = tuple(array.astype(jnp.bfloat16) for array in moments)
    up_held, _ = lax.optimization_barrier((rounded[:2], scaled_mine))
    up_arrived = tuple(partner(array, FAR, 1) for array in up_held)
    pair_mine, for_other, left = expert_stage(
        rows_mine, rows_other, scaled_mine, scaled_other, gathered, inv_model, inv_hidden
    )
    parts = weight_stage(
        left, rows_mine, rows_other, scaled_mine, scaled_other, chips, inv_model, inv_hidden
    )
    from_other = partner(for_other, CORE, 1)
    pair_grad = (pair_mine + from_other.astype(jnp.float32)).astype(jnp.bfloat16)
    up_arrived, parts = lax.optimization_barrier((up_arrived, parts))
    back_rows, _ = along_high(pair_grad, True)
    down_held, back_rows = lax.optimization_barrier((rounded[2:], back_rows))
    down_arrived = tuple(partner(array, FAR, 1) for array in down_held)
    returned = along_side(pick(regroup, back_rows))
    token_grad = lax.dot_general(
        token_select, returned, (((0,), (0,)), ((), ())), preferred_element_type=jnp.float32
    ).astype(jnp.bfloat16)

    own, beside = lax.psum_scatter(
        parts.reshape(ring, near, 2 * local_hidden, model_width),
        RING,
        scatter_dimension=0,
        tiled=False,
    )
    down_arrived, beside = lax.optimization_barrier((down_arrived, beside))
    arrived = (*up_arrived, *down_arrived)
    summed = own.astype(jnp.float32) + partner(beside, NEAR, 1).astype(jnp.float32)
    moments = tuple(
        jnp.where(swapped, new.astype(jnp.float32), old) for new, old in zip(arrived, moments)
    )
    new_up, up_first_new, up_second_new = adam_update(
        weights[:local_hidden], moments[0], moments[1], summed[:local_hidden]
    )
    new_down, down_first_new, down_second_new = adam_update(
        weights[local_hidden:], moments[2], moments[3], summed[local_hidden:]
    )
    return (
        token_grad,
        new_up[None],
        new_down[None],
        up_first_new[None],
        up_second_new[None],
        down_first_new[None],
        down_second_new[None],
    )


def solution(mesh):
    dp, expert = (mesh.shape[name] for name in ("dp", "expert"))
    fine = Mesh(
        mesh.devices.reshape(2, dp // 4, 2, 2, HIGHS // 2, expert // HIGHS),
        (NEAR, RING, CORE, *HIGH, SIDE),
    )
    rows = P((NEAR, RING, CORE, *HIGH, SIDE), None)
    slots = P((*HIGH, SIDE), (NEAR, RING, CORE), None)
    return jax.shard_map(
        on_device,
        mesh=fine,
        in_specs=(rows, rows, rows, rows, P()) + (slots,) * 6,
        out_specs=(rows,) + (slots,) * 6,
        check_vma=False,
    )
```

```python
import functools

import jax
import jax.numpy as jnp
from jax import lax
from jax.experimental import pallas as pl
from jax.experimental.pallas import tpu as pltpu
from jax.sharding import Mesh
from jax.sharding import PartitionSpec as P

ADAM_STEP = 20


beta_first = 0.9
beta_second = 0.95
step_size = 0.05
adam_epsilon = 1e-08

NEAR = "near"
RING = "ring"
CORE = "core"
FAR = "far"
STEP = "step"
HIGH = (FAR, STEP)
SIDE = "side"
HIGHS = 4


def partner(array, axis, flip):
    return lax.ppermute(array, axis, [(i, i ^ flip) for i in range(lax.axis_size(axis))])


def z_routes():
    routes = []
    for step, crosses in ((1, False), (-1, True), (2, True)):
        pairs = []
        for near in range(2):
            sign = 1 if near == 0 else -1
            for high in range(HIGHS):
                other = (1 - near) if crosses else near
                pairs.append((near * HIGHS + high, other * HIGHS + (high + sign * step) % HIGHS))
        routes.append(pairs)
    return routes


def adam_update(weight, first, second, gradient):
    first_new = beta_first * first + (1.0 - beta_first) * gradient
    second_new = beta_second * second + (1.0 - beta_second) * gradient * gradient
    corr_first = 1.0 - beta_first**ADAM_STEP
    corr_second = 1.0 - beta_second**ADAM_STEP
    stepped = weight.astype(jnp.float32) - step_size * (first_new / corr_first) / (
        jnp.sqrt(second_new / corr_second) + adam_epsilon
    )
    return (stepped.astype(jnp.bfloat16), first_new, second_new)


def dispatch_kernel(
    capacity,
    flags_ref,
    routes_ref,
    probs_ref,
    tokens_ref,
    out_grad_ref,
    token_rows_ref,
    scaled_rows_ref,
    select_ref,
):
    tops, count = routes_ref.shape
    experts = flags_ref.shape[0]
    rows, width = token_rows_ref.shape
    side = experts // HIGHS
    half_axis = experts // 2
    my_high = lax.axis_index(FAR) * (HIGHS // 2) + lax.axis_index(STEP)
    my_near = lax.axis_index(NEAR)
    ids = lax.broadcasted_iota(jnp.int32, (experts, 1), 0)
    slot = jnp.where(flags_ref[...] == 1, jnp.bitwise_xor(ids, half_axis), ids)
    away = lax.shift_right_logical(slot, side.bit_length() - 1) - my_high
    away = jnp.bitwise_and(jnp.where(my_near == 0, away, -away), HIGHS - 1)
    block = jnp.where(away >= 2, 5 - away, away)
    base = jnp.bitwise_and(slot, side - 1) * (HIGHS * capacity) + block * capacity
    base = base.astype(jnp.float32)
    expert_ids = lax.broadcasted_iota(jnp.int32, (experts, count), 0)
    before = (
        lax.broadcasted_iota(jnp.int32, (count, count), 0)
        < lax.broadcasted_iota(jnp.int32, (count, count), 1)
    )
    before = jnp.where(before, 1.0, 0.0).astype(jnp.bfloat16)
    row_ids = lax.broadcasted_iota(jnp.int32, (rows, count), 0)
    token_pick = jnp.zeros((rows, count), jnp.float32)
    prob_pick = jnp.zeros((rows, count), jnp.float32)
    for k in range(tops):
        onehot = jnp.where(routes_ref[k : k + 1] == expert_ids, 1.0, 0.0)
        earlier = jnp.dot(onehot.astype(jnp.bfloat16), before, preferred_element_type=jnp.float32)
        row = jnp.sum(onehot * (base + earlier), axis=0, keepdims=True).astype(jnp.int32)
        hit = row_ids == row
        token_pick = token_pick + jnp.where(hit, 1.0, 0.0)
        prob_pick = prob_pick + jnp.where(hit, probs_ref[k : k + 1].astype(jnp.float32), 0.0)
        base = base + jnp.sum(onehot, axis=1, keepdims=True)
    token_pick = token_pick.astype(jnp.bfloat16)
    prob_pick = prob_pick.astype(jnp.bfloat16)
    select_ref[...] = token_pick
    piece = 512
    for at in range(0, width, piece):
        cut = slice(at, min(at + piece, width))
        for pick, source, target in (
            (token_pick, tokens_ref, token_rows_ref),
            (prob_pick, out_grad_ref, scaled_rows_ref),
        ):
            target[:, cut] = jnp.dot(
                pick, source[:, cut], preferred_element_type=jnp.float32
            ).astype(jnp.bfloat16)


def dispatch(swap_flags, routes, probs, tokens, out_grad, capacity):
    count, width = tokens.shape
    rows = swap_flags.shape[0] * capacity
    whole = pl.BlockSpec(memory_space=pltpu.VMEM)
    return pl.pallas_call(
        functools.partial(dispatch_kernel, capacity),
        in_specs=[whole] * 5,
        out_specs=[whole] * 3,
        out_shape=[
            jax.ShapeDtypeStruct((rows, width), jnp.bfloat16),
            jax.ShapeDtypeStruct((rows, width), jnp.bfloat16),
            jax.ShapeDtypeStruct((rows, count), jnp.bfloat16),
        ],
        compiler_params=pltpu.CompilerParams(vmem_limit_bytes=24 * 1024 * 1024),
        cost_estimate=pl.CostEstimate(flops=0, bytes_accessed=1024, transcendentals=0),
    )(swap_flags.reshape(-1, 1), routes.T, probs.T, tokens, out_grad)


def expert_kernel(
    steps,
    inv_model,
    inv_hidden,
    mine_ref,
    other_ref,
    mine_scaled_ref,
    other_scaled_ref,
    weight_ref,
    pair_ref,
    pair_other_ref,
    left_ref,
    pre_ref,
    back_ref,
    delta_ref,
):
    step = pl.program_id(0)
    chips, both, _ = weight_ref.shape
    local = both // 2
    rows = mine_ref.shape[0]
    contract_last = (((1,), (1,)), ((), ()))
    up = jnp.concatenate([weight_ref[i, :local] for i in range(chips)], axis=0)

    @pl.when(step == 0)
    def _():
        pre_ref[...] = jnp.zeros_like(pre_ref)
        back_ref[...] = jnp.zeros_like(back_ref)

    @pl.when(step < steps)
    def _():
        down = jnp.concatenate([weight_ref[i, local:] for i in range(chips)], axis=0)
        token = jnp.concatenate((mine_ref[...], other_ref[...]), axis=0)
        pre_ref[...] += lax.dot_general(
            up, token, contract_last, preferred_element_type=jnp.float32
        )
        scaled = jnp.concatenate((mine_scaled_ref[...], other_scaled_ref[...]), axis=0)
        back_ref[...] += lax.dot_general(
            down, scaled, contract_last, preferred_element_type=jnp.float32
        )

    @pl.when(step == steps - 1)
    def _():
        pre_act = pre_ref[...] * inv_model
        sigmoid_act = 1.0 / (1.0 + jnp.exp(-pre_act))
        delta = (
            back_ref[...] * inv_hidden * sigmoid_act * (1.0 + pre_act * (1.0 - sigmoid_act))
        ).astype(jnp.bfloat16)
        left_ref[0] = delta
        left_ref[1] = (pre_act * sigmoid_act).astype(jnp.bfloat16)
        delta_ref[...] = delta.T

    @pl.when(step >= steps)
    def _():
        pair = jnp.dot(delta_ref[...], up, preferred_element_type=jnp.float32) * inv_model
        pair_ref[...] = pair[:rows]
        pair_other_ref[...] = pair[rows:].astype(jnp.bfloat16)


def expert_stage(mine, other, mine_scaled, other_scaled, weights, inv_model, inv_hidden):
    rows, width = mine.shape
    chips, both, _ = weights.shape
    hidden = chips * both // 2
    block = 512
    steps = width // block

    def early(i):
        return jnp.minimum(i, steps - 1)

    def late(i):
        return jnp.maximum(i - steps, 0)

    row_spec = pl.BlockSpec((rows, block), lambda i: (0, early(i)))
    late_spec = pl.BlockSpec((rows, block), lambda i: (0, late(i)))
    return pl.pallas_call(
        functools.partial(expert_kernel, steps, inv_model, inv_hidden),
        grid=(2 * steps,),
        in_specs=[row_spec] * 4 + [pl.BlockSpec((chips, both, block), lambda i: (0, 0, i % steps))],
        out_specs=[
            late_spec,
            late_spec,
            pl.BlockSpec((2, hidden, 2 * rows), lambda i: (0, 0, 0)),
        ],
        out_shape=[
            jax.ShapeDtypeStruct((rows, width), jnp.float32),
            jax.ShapeDtypeStruct((rows, width), jnp.bfloat16),
            jax.ShapeDtypeStruct((2, hidden, 2 * rows), jnp.bfloat16),
        ],
        scratch_shapes=[
            pltpu.VMEM((hidden, 2 * rows), jnp.float32),
            pltpu.VMEM((hidden, 2 * rows), jnp.float32),
            pltpu.VMEM((2 * rows, hidden), jnp.bfloat16),
        ],
        compiler_params=pltpu.CompilerParams(
            dimension_semantics=("arbitrary",), vmem_limit_bytes=60 * 1024 * 1024
        ),
        cost_estimate=pl.CostEstimate(
            flops=12 * rows * hidden * width, bytes_accessed=32 * rows * width, transcendentals=0
        ),
    )(mine, other, mine_scaled, other_scaled, weights)


def weight_kernel(
    inv_model,
    inv_hidden,
    left_ref,
    mine_ref,
    other_ref,
    mine_scaled_ref,
    other_scaled_ref,
    part_ref,
):
    chips, both, _ = part_ref.shape
    local = both // 2
    for kind, mine, other, scale in (
        (0, mine_ref, other_ref, inv_model),
        (1, mine_scaled_ref, other_scaled_ref, inv_hidden),
    ):
        right = jnp.concatenate((mine[...], other[...]), axis=0)
        part = jnp.dot(left_ref[kind], right, preferred_element_type=jnp.float32) * scale
        part = part.astype(jnp.bfloat16)
        for i in range(chips):
            part_ref[i, kind * local : (kind + 1) * local] = part[i * local : (i + 1) * local]


def weight_stage(left, mine, other, mine_scaled, other_scaled, chips, inv_model, inv_hidden):
    rows, width = mine.shape
    both = 2 * left.shape[1] // chips
    block = 512
    row_spec = pl.BlockSpec((rows, block), lambda i: (0, i))
    return pl.pallas_call(
        functools.partial(weight_kernel, inv_model, inv_hidden),
        grid=(width // block,),
        in_specs=[pl.BlockSpec(left.shape, lambda i: (0, 0, 0))] + [row_spec] * 4,
        out_specs=pl.BlockSpec((chips, both, block), lambda i: (0, 0, i)),
        out_shape=jax.ShapeDtypeStruct((chips, both, width), jnp.bfloat16),
        compiler_params=pltpu.CompilerParams(
            dimension_semantics=("arbitrary",), vmem_limit_bytes=60 * 1024 * 1024
        ),
        cost_estimate=pl.CostEstimate(flops=0, bytes_accessed=1024, transcendentals=0),
    )(left, mine, other, mine_scaled, other_scaled)


def on_device(
    tokens,
    out_grad,
    routes,
    probs,
    swap_flags,
    up_weight,
    down_weight,
    up_first,
    up_second,
    down_first,
    down_second,
):
    model_width = tokens.shape[1]
    high = lax.axis_size(HIGH)
    side = lax.axis_size(SIDE)
    experts = high * side
    ring = lax.axis_size(RING)
    near = lax.axis_size(NEAR)
    chips = ring * near
    half_axis = experts // 2
    capacity = max(2, routes.size * 5 // (4 * experts))
    side_rows = high * capacity
    high_rows = side * capacity
    buffer_rows = experts * capacity
    local_hidden = up_weight.shape[1]
    hidden_units = local_hidden * chips * lax.axis_size(CORE)
    inv_model = model_width ** (-0.5)
    inv_hidden = hidden_units ** (-0.5)
    my_high = lax.axis_index(HIGH)
    my_index = my_high * side + lax.axis_index(SIDE)
    expert_ids = jnp.arange(experts, dtype=jnp.int32)
    flag_mine = jnp.sum(jnp.where(expert_ids == my_index, swap_flags, 0))
    swapped = flag_mine == 1

    weights = jnp.concatenate((up_weight[0], down_weight[0]), axis=0)
    weights_partner = partner(weights, FAR, 1)

    send_tokens, send_scaled, token_select = dispatch(
        swap_flags, routes, probs, tokens, out_grad, capacity
    )
    buffer_ids = jnp.arange(buffer_rows, dtype=jnp.int32)
    other_order = (
        (buffer_ids // capacity % high) * side_rows
        + (buffer_ids // side_rows) * capacity
        + buffer_ids % capacity
    )
    regroup = (buffer_ids[None, :] == other_order[:, None]).astype(jnp.bfloat16)

    def along_side(rows):
        return lax.all_to_all(
            rows.reshape(side, side_rows, model_width),
            SIDE,
            split_axis=0,
            concat_axis=0,
            tiled=True,
        ).reshape(buffer_rows, model_width)

    def pick(matrix, rows):
        return jnp.dot(matrix, rows, preferred_element_type=jnp.float32).astype(jnp.bfloat16)

    ways = z_routes()

    def along_high(rows, back):
        blocks = [rows[i * high_rows : (i + 1) * high_rows] for i in range(high)]
        moved = [
            lax.ppermute(
                array, (NEAR, *HIGH), [(b, a) for a, b in way] if back else way
            )
            for array, way in zip(blocks[1:], ways)
        ]
        return jnp.concatenate(blocks[:1] + moved, axis=0), moved[-1]

    token_rows = pick(regroup, along_side(send_tokens))
    side_scaled = along_side(send_scaled)
    scaled_rows = pick(regroup, side_scaled)

    rows_mine, farthest = along_high(token_rows, False)

    weights = jnp.where(swapped, weights_partner, weights)
    weights, _ = lax.optimization_barrier((weights, token_rows))
    both = jnp.stack((weights, partner(weights, NEAR, 1)), axis=0)
    both, _, _ = lax.optimization_barrier((both, side_scaled, farthest))
    gathered = lax.all_gather(both, RING, axis=0).reshape(
        chips, 2 * local_hidden, model_width
    )

    scaled_mine, _ = along_high(scaled_rows, False)
    rows_other = partner(rows_mine, CORE, 1)
    scaled_other = partner(scaled_mine, CORE, 1)
    moments = (up_first[0], up_second[0], down_first[0], down_second[0])

    rounded = tuple(array.astype(jnp.bfloat16) for array in moments)
    up_held, _ = lax.optimization_barrier((rounded[:2], scaled_mine))
    up_arrived = tuple(partner(array, FAR, 1) for array in up_held)
    pair_mine, for_other, left = expert_stage(
        rows_mine, rows_other, scaled_mine, scaled_other, gathered, inv_model, inv_hidden
    )
    parts = weight_stage(
        left, rows_mine, rows_other, scaled_mine, scaled_other, chips, inv_model, inv_hidden
    )
    from_other = partner(for_other, CORE, 1)
    pair_grad = (pair_mine + from_other.astype(jnp.float32)).astype(jnp.bfloat16)
    up_arrived, parts = lax.optimization_barrier((up_arrived, parts))
    down_held, _ = lax.optimization_barrier((rounded[2], parts))
    down_arrived = partner(down_held, FAR, 1)
    down_arrived, pair_grad = lax.optimization_barrier((down_arrived, pair_grad))
    back_rows, _ = along_high(pair_grad, True)
    late_held, back_rows = lax.optimization_barrier((rounded[3], back_rows))
    late_arrived = partner(late_held, FAR, 1)
    returned = along_side(pick(regroup, back_rows))
    late_arrived, returned = lax.optimization_barrier((late_arrived, returned))
    token_grad = lax.dot_general(
        token_select, returned, (((0,), (0,)), ((), ())), preferred_element_type=jnp.float32
    ).astype(jnp.bfloat16)

    own, beside = lax.psum_scatter(
        parts.reshape(ring, near, 2 * local_hidden, model_width),
        RING,
        scatter_dimension=0,
        tiled=False,
    )
    arrived = (*up_arrived, down_arrived, late_arrived)
    summed = own.astype(jnp.float32) + partner(beside, NEAR, 1).astype(jnp.float32)
    moments = tuple(
        jnp.where(swapped, new.astype(jnp.float32), old) for new, old in zip(arrived, moments)
    )
    new_up, up_first_new, up_second_new = adam_update(
        weights[:local_hidden], moments[0], moments[1], summed[:local_hidden]
    )
    new_down, down_first_new, down_second_new = adam_update(
        weights[local_hidden:], moments[2], moments[3], summed[local_hidden:]
    )
    return (
        token_grad,
        new_up[None],
        new_down[None],
        up_first_new[None],
        up_second_new[None],
        down_first_new[None],
        down_second_new[None],
    )


def solution(mesh):
    dp, expert = (mesh.shape[name] for name in ("dp", "expert"))
    fine = Mesh(
        mesh.devices.reshape(2, dp // 4, 2, 2, HIGHS // 2, expert // HIGHS),
        (NEAR, RING, CORE, *HIGH, SIDE),
    )
    rows = P((NEAR, RING, CORE, *HIGH, SIDE), None)
    slots = P((*HIGH, SIDE), (NEAR, RING, CORE), None)
    return jax.shard_map(
        on_device,
        mesh=fine,
        in_specs=(rows, rows, rows, rows, P()) + (slots,) * 6,
        out_specs=(rows,) + (slots,) * 6,
        check_vma=False,
    )
```

```python
import functools

import jax
import jax.numpy as jnp
from jax import lax
from jax.experimental import pallas as pl
from jax.experimental.pallas import tpu as pltpu
from jax.sharding import Mesh
from jax.sharding import PartitionSpec as P

ADAM_STEP = 20


beta_first = 0.9
beta_second = 0.95
step_size = 0.05
adam_epsilon = 1e-08

NEAR = "near"
RING = "ring"
CORE = "core"
FAR = "far"
STEP = "step"
HIGH = (FAR, STEP)
SIDE = "side"
HIGHS = 4


def partner(array, axis, flip):
    return lax.ppermute(array, axis, [(i, i ^ flip) for i in range(lax.axis_size(axis))])


def z_routes():
    routes = []
    for step, crosses in ((1, False), (-1, True), (2, True)):
        pairs = []
        for near in range(2):
            sign = 1 if near == 0 else -1
            for high in range(HIGHS):
                other = (1 - near) if crosses else near
                pairs.append((near * HIGHS + high, other * HIGHS + (high + sign * step) % HIGHS))
        routes.append(pairs)
    return routes


def adam_update(weight, first, second, gradient):
    first_new = beta_first * first + (1.0 - beta_first) * gradient
    second_new = beta_second * second + (1.0 - beta_second) * gradient * gradient
    corr_first = 1.0 - beta_first**ADAM_STEP
    corr_second = 1.0 - beta_second**ADAM_STEP
    stepped = weight.astype(jnp.float32) - step_size * (first_new / corr_first) / (
        jnp.sqrt(second_new / corr_second) + adam_epsilon
    )
    return (stepped.astype(jnp.bfloat16), first_new, second_new)


def dispatch_kernel(
    capacity,
    flags_ref,
    routes_ref,
    probs_ref,
    tokens_ref,
    out_grad_ref,
    token_rows_ref,
    scaled_rows_ref,
    select_ref,
):
    tops, count = routes_ref.shape
    experts = flags_ref.shape[0]
    rows, width = token_rows_ref.shape
    side = experts // HIGHS
    half_axis = experts // 2
    my_high = lax.axis_index(FAR) * (HIGHS // 2) + lax.axis_index(STEP)
    my_near = lax.axis_index(NEAR)
    ids = lax.broadcasted_iota(jnp.int32, (experts, 1), 0)
    slot = jnp.where(flags_ref[...] == 1, jnp.bitwise_xor(ids, half_axis), ids)
    away = lax.shift_right_logical(slot, side.bit_length() - 1) - my_high
    away = jnp.bitwise_and(jnp.where(my_near == 0, away, -away), HIGHS - 1)
    block = jnp.where(away >= 2, 5 - away, away)
    base = jnp.bitwise_and(slot, side - 1) * (HIGHS * capacity) + block * capacity
    base = base.astype(jnp.float32)
    expert_ids = lax.broadcasted_iota(jnp.int32, (experts, count), 0)
    before = (
        lax.broadcasted_iota(jnp.int32, (count, count), 0)
        < lax.broadcasted_iota(jnp.int32, (count, count), 1)
    )
    before = jnp.where(before, 1.0, 0.0).astype(jnp.bfloat16)
    row_ids = lax.broadcasted_iota(jnp.int32, (rows, count), 0)
    token_pick = jnp.zeros((rows, count), jnp.float32)
    prob_pick = jnp.zeros((rows, count), jnp.float32)
    for k in range(tops):
        onehot = jnp.where(routes_ref[k : k + 1] == expert_ids, 1.0, 0.0)
        earlier = jnp.dot(onehot.astype(jnp.bfloat16), before, preferred_element_type=jnp.float32)
        row = jnp.sum(onehot * (base + earlier), axis=0, keepdims=True).astype(jnp.int32)
        hit = row_ids == row
        token_pick = token_pick + jnp.where(hit, 1.0, 0.0)
        prob_pick = prob_pick + jnp.where(hit, probs_ref[k : k + 1].astype(jnp.float32), 0.0)
        base = base + jnp.sum(onehot, axis=1, keepdims=True)
    token_pick = token_pick.astype(jnp.bfloat16)
    prob_pick = prob_pick.astype(jnp.bfloat16)
    select_ref[...] = token_pick
    piece = 512
    for at in range(0, width, piece):
        cut = slice(at, min(at + piece, width))
        for pick, source, target in (
            (token_pick, tokens_ref, token_rows_ref),
            (prob_pick, out_grad_ref, scaled_rows_ref),
        ):
            target[:, cut] = jnp.dot(
                pick, source[:, cut], preferred_element_type=jnp.float32
            ).astype(jnp.bfloat16)


def dispatch(swap_flags, routes, probs, tokens, out_grad, capacity):
    count, width = tokens.shape
    rows = swap_flags.shape[0] * capacity
    whole = pl.BlockSpec(memory_space=pltpu.VMEM)
    return pl.pallas_call(
        functools.partial(dispatch_kernel, capacity),
        in_specs=[whole] * 5,
        out_specs=[whole] * 3,
        out_shape=[
            jax.ShapeDtypeStruct((rows, width), jnp.bfloat16),
            jax.ShapeDtypeStruct((rows, width), jnp.bfloat16),
            jax.ShapeDtypeStruct((rows, count), jnp.bfloat16),
        ],
        compiler_params=pltpu.CompilerParams(vmem_limit_bytes=24 * 1024 * 1024),
        cost_estimate=pl.CostEstimate(flops=0, bytes_accessed=1024, transcendentals=0),
    )(swap_flags.reshape(-1, 1), routes.T, probs.T, tokens, out_grad)


def expert_kernel(
    steps,
    inv_model,
    inv_hidden,
    mine_ref,
    other_ref,
    mine_scaled_ref,
    other_scaled_ref,
    weight_ref,
    delta_ref,
    delta_other_ref,
    left_ref,
    pre_ref,
    back_ref,
):
    step = pl.program_id(0)
    chips, both, _ = weight_ref.shape
    local = both // 2
    rows = mine_ref.shape[0]
    contract_last = (((1,), (1,)), ((), ()))

    @pl.when(step == 0)
    def _():
        pre_ref[...] = jnp.zeros_like(pre_ref)
        back_ref[...] = jnp.zeros_like(back_ref)

    up = jnp.concatenate([weight_ref[i, :local] for i in range(chips)], axis=0)
    token = jnp.concatenate((mine_ref[...], other_ref[...]), axis=0)
    pre_ref[...] += lax.dot_general(up, token, contract_last, preferred_element_type=jnp.float32)
    down = jnp.concatenate([weight_ref[i, local:] for i in range(chips)], axis=0)
    scaled = jnp.concatenate((mine_scaled_ref[...], other_scaled_ref[...]), axis=0)
    back_ref[...] += lax.dot_general(
        down, scaled, contract_last, preferred_element_type=jnp.float32
    )

    @pl.when(step == steps - 1)
    def _():
        pre_act = pre_ref[...] * inv_model
        sigmoid_act = 1.0 / (1.0 + jnp.exp(-pre_act))
        delta = (
            back_ref[...] * inv_hidden * sigmoid_act * (1.0 + pre_act * (1.0 - sigmoid_act))
        ).astype(jnp.bfloat16)
        left_ref[0] = delta
        left_ref[1] = (pre_act * sigmoid_act).astype(jnp.bfloat16)
        turned = delta.T
        delta_ref[...] = turned[:rows]
        delta_other_ref[...] = turned[rows:]


def expert_stage(mine, other, mine_scaled, other_scaled, weights, inv_model, inv_hidden):
    rows, width = mine.shape
    chips, both, _ = weights.shape
    hidden = chips * both // 2
    block = 896
    steps = width // block
    row_spec = pl.BlockSpec((rows, block), lambda i: (0, i))
    delta_spec = pl.BlockSpec((rows, hidden), lambda i: (0, 0))
    return pl.pallas_call(
        functools.partial(expert_kernel, steps, inv_model, inv_hidden),
        grid=(steps,),
        in_specs=[row_spec] * 4 + [pl.BlockSpec((chips, both, block), lambda i: (0, 0, i))],
        out_specs=[
            delta_spec,
            delta_spec,
            pl.BlockSpec((2, hidden, 2 * rows), lambda i: (0, 0, 0)),
        ],
        out_shape=[
            jax.ShapeDtypeStruct((rows, hidden), jnp.bfloat16),
            jax.ShapeDtypeStruct((rows, hidden), jnp.bfloat16),
            jax.ShapeDtypeStruct((2, hidden, 2 * rows), jnp.bfloat16),
        ],
        scratch_shapes=[
            pltpu.VMEM((hidden, 2 * rows), jnp.float32),
            pltpu.VMEM((hidden, 2 * rows), jnp.float32),
        ],
        compiler_params=pltpu.CompilerParams(
            dimension_semantics=("arbitrary",), vmem_limit_bytes=60 * 1024 * 1024
        ),
        cost_estimate=pl.CostEstimate(
            flops=12 * rows * hidden * width, bytes_accessed=32 * rows * width, transcendentals=0
        ),
    )(mine, other, mine_scaled, other_scaled, weights)


def pair_kernel(inv_model, delta_ref, delta_other_ref, weight_ref, pair_ref, pair_other_ref):
    chips, both, _ = weight_ref.shape
    local = both // 2
    up = jnp.concatenate([weight_ref[i, :local] for i in range(chips)], axis=0)
    rows = delta_ref.shape[0]
    delta = jnp.concatenate((delta_ref[...], delta_other_ref[...]), axis=0)
    pair = jnp.dot(delta, up, preferred_element_type=jnp.float32) * inv_model
    pair_ref[...] = pair[:rows]
    pair_other_ref[...] = pair[rows:].astype(jnp.bfloat16)


def pair_stage(delta, delta_other, weights, inv_model):
    rows, hidden = delta.shape
    chips, both, width = weights.shape
    block = 896
    delta_spec = pl.BlockSpec((rows, hidden), lambda i: (0, 0))
    pair_spec = pl.BlockSpec((rows, block), lambda i: (0, i))
    return pl.pallas_call(
        functools.partial(pair_kernel, inv_model),
        grid=(width // block,),
        in_specs=[
            delta_spec,
            delta_spec,
            pl.BlockSpec((chips, both, block), lambda i: (0, 0, i)),
        ],
        out_specs=[pair_spec, pair_spec],
        out_shape=[
            jax.ShapeDtypeStruct((rows, width), jnp.float32),
            jax.ShapeDtypeStruct((rows, width), jnp.bfloat16),
        ],
        compiler_params=pltpu.CompilerParams(
            dimension_semantics=("arbitrary",), vmem_limit_bytes=60 * 1024 * 1024
        ),
        cost_estimate=pl.CostEstimate(flops=0, bytes_accessed=1024, transcendentals=0),
    )(delta, delta_other, weights)


def weight_kernel(
    inv_model,
    inv_hidden,
    left_ref,
    mine_ref,
    other_ref,
    mine_scaled_ref,
    other_scaled_ref,
    part_ref,
):
    chips, both, _ = part_ref.shape
    local = both // 2
    for kind, mine, other, scale in (
        (0, mine_ref, other_ref, inv_model),
        (1, mine_scaled_ref, other_scaled_ref, inv_hidden),
    ):
        right = jnp.concatenate((mine[...], other[...]), axis=0)
        part = jnp.dot(left_ref[kind], right, preferred_element_type=jnp.float32) * scale
        part = part.astype(jnp.bfloat16)
        for i in range(chips):
            part_ref[i, kind * local : (kind + 1) * local] = part[i * local : (i + 1) * local]


def weight_stage(left, mine, other, mine_scaled, other_scaled, chips, inv_model, inv_hidden):
    rows, width = mine.shape
    both = 2 * left.shape[1] // chips
    block = 896
    row_spec = pl.BlockSpec((rows, block), lambda i: (0, i))
    return pl.pallas_call(
        functools.partial(weight_kernel, inv_model, inv_hidden),
        grid=(width // block,),
        in_specs=[pl.BlockSpec(left.shape, lambda i: (0, 0, 0))] + [row_spec] * 4,
        out_specs=pl.BlockSpec((chips, both, block), lambda i: (0, 0, i)),
        out_shape=jax.ShapeDtypeStruct((chips, both, width), jnp.bfloat16),
        compiler_params=pltpu.CompilerParams(
            dimension_semantics=("arbitrary",), vmem_limit_bytes=60 * 1024 * 1024
        ),
        cost_estimate=pl.CostEstimate(flops=0, bytes_accessed=1024, transcendentals=0),
    )(left, mine, other, mine_scaled, other_scaled)


def on_device(
    tokens,
    out_grad,
    routes,
    probs,
    swap_flags,
    up_weight,
    down_weight,
    up_first,
    up_second,
    down_first,
    down_second,
):
    model_width = tokens.shape[1]
    high = lax.axis_size(HIGH)
    side = lax.axis_size(SIDE)
    experts = high * side
    ring = lax.axis_size(RING)
    near = lax.axis_size(NEAR)
    chips = ring * near
    half_axis = experts // 2
    capacity = max(2, routes.size * 5 // (4 * experts))
    side_rows = high * capacity
    high_rows = side * capacity
    buffer_rows = experts * capacity
    local_hidden = up_weight.shape[1]
    hidden_units = local_hidden * chips * lax.axis_size(CORE)
    inv_model = model_width ** (-0.5)
    inv_hidden = hidden_units ** (-0.5)
    my_high = lax.axis_index(HIGH)
    my_index = my_high * side + lax.axis_index(SIDE)
    expert_ids = jnp.arange(experts, dtype=jnp.int32)
    flag_mine = jnp.sum(jnp.where(expert_ids == my_index, swap_flags, 0))
    swapped = flag_mine == 1

    weights = jnp.concatenate((up_weight[0], down_weight[0]), axis=0)
    weights_partner = partner(weights, FAR, 1)

    send_tokens, send_scaled, token_select = dispatch(
        swap_flags, routes, probs, tokens, out_grad, capacity
    )
    buffer_ids = jnp.arange(buffer_rows, dtype=jnp.int32)
    other_order = (
        (buffer_ids // capacity % high) * side_rows
        + (buffer_ids // side_rows) * capacity
        + buffer_ids % capacity
    )
    regroup = (buffer_ids[None, :] == other_order[:, None]).astype(jnp.bfloat16)

    def along_side(rows):
        return lax.all_to_all(
            rows.reshape(side, side_rows, model_width),
            SIDE,
            split_axis=0,
            concat_axis=0,
            tiled=True,
        ).reshape(buffer_rows, model_width)

    def pick(matrix, rows):
        return jnp.dot(matrix, rows, preferred_element_type=jnp.float32).astype(jnp.bfloat16)

    ways = z_routes()

    def along_high(rows, back):
        blocks = [rows[i * high_rows : (i + 1) * high_rows] for i in range(high)]
        moved = [
            lax.ppermute(
                array, (NEAR, *HIGH), [(b, a) for a, b in way] if back else way
            )
            for array, way in zip(blocks[1:], ways)
        ]
        return jnp.concatenate(blocks[:1] + moved, axis=0), moved

    token_rows = pick(regroup, along_side(send_tokens))
    side_scaled = along_side(send_scaled)
    scaled_rows = pick(regroup, side_scaled)

    rows_mine, token_blocks = along_high(token_rows, False)

    weights = jnp.where(swapped, weights_partner, weights)
    weights, _ = lax.optimization_barrier((weights, token_rows))
    both = jnp.stack((weights, partner(weights, NEAR, 1)), axis=0)
    both, _, _ = lax.optimization_barrier((both, side_scaled, token_blocks))
    gathered = lax.all_gather(both, RING, axis=0).reshape(
        chips, 2 * local_hidden, model_width
    )

    scaled_mine, _ = along_high(scaled_rows, False)
    rows_other = partner(rows_mine, CORE, 1)
    scaled_other = partner(scaled_mine, CORE, 1)
    moments = (up_first[0], up_second[0], down_first[0], down_second[0])

    rounded = tuple(array.astype(jnp.bfloat16) for array in moments)
    up_held, _ = lax.optimization_barrier((rounded[:2], scaled_mine))
    up_arrived = tuple(partner(array, FAR, 1) for array in up_held)
    delta_mine, delta_other, left = expert_stage(
        rows_mine, rows_other, scaled_mine, scaled_other, gathered, inv_model, inv_hidden
    )
    parts = weight_stage(
        left, rows_mine, rows_other, scaled_mine, scaled_other, chips, inv_model, inv_hidden
    )
    up_arrived, delta_mine, parts = lax.optimization_barrier((up_arrived, delta_mine, parts))
    pair_mine, for_other = pair_stage(delta_mine, delta_other, gathered, inv_model)
    from_other = partner(for_other, CORE, 1)
    pair_grad = (pair_mine + from_other.astype(jnp.float32)).astype(jnp.bfloat16)
    down_held, _ = lax.optimization_barrier((rounded[2], parts))
    down_arrived = partner(down_held, FAR, 1)
    down_arrived, pair_grad = lax.optimization_barrier((down_arrived, pair_grad))
    back_rows, _ = along_high(pair_grad, True)
    late_held, back_rows = lax.optimization_barrier((rounded[3], back_rows))
    late_arrived = partner(late_held, FAR, 1)
    returned = along_side(pick(regroup, back_rows))
    token_grad = lax.dot_general(
        token_select, returned, (((0,), (0,)), ((), ())), preferred_element_type=jnp.float32
    ).astype(jnp.bfloat16)

    own, beside = lax.psum_scatter(
        parts.reshape(ring, near, 2 * local_hidden, model_width),
        RING,
        scatter_dimension=0,
        tiled=False,
    )
    late_arrived, beside = lax.optimization_barrier((late_arrived, beside))
    arrived = (*up_arrived, down_arrived, late_arrived)
    summed = own.astype(jnp.float32) + partner(beside, NEAR, 1).astype(jnp.float32)
    moments = tuple(
        jnp.where(swapped, new.astype(jnp.float32), old) for new, old in zip(arrived, moments)
    )
    new_up, up_first_new, up_second_new = adam_update(
        weights[:local_hidden], moments[0], moments[1], summed[:local_hidden]
    )
    new_down, down_first_new, down_second_new = adam_update(
        weights[local_hidden:], moments[2], moments[3], summed[local_hidden:]
    )
    return (
        token_grad,
        new_up[None],
        new_down[None],
        up_first_new[None],
        up_second_new[None],
        down_first_new[None],
        down_second_new[None],
    )


def solution(mesh):
    dp, expert = (mesh.shape[name] for name in ("dp", "expert"))
    fine = Mesh(
        mesh.devices.reshape(2, dp // 4, 2, 2, HIGHS // 2, expert // HIGHS),
        (NEAR, RING, CORE, *HIGH, SIDE),
    )
    rows = P((NEAR, RING, CORE, *HIGH, SIDE), None)
    slots = P((*HIGH, SIDE), (NEAR, RING, CORE), None)
    return jax.shard_map(
        on_device,
        mesh=fine,
        in_specs=(rows, rows, rows, rows, P()) + (slots,) * 6,
        out_specs=(rows,) + (slots,) * 6,
        check_vma=False,
    )
```

```python
import functools

import jax
import jax.numpy as jnp
from jax import lax
from jax.experimental import pallas as pl
from jax.experimental.pallas import tpu as pltpu
from jax.sharding import Mesh
from jax.sharding import PartitionSpec as P

ADAM_STEP = 20


beta_first = 0.9
beta_second = 0.95
step_size = 0.05
adam_epsilon = 1e-08

NEAR = "near"
RING = "ring"
CORE = "core"
FAR = "far"
STEP = "step"
HIGH = (FAR, STEP)
SIDE = "side"
HIGHS = 4


def partner(array, axis, flip):
    return lax.ppermute(array, axis, [(i, i ^ flip) for i in range(lax.axis_size(axis))])


def z_routes():
    routes = []
    for step, crosses in ((1, False), (-1, True), (2, True)):
        pairs = []
        for near in range(2):
            sign = 1 if near == 0 else -1
            for high in range(HIGHS):
                other = (1 - near) if crosses else near
                pairs.append((near * HIGHS + high, other * HIGHS + (high + sign * step) % HIGHS))
        routes.append(pairs)
    return routes


def adam_update(weight, first, second, gradient):
    first_new = beta_first * first + (1.0 - beta_first) * gradient
    second_new = beta_second * second + (1.0 - beta_second) * gradient * gradient
    corr_first = 1.0 - beta_first**ADAM_STEP
    corr_second = 1.0 - beta_second**ADAM_STEP
    stepped = weight.astype(jnp.float32) - step_size * (first_new / corr_first) / (
        jnp.sqrt(second_new / corr_second) + adam_epsilon
    )
    return (stepped.astype(jnp.bfloat16), first_new, second_new)


def dispatch_kernel(
    capacity,
    flags_ref,
    routes_ref,
    probs_ref,
    tokens_ref,
    out_grad_ref,
    token_rows_ref,
    scaled_rows_ref,
    select_ref,
):
    tops, count = routes_ref.shape
    experts = flags_ref.shape[0]
    rows, width = token_rows_ref.shape
    side = experts // HIGHS
    half_axis = experts // 2
    my_high = lax.axis_index(FAR) * (HIGHS // 2) + lax.axis_index(STEP)
    my_near = lax.axis_index(NEAR)
    ids = lax.broadcasted_iota(jnp.int32, (experts, 1), 0)
    slot = jnp.where(flags_ref[...] == 1, jnp.bitwise_xor(ids, half_axis), ids)
    away = lax.shift_right_logical(slot, side.bit_length() - 1) - my_high
    away = jnp.bitwise_and(jnp.where(my_near == 0, away, -away), HIGHS - 1)
    block = jnp.where(away >= 2, 5 - away, away)
    base = jnp.bitwise_and(slot, side - 1) * (HIGHS * capacity) + block * capacity
    base = base.astype(jnp.float32)
    expert_ids = lax.broadcasted_iota(jnp.int32, (experts, count), 0)
    before = (
        lax.broadcasted_iota(jnp.int32, (count, count), 0)
        < lax.broadcasted_iota(jnp.int32, (count, count), 1)
    )
    before = jnp.where(before, 1.0, 0.0).astype(jnp.bfloat16)
    row_ids = lax.broadcasted_iota(jnp.int32, (rows, count), 0)
    token_pick = jnp.zeros((rows, count), jnp.float32)
    prob_pick = jnp.zeros((rows, count), jnp.float32)
    for k in range(tops):
        onehot = jnp.where(routes_ref[k : k + 1] == expert_ids, 1.0, 0.0)
        earlier = jnp.dot(onehot.astype(jnp.bfloat16), before, preferred_element_type=jnp.float32)
        row = jnp.sum(onehot * (base + earlier), axis=0, keepdims=True).astype(jnp.int32)
        hit = row_ids == row
        token_pick = token_pick + jnp.where(hit, 1.0, 0.0)
        prob_pick = prob_pick + jnp.where(hit, probs_ref[k : k + 1].astype(jnp.float32), 0.0)
        base = base + jnp.sum(onehot, axis=1, keepdims=True)
    token_pick = token_pick.astype(jnp.bfloat16)
    prob_pick = prob_pick.astype(jnp.bfloat16)
    select_ref[...] = token_pick
    piece = 512
    for at in range(0, width, piece):
        cut = slice(at, min(at + piece, width))
        for pick, source, target in (
            (token_pick, tokens_ref, token_rows_ref),
            (prob_pick, out_grad_ref, scaled_rows_ref),
        ):
            target[:, cut] = jnp.dot(
                pick, source[:, cut], preferred_element_type=jnp.float32
            ).astype(jnp.bfloat16)


def dispatch(swap_flags, routes, probs, tokens, out_grad, capacity):
    count, width = tokens.shape
    rows = swap_flags.shape[0] * capacity
    whole = pl.BlockSpec(memory_space=pltpu.VMEM)
    return pl.pallas_call(
        functools.partial(dispatch_kernel, capacity),
        in_specs=[whole] * 5,
        out_specs=[whole] * 3,
        out_shape=[
            jax.ShapeDtypeStruct((rows, width), jnp.bfloat16),
            jax.ShapeDtypeStruct((rows, width), jnp.bfloat16),
            jax.ShapeDtypeStruct((rows, count), jnp.bfloat16),
        ],
        compiler_params=pltpu.CompilerParams(vmem_limit_bytes=24 * 1024 * 1024),
        cost_estimate=pl.CostEstimate(flops=0, bytes_accessed=1024, transcendentals=0),
    )(swap_flags.reshape(-1, 1), routes.T, probs.T, tokens, out_grad)


def expert_kernel(
    steps,
    inv_model,
    inv_hidden,
    mine_ref,
    other_ref,
    mine_scaled_ref,
    other_scaled_ref,
    weight_ref,
    pair_ref,
    pair_other_ref,
    left_ref,
    pre_ref,
    back_ref,
    delta_ref,
):
    step = pl.program_id(0)
    chips, both, _ = weight_ref.shape
    local = both // 2
    rows = mine_ref.shape[0]
    contract_last = (((1,), (1,)), ((), ()))
    up = jnp.concatenate([weight_ref[i, :local] for i in range(chips)], axis=0)

    @pl.when(step == 0)
    def _():
        pre_ref[...] = jnp.zeros_like(pre_ref)
        back_ref[...] = jnp.zeros_like(back_ref)

    @pl.when(step < steps)
    def _():
        down = jnp.concatenate([weight_ref[i, local:] for i in range(chips)], axis=0)
        token = jnp.concatenate((mine_ref[...], other_ref[...]), axis=0)
        pre_ref[...] += lax.dot_general(
            up, token, contract_last, preferred_element_type=jnp.float32
        )
        scaled = jnp.concatenate((mine_scaled_ref[...], other_scaled_ref[...]), axis=0)
        back_ref[...] += lax.dot_general(
            down, scaled, contract_last, preferred_element_type=jnp.float32
        )

    @pl.when(step == steps - 1)
    def _():
        pre_act = pre_ref[...] * inv_model
        sigmoid_act = 1.0 / (1.0 + jnp.exp(-pre_act))
        delta = (
            back_ref[...] * inv_hidden * sigmoid_act * (1.0 + pre_act * (1.0 - sigmoid_act))
        ).astype(jnp.bfloat16)
        left_ref[0] = delta
        left_ref[1] = (pre_act * sigmoid_act).astype(jnp.bfloat16)
        delta_ref[...] = delta.T

    @pl.when(step >= steps)
    def _():
        pair = jnp.dot(delta_ref[...], up, preferred_element_type=jnp.float32) * inv_model
        pair_ref[...] = pair[:rows]
        pair_other_ref[...] = pair[rows:].astype(jnp.bfloat16)


def expert_stage(mine, other, mine_scaled, other_scaled, weights, inv_model, inv_hidden):
    rows, width = mine.shape
    chips, both, _ = weights.shape
    hidden = chips * both // 2
    block = 1792
    steps = width // block

    def early(i):
        return jnp.minimum(i, steps - 1)

    def late(i):
        return jnp.maximum(i - steps, 0)

    row_spec = pl.BlockSpec((rows, block), lambda i: (0, early(i)))
    late_spec = pl.BlockSpec((rows, block), lambda i: (0, late(i)))
    return pl.pallas_call(
        functools.partial(expert_kernel, steps, inv_model, inv_hidden),
        grid=(2 * steps,),
        in_specs=[row_spec] * 4 + [pl.BlockSpec((chips, both, block), lambda i: (0, 0, i % steps))],
        out_specs=[
            late_spec,
            late_spec,
            pl.BlockSpec((2, hidden, 2 * rows), lambda i: (0, 0, 0)),
        ],
        out_shape=[
            jax.ShapeDtypeStruct((rows, width), jnp.float32),
            jax.ShapeDtypeStruct((rows, width), jnp.bfloat16),
            jax.ShapeDtypeStruct((2, hidden, 2 * rows), jnp.bfloat16),
        ],
        scratch_shapes=[
            pltpu.VMEM((hidden, 2 * rows), jnp.float32),
            pltpu.VMEM((hidden, 2 * rows), jnp.float32),
            pltpu.VMEM((2 * rows, hidden), jnp.bfloat16),
        ],
        compiler_params=pltpu.CompilerParams(
            dimension_semantics=("arbitrary",), vmem_limit_bytes=60 * 1024 * 1024
        ),
        cost_estimate=pl.CostEstimate(
            flops=12 * rows * hidden * width, bytes_accessed=32 * rows * width, transcendentals=0
        ),
    )(mine, other, mine_scaled, other_scaled, weights)


def weight_kernel(
    inv_model,
    inv_hidden,
    left_ref,
    mine_ref,
    other_ref,
    mine_scaled_ref,
    other_scaled_ref,
    part_ref,
):
    chips, both, _ = part_ref.shape
    local = both // 2
    for kind, mine, other, scale in (
        (0, mine_ref, other_ref, inv_model),
        (1, mine_scaled_ref, other_scaled_ref, inv_hidden),
    ):
        right = jnp.concatenate((mine[...], other[...]), axis=0)
        part = jnp.dot(left_ref[kind], right, preferred_element_type=jnp.float32) * scale
        part = part.astype(jnp.bfloat16)
        for i in range(chips):
            part_ref[i, kind * local : (kind + 1) * local] = part[i * local : (i + 1) * local]


def weight_stage(left, mine, other, mine_scaled, other_scaled, chips, inv_model, inv_hidden):
    rows, width = mine.shape
    both = 2 * left.shape[1] // chips
    block = 896
    row_spec = pl.BlockSpec((rows, block), lambda i: (0, i))
    return pl.pallas_call(
        functools.partial(weight_kernel, inv_model, inv_hidden),
        grid=(width // block,),
        in_specs=[pl.BlockSpec(left.shape, lambda i: (0, 0, 0))] + [row_spec] * 4,
        out_specs=pl.BlockSpec((chips, both, block), lambda i: (0, 0, i)),
        out_shape=jax.ShapeDtypeStruct((chips, both, width), jnp.bfloat16),
        compiler_params=pltpu.CompilerParams(
            dimension_semantics=("arbitrary",), vmem_limit_bytes=60 * 1024 * 1024
        ),
        cost_estimate=pl.CostEstimate(flops=0, bytes_accessed=1024, transcendentals=0),
    )(left, mine, other, mine_scaled, other_scaled)


def on_device(
    tokens,
    out_grad,
    routes,
    probs,
    swap_flags,
    up_weight,
    down_weight,
    up_first,
    up_second,
    down_first,
    down_second,
):
    model_width = tokens.shape[1]
    high = lax.axis_size(HIGH)
    side = lax.axis_size(SIDE)
    experts = high * side
    ring = lax.axis_size(RING)
    near = lax.axis_size(NEAR)
    chips = ring * near
    half_axis = experts // 2
    capacity = max(2, routes.size * 5 // (4 * experts))
    side_rows = high * capacity
    high_rows = side * capacity
    buffer_rows = experts * capacity
    local_hidden = up_weight.shape[1]
    hidden_units = local_hidden * chips * lax.axis_size(CORE)
    inv_model = model_width ** (-0.5)
    inv_hidden = hidden_units ** (-0.5)
    my_high = lax.axis_index(HIGH)
    my_index = my_high * side + lax.axis_index(SIDE)
    expert_ids = jnp.arange(experts, dtype=jnp.int32)
    flag_mine = jnp.sum(jnp.where(expert_ids == my_index, swap_flags, 0))
    swapped = flag_mine == 1

    weights = jnp.concatenate((up_weight[0], down_weight[0]), axis=0)
    weights_partner = partner(weights, FAR, 1)

    send_tokens, send_scaled, token_select = dispatch(
        swap_flags, routes, probs, tokens, out_grad, capacity
    )
    buffer_ids = jnp.arange(buffer_rows, dtype=jnp.int32)
    other_order = (
        (buffer_ids // capacity % high) * side_rows
        + (buffer_ids // side_rows) * capacity
        + buffer_ids % capacity
    )
    regroup = (buffer_ids[None, :] == other_order[:, None]).astype(jnp.bfloat16)

    def along_side(rows):
        return lax.all_to_all(
            rows.reshape(side, side_rows, model_width),
            SIDE,
            split_axis=0,
            concat_axis=0,
            tiled=True,
        ).reshape(buffer_rows, model_width)

    def pick(matrix, rows):
        return jnp.dot(matrix, rows, preferred_element_type=jnp.float32).astype(jnp.bfloat16)

    ways = z_routes()

    def along_high(rows, back):
        blocks = [rows[i * high_rows : (i + 1) * high_rows] for i in range(high)]
        moved = [
            lax.ppermute(
                array, (NEAR, *HIGH), [(b, a) for a, b in way] if back else way
            )
            for array, way in zip(blocks[1:], ways)
        ]
        return jnp.concatenate(blocks[:1] + moved, axis=0), moved[1]

    token_rows = pick(regroup, along_side(send_tokens))
    side_scaled = along_side(send_scaled)
    scaled_rows = pick(regroup, side_scaled)

    rows_mine, nearest = along_high(token_rows, False)

    weights = jnp.where(swapped, weights_partner, weights)
    weights, _ = lax.optimization_barrier((weights, token_rows))
    both = jnp.stack((weights, partner(weights, NEAR, 1)), axis=0)
    both, _, _ = lax.optimization_barrier((both, side_scaled, nearest))
    gathered = lax.all_gather(both, RING, axis=0).reshape(
        chips, 2 * local_hidden, model_width
    )

    scaled_mine, _ = along_high(scaled_rows, False)
    rows_other = partner(rows_mine, CORE, 1)
    scaled_other = partner(scaled_mine, CORE, 1)
    moments = (up_first[0], up_second[0], down_first[0], down_second[0])

    rounded = tuple(array.astype(jnp.bfloat16) for array in moments)
    up_held, _ = lax.optimization_barrier((rounded[:2], scaled_mine))
    up_arrived = tuple(partner(array, FAR, 1) for array in up_held)
    pair_mine, for_other, left = expert_stage(
        rows_mine, rows_other, scaled_mine, scaled_other, gathered, inv_model, inv_hidden
    )
    parts = weight_stage(
        left, rows_mine, rows_other, scaled_mine, scaled_other, chips, inv_model, inv_hidden
    )
    from_other = partner(for_other, CORE, 1)
    pair_grad = (pair_mine + from_other.astype(jnp.float32)).astype(jnp.bfloat16)
    up_arrived, parts = lax.optimization_barrier((up_arrived, parts))
    down_held, _ = lax.optimization_barrier((rounded[2], parts))
    down_arrived = partner(down_held, FAR, 1)
    down_arrived, pair_grad = lax.optimization_barrier((down_arrived, pair_grad))
    back_rows, _ = along_high(pair_grad, True)
    late_held, back_rows = lax.optimization_barrier((rounded[3], back_rows))
    late_arrived = partner(late_held, FAR, 1)
    returned = along_side(pick(regroup, back_rows))
    token_grad = lax.dot_general(
        token_select, returned, (((0,), (0,)), ((), ())), preferred_element_type=jnp.float32
    ).astype(jnp.bfloat16)

    own, beside = lax.psum_scatter(
        parts.reshape(ring, near, 2 * local_hidden, model_width),
        RING,
        scatter_dimension=0,
        tiled=False,
    )
    late_arrived, beside = lax.optimization_barrier((late_arrived, beside))
    arrived = (*up_arrived, down_arrived, late_arrived)
    summed = own.astype(jnp.float32) + partner(beside, NEAR, 1).astype(jnp.float32)
    moments = tuple(
        jnp.where(swapped, new.astype(jnp.float32), old) for new, old in zip(arrived, moments)
    )
    new_up, up_first_new, up_second_new = adam_update(
        weights[:local_hidden], moments[0], moments[1], summed[:local_hidden]
    )
    new_down, down_first_new, down_second_new = adam_update(
        weights[local_hidden:], moments[2], moments[3], summed[local_hidden:]
    )
    return (
        token_grad,
        new_up[None],
        new_down[None],
        up_first_new[None],
        up_second_new[None],
        down_first_new[None],
        down_second_new[None],
    )


def solution(mesh):
    dp, expert = (mesh.shape[name] for name in ("dp", "expert"))
    fine = Mesh(
        mesh.devices.reshape(2, dp // 4, 2, 2, HIGHS // 2, expert // HIGHS),
        (NEAR, RING, CORE, *HIGH, SIDE),
    )
    rows = P((NEAR, RING, CORE, *HIGH, SIDE), None)
    slots = P((*HIGH, SIDE), (NEAR, RING, CORE), None)
    return jax.shard_map(
        on_device,
        mesh=fine,
        in_specs=(rows, rows, rows, rows, P()) + (slots,) * 6,
        out_specs=(rows,) + (slots,) * 6,
        check_vma=False,
    )
```

```python
import functools

import jax
import jax.numpy as jnp
from jax import lax
from jax.experimental import pallas as pl
from jax.experimental.pallas import tpu as pltpu
from jax.sharding import Mesh
from jax.sharding import PartitionSpec as P

ADAM_STEP = 20


beta_first = 0.9
beta_second = 0.95
step_size = 0.05
adam_epsilon = 1e-08

NEAR = "near"
RING = "ring"
CORE = "core"
FAR = "far"
STEP = "step"
HIGH = (FAR, STEP)
SIDE = "side"
HIGHS = 4


def partner(array, axis, flip):
    return lax.ppermute(array, axis, [(i, i ^ flip) for i in range(lax.axis_size(axis))])


def z_routes():
    routes = []
    for step, crosses in ((1, False), (-1, True), (2, True)):
        pairs = []
        for near in range(2):
            sign = 1 if near == 0 else -1
            for high in range(HIGHS):
                other = (1 - near) if crosses else near
                pairs.append((near * HIGHS + high, other * HIGHS + (high + sign * step) % HIGHS))
        routes.append(pairs)
    return routes


def adam_update(weight, first, second, gradient):
    first_new = beta_first * first + (1.0 - beta_first) * gradient
    second_new = beta_second * second + (1.0 - beta_second) * gradient * gradient
    corr_first = 1.0 - beta_first**ADAM_STEP
    corr_second = 1.0 - beta_second**ADAM_STEP
    stepped = weight.astype(jnp.float32) - step_size * (first_new / corr_first) / (
        jnp.sqrt(second_new / corr_second) + adam_epsilon
    )
    return (stepped.astype(jnp.bfloat16), first_new, second_new)


def dispatch_kernel(
    capacity,
    experts,
    routes_ref,
    probs_ref,
    tokens_ref,
    out_grad_ref,
    token_rows_ref,
    scaled_rows_ref,
    select_ref,
):
    tops, count = routes_ref.shape
    rows, width = token_rows_ref.shape
    side = experts // HIGHS
    my_high = lax.axis_index(FAR) * (HIGHS // 2) + lax.axis_index(STEP)
    my_near = lax.axis_index(NEAR)
    ids = lax.broadcasted_iota(jnp.int32, (experts, 1), 0)
    away = lax.shift_right_logical(ids, side.bit_length() - 1) - my_high
    away = jnp.bitwise_and(jnp.where(my_near == 0, away, -away), HIGHS - 1)
    block = jnp.where(away >= 2, 5 - away, away)
    base = jnp.bitwise_and(ids, side - 1) * (HIGHS * capacity) + block * capacity
    base = base.astype(jnp.float32)
    expert_ids = lax.broadcasted_iota(jnp.int32, (experts, count), 0)
    before = (
        lax.broadcasted_iota(jnp.int32, (count, count), 0)
        < lax.broadcasted_iota(jnp.int32, (count, count), 1)
    )
    before = jnp.where(before, 1.0, 0.0).astype(jnp.bfloat16)
    row_ids = lax.broadcasted_iota(jnp.int32, (rows, count), 0)
    token_pick = jnp.zeros((rows, count), jnp.float32)
    prob_pick = jnp.zeros((rows, count), jnp.float32)
    for k in range(tops):
        onehot = jnp.where(routes_ref[k : k + 1] == expert_ids, 1.0, 0.0)
        earlier = jnp.dot(onehot.astype(jnp.bfloat16), before, preferred_element_type=jnp.float32)
        row = jnp.sum(onehot * (base + earlier), axis=0, keepdims=True).astype(jnp.int32)
        hit = row_ids == row
        token_pick = token_pick + jnp.where(hit, 1.0, 0.0)
        prob_pick = prob_pick + jnp.where(hit, probs_ref[k : k + 1].astype(jnp.float32), 0.0)
        base = base + jnp.sum(onehot, axis=1, keepdims=True)
    token_pick = token_pick.astype(jnp.bfloat16)
    prob_pick = prob_pick.astype(jnp.bfloat16)
    select_ref[...] = token_pick
    piece = 512
    for at in range(0, width, piece):
        cut = slice(at, min(at + piece, width))
        for pick, source, target in (
            (token_pick, tokens_ref, token_rows_ref),
            (prob_pick, out_grad_ref, scaled_rows_ref),
        ):
            target[:, cut] = jnp.dot(
                pick, source[:, cut], preferred_element_type=jnp.float32
            ).astype(jnp.bfloat16)


def dispatch(experts, routes, probs, tokens, out_grad, capacity):
    count, width = tokens.shape
    rows = experts * capacity
    whole = pl.BlockSpec(memory_space=pltpu.VMEM)
    return pl.pallas_call(
        functools.partial(dispatch_kernel, capacity, experts),
        in_specs=[whole] * 4,
        out_specs=[whole] * 3,
        out_shape=[
            jax.ShapeDtypeStruct((rows, width), jnp.bfloat16),
            jax.ShapeDtypeStruct((rows, width), jnp.bfloat16),
            jax.ShapeDtypeStruct((rows, count), jnp.bfloat16),
        ],
        compiler_params=pltpu.CompilerParams(vmem_limit_bytes=24 * 1024 * 1024),
        cost_estimate=pl.CostEstimate(flops=0, bytes_accessed=1024, transcendentals=0),
    )(routes.T, probs.T, tokens, out_grad)


def expert_kernel(
    steps,
    inv_model,
    inv_hidden,
    mine_ref,
    other_ref,
    mine_scaled_ref,
    other_scaled_ref,
    weight_ref,
    pair_ref,
    pair_other_ref,
    left_ref,
    pre_ref,
    back_ref,
    delta_ref,
):
    step = pl.program_id(0)
    chips, both, _ = weight_ref.shape
    local = both // 2
    rows = mine_ref.shape[0]
    contract_last = (((1,), (1,)), ((), ()))
    up = jnp.concatenate([weight_ref[i, :local] for i in range(chips)], axis=0)

    @pl.when(step == 0)
    def _():
        pre_ref[...] = jnp.zeros_like(pre_ref)
        back_ref[...] = jnp.zeros_like(back_ref)

    @pl.when(step < steps)
    def _():
        down = jnp.concatenate([weight_ref[i, local:] for i in range(chips)], axis=0)
        token = jnp.concatenate((mine_ref[...], other_ref[...]), axis=0)
        pre_ref[...] += lax.dot_general(
            up, token, contract_last, preferred_element_type=jnp.float32
        )
        scaled = jnp.concatenate((mine_scaled_ref[...], other_scaled_ref[...]), axis=0)
        back_ref[...] += lax.dot_general(
            down, scaled, contract_last, preferred_element_type=jnp.float32
        )

    @pl.when(step == steps - 1)
    def _():
        pre_act = pre_ref[...] * inv_model
        sigmoid_act = 1.0 / (1.0 + jnp.exp(-pre_act))
        delta = (
            back_ref[...] * inv_hidden * sigmoid_act * (1.0 + pre_act * (1.0 - sigmoid_act))
        ).astype(jnp.bfloat16)
        left_ref[0] = delta
        left_ref[1] = (pre_act * sigmoid_act).astype(jnp.bfloat16)
        delta_ref[...] = delta.T

    @pl.when(step >= steps)
    def _():
        pair = jnp.dot(delta_ref[...], up, preferred_element_type=jnp.float32) * inv_model
        pair_ref[...] = pair[:rows]
        pair_other_ref[...] = pair[rows:].astype(jnp.bfloat16)


def expert_stage(mine, other, mine_scaled, other_scaled, weights, inv_model, inv_hidden):
    rows, width = mine.shape
    chips, both, _ = weights.shape
    hidden = chips * both // 2
    block = 1792
    steps = width // block

    def early(i):
        return jnp.minimum(i, steps - 1)

    def late(i):
        return jnp.maximum(i - steps, 0)

    row_spec = pl.BlockSpec((rows, block), lambda i: (0, early(i)))
    late_spec = pl.BlockSpec((rows, block), lambda i: (0, late(i)))
    return pl.pallas_call(
        functools.partial(expert_kernel, steps, inv_model, inv_hidden),
        grid=(2 * steps,),
        in_specs=[row_spec] * 4 + [pl.BlockSpec((chips, both, block), lambda i: (0, 0, i % steps))],
        out_specs=[
            late_spec,
            late_spec,
            pl.BlockSpec((2, hidden, 2 * rows), lambda i: (0, 0, 0)),
        ],
        out_shape=[
            jax.ShapeDtypeStruct((rows, width), jnp.float32),
            jax.ShapeDtypeStruct((rows, width), jnp.bfloat16),
            jax.ShapeDtypeStruct((2, hidden, 2 * rows), jnp.bfloat16),
        ],
        scratch_shapes=[
            pltpu.VMEM((hidden, 2 * rows), jnp.float32),
            pltpu.VMEM((hidden, 2 * rows), jnp.float32),
            pltpu.VMEM((2 * rows, hidden), jnp.bfloat16),
        ],
        compiler_params=pltpu.CompilerParams(
            dimension_semantics=("arbitrary",), vmem_limit_bytes=60 * 1024 * 1024
        ),
        cost_estimate=pl.CostEstimate(
            flops=12 * rows * hidden * width, bytes_accessed=32 * rows * width, transcendentals=0
        ),
    )(mine, other, mine_scaled, other_scaled, weights)


def weight_kernel(
    inv_model,
    inv_hidden,
    left_ref,
    mine_ref,
    other_ref,
    mine_scaled_ref,
    other_scaled_ref,
    part_ref,
):
    chips, both, _ = part_ref.shape
    local = both // 2
    for kind, mine, other, scale in (
        (0, mine_ref, other_ref, inv_model),
        (1, mine_scaled_ref, other_scaled_ref, inv_hidden),
    ):
        right = jnp.concatenate((mine[...], other[...]), axis=0)
        part = jnp.dot(left_ref[kind], right, preferred_element_type=jnp.float32) * scale
        part = part.astype(jnp.bfloat16)
        for i in range(chips):
            part_ref[i, kind * local : (kind + 1) * local] = part[i * local : (i + 1) * local]


def weight_stage(left, mine, other, mine_scaled, other_scaled, chips, inv_model, inv_hidden):
    rows, width = mine.shape
    both = 2 * left.shape[1] // chips
    block = 896
    row_spec = pl.BlockSpec((rows, block), lambda i: (0, i))
    return pl.pallas_call(
        functools.partial(weight_kernel, inv_model, inv_hidden),
        grid=(width // block,),
        in_specs=[pl.BlockSpec(left.shape, lambda i: (0, 0, 0))] + [row_spec] * 4,
        out_specs=pl.BlockSpec((chips, both, block), lambda i: (0, 0, i)),
        out_shape=jax.ShapeDtypeStruct((chips, both, width), jnp.bfloat16),
        compiler_params=pltpu.CompilerParams(
            dimension_semantics=("arbitrary",), vmem_limit_bytes=60 * 1024 * 1024
        ),
        cost_estimate=pl.CostEstimate(flops=0, bytes_accessed=1024, transcendentals=0),
    )(left, mine, other, mine_scaled, other_scaled)


def on_device(
    tokens,
    out_grad,
    routes,
    probs,
    swap_flags,
    up_weight,
    down_weight,
    up_first,
    up_second,
    down_first,
    down_second,
):
    model_width = tokens.shape[1]
    high = lax.axis_size(HIGH)
    side = lax.axis_size(SIDE)
    experts = high * side
    ring = lax.axis_size(RING)
    near = lax.axis_size(NEAR)
    chips = ring * near
    capacity = max(2, routes.size * 5 // (4 * experts))
    side_rows = high * capacity
    high_rows = side * capacity
    buffer_rows = experts * capacity
    local_hidden = up_weight.shape[1]
    hidden_units = local_hidden * chips * lax.axis_size(CORE)
    inv_model = model_width ** (-0.5)
    inv_hidden = hidden_units ** (-0.5)
    my_high = lax.axis_index(HIGH)
    my_index = my_high * side + lax.axis_index(SIDE)
    expert_ids = jnp.arange(experts, dtype=jnp.int32)
    flag_mine = jnp.sum(jnp.where(expert_ids == my_index, swap_flags, 0))
    swapped = flag_mine == 1

    weights = jnp.concatenate((up_weight[0], down_weight[0]), axis=0)
    moments = (up_first[0], up_second[0], down_first[0], down_second[0])
    rounded = tuple(array.astype(jnp.bfloat16) for array in moments)
    first_arrived = partner(rounded[0], FAR, 1)

    send_tokens, send_scaled, token_select = dispatch(
        experts, routes, probs, tokens, out_grad, capacity
    )
    buffer_ids = jnp.arange(buffer_rows, dtype=jnp.int32)
    other_order = (
        (buffer_ids // capacity % high) * side_rows
        + (buffer_ids // side_rows) * capacity
        + buffer_ids % capacity
    )
    regroup = (buffer_ids[None, :] == other_order[:, None]).astype(jnp.bfloat16)

    def along_side(rows):
        return lax.all_to_all(
            rows.reshape(side, side_rows, model_width),
            SIDE,
            split_axis=0,
            concat_axis=0,
            tiled=True,
        ).reshape(buffer_rows, model_width)

    def pick(matrix, rows):
        return jnp.dot(matrix, rows, preferred_element_type=jnp.float32).astype(jnp.bfloat16)

    ways = z_routes()

    def along_high(rows, back):
        blocks = [rows[i * high_rows : (i + 1) * high_rows] for i in range(high)]
        moved = [
            lax.ppermute(
                array, (NEAR, *HIGH), [(b, a) for a, b in way] if back else way
            )
            for array, way in zip(blocks[1:], ways)
        ]
        return jnp.concatenate(blocks[:1] + moved, axis=0)

    side_tokens = along_side(send_tokens)
    token_rows = pick(regroup, side_tokens)
    side_scaled = along_side(send_scaled)
    scaled_rows = pick(regroup, side_scaled)

    rows_mine = along_high(token_rows, False)

    both = jnp.stack((weights, partner(weights, NEAR, 1)), axis=0)
    first_arrived, both, _ = lax.optimization_barrier((first_arrived, both, side_tokens))
    gathered = lax.all_gather(both, RING, axis=0).reshape(
        chips, 2 * local_hidden, model_width
    )

    scaled_mine = along_high(scaled_rows, False)
    rows_other = partner(rows_mine, CORE, 1)
    scaled_other = partner(scaled_mine, CORE, 1)
    down_held, _ = lax.optimization_barrier((rounded[2:], scaled_mine))
    down_arrived = tuple(partner(array, FAR, 1) for array in down_held)
    pair_mine, for_other, left = expert_stage(
        rows_mine, rows_other, scaled_mine, scaled_other, gathered, inv_model, inv_hidden
    )
    parts = weight_stage(
        left, rows_mine, rows_other, scaled_mine, scaled_other, chips, inv_model, inv_hidden
    )
    from_other = partner(for_other, CORE, 1)
    pair_grad = (pair_mine + from_other.astype(jnp.float32)).astype(jnp.bfloat16)
    down_arrived, parts = lax.optimization_barrier((down_arrived, parts))
    held, _ = lax.optimization_barrier(((rounded[1], weights), parts))
    second_arrived, weights_arrived = (partner(array, FAR, 1) for array in held)
    second_arrived, weights_arrived, pair_grad = lax.optimization_barrier(
        (second_arrived, weights_arrived, pair_grad)
    )
    back_rows = along_high(pair_grad, True)
    returned = along_side(pick(regroup, back_rows))
    token_grad = lax.dot_general(
        token_select, returned, (((0,), (0,)), ((), ())), preferred_element_type=jnp.float32
    ).astype(jnp.bfloat16)

    own, beside = lax.psum_scatter(
        parts.reshape(ring, near, 2 * local_hidden, model_width),
        RING,
        scatter_dimension=0,
        tiled=False,
    )
    arrived = (first_arrived, second_arrived, *down_arrived)
    summed = own.astype(jnp.float32) + partner(beside, NEAR, 1).astype(jnp.float32)
    summed_partner = partner(summed.astype(jnp.bfloat16), FAR, 1)
    summed = jnp.where(swapped, summed_partner.astype(jnp.float32), summed)
    weights = jnp.where(swapped, weights_arrived, weights)
    moments = tuple(
        jnp.where(swapped, new.astype(jnp.float32), old) for new, old in zip(arrived, moments)
    )
    new_up, up_first_new, up_second_new = adam_update(
        weights[:local_hidden], moments[0], moments[1], summed[:local_hidden]
    )
    new_down, down_first_new, down_second_new = adam_update(
        weights[local_hidden:], moments[2], moments[3], summed[local_hidden:]
    )
    return (
        token_grad,
        new_up[None],
        new_down[None],
        up_first_new[None],
        up_second_new[None],
        down_first_new[None],
        down_second_new[None],
    )


def solution(mesh):
    dp, expert = (mesh.shape[name] for name in ("dp", "expert"))
    fine = Mesh(
        mesh.devices.reshape(2, dp // 4, 2, 2, HIGHS // 2, expert // HIGHS),
        (NEAR, RING, CORE, *HIGH, SIDE),
    )
    rows = P((NEAR, RING, CORE, *HIGH, SIDE), None)
    slots = P((*HIGH, SIDE), (NEAR, RING, CORE), None)
    return jax.shard_map(
        on_device,
        mesh=fine,
        in_specs=(rows, rows, rows, rows, P()) + (slots,) * 6,
        out_specs=(rows,) + (slots,) * 6,
        check_vma=False,
    )
```

```python
import functools

import jax
import jax.numpy as jnp
from jax import lax
from jax.experimental import pallas as pl
from jax.experimental.pallas import tpu as pltpu
from jax.sharding import Mesh
from jax.sharding import PartitionSpec as P

ADAM_STEP = 20


beta_first = 0.9
beta_second = 0.95
step_size = 0.05
adam_epsilon = 1e-08

NEAR = "near"
RING = "ring"
CORE = "core"
FAR = "far"
STEP = "step"
HIGH = (FAR, STEP)
SIDE = "side"
HIGHS = 4


def partner(array, axis, flip):
    return lax.ppermute(array, axis, [(i, i ^ flip) for i in range(lax.axis_size(axis))])


def z_routes():
    routes = []
    for step, crosses in ((1, False), (-1, True), (2, True)):
        pairs = []
        for near in range(2):
            sign = 1 if near == 0 else -1
            for high in range(HIGHS):
                other = (1 - near) if crosses else near
                pairs.append((near * HIGHS + high, other * HIGHS + (high + sign * step) % HIGHS))
        routes.append(pairs)
    return routes


def adam_update(weight, first, second, gradient):
    first_new = beta_first * first + (1.0 - beta_first) * gradient
    second_new = beta_second * second + (1.0 - beta_second) * gradient * gradient
    corr_first = 1.0 - beta_first**ADAM_STEP
    corr_second = 1.0 - beta_second**ADAM_STEP
    stepped = weight.astype(jnp.float32) - step_size * (first_new / corr_first) / (
        jnp.sqrt(second_new / corr_second) + adam_epsilon
    )
    return (stepped.astype(jnp.bfloat16), first_new, second_new)


def dispatch_kernel(
    capacity,
    flags_ref,
    routes_ref,
    probs_ref,
    tokens_ref,
    out_grad_ref,
    token_rows_ref,
    scaled_rows_ref,
    select_ref,
):
    tops, count = routes_ref.shape
    experts = flags_ref.shape[0]
    rows, width = token_rows_ref.shape
    side = experts // HIGHS
    half_axis = experts // 2
    my_high = lax.axis_index(FAR) * (HIGHS // 2) + lax.axis_index(STEP)
    my_near = lax.axis_index(NEAR)
    ids = lax.broadcasted_iota(jnp.int32, (experts, 1), 0)
    slot = jnp.where(flags_ref[...] == 1, jnp.bitwise_xor(ids, half_axis), ids)
    away = lax.shift_right_logical(slot, side.bit_length() - 1) - my_high
    away = jnp.bitwise_and(jnp.where(my_near == 0, away, -away), HIGHS - 1)
    block = jnp.where(away >= 2, 5 - away, away)
    base = jnp.bitwise_and(slot, side - 1) * (HIGHS * capacity) + block * capacity
    base = base.astype(jnp.float32)
    expert_ids = lax.broadcasted_iota(jnp.int32, (experts, count), 0)
    before = (
        lax.broadcasted_iota(jnp.int32, (count, count), 0)
        < lax.broadcasted_iota(jnp.int32, (count, count), 1)
    )
    before = jnp.where(before, 1.0, 0.0).astype(jnp.bfloat16)
    row_ids = lax.broadcasted_iota(jnp.int32, (rows, count), 0)
    token_pick = jnp.zeros((rows, count), jnp.float32)
    prob_pick = jnp.zeros((rows, count), jnp.float32)
    for k in range(tops):
        onehot = jnp.where(routes_ref[k : k + 1] == expert_ids, 1.0, 0.0)
        earlier = jnp.dot(onehot.astype(jnp.bfloat16), before, preferred_element_type=jnp.float32)
        row = jnp.sum(onehot * (base + earlier), axis=0, keepdims=True).astype(jnp.int32)
        hit = row_ids == row
        token_pick = token_pick + jnp.where(hit, 1.0, 0.0)
        prob_pick = prob_pick + jnp.where(hit, probs_ref[k : k + 1].astype(jnp.float32), 0.0)
        base = base + jnp.sum(onehot, axis=1, keepdims=True)
    token_pick = token_pick.astype(jnp.bfloat16)
    prob_pick = prob_pick.astype(jnp.bfloat16)
    select_ref[...] = token_pick
    piece = 512
    for at in range(0, width, piece):
        cut = slice(at, min(at + piece, width))
        for pick, source, target in (
            (token_pick, tokens_ref, token_rows_ref),
            (prob_pick, out_grad_ref, scaled_rows_ref),
        ):
            target[:, cut] = jnp.dot(
                pick, source[:, cut], preferred_element_type=jnp.float32
            ).astype(jnp.bfloat16)


def dispatch(swap_flags, routes, probs, tokens, out_grad, capacity):
    count, width = tokens.shape
    rows = swap_flags.shape[0] * capacity
    whole = pl.BlockSpec(memory_space=pltpu.VMEM)
    return pl.pallas_call(
        functools.partial(dispatch_kernel, capacity),
        in_specs=[whole] * 5,
        out_specs=[whole] * 3,
        out_shape=[
            jax.ShapeDtypeStruct((rows, width), jnp.bfloat16),
            jax.ShapeDtypeStruct((rows, width), jnp.bfloat16),
            jax.ShapeDtypeStruct((rows, count), jnp.bfloat16),
        ],
        compiler_params=pltpu.CompilerParams(vmem_limit_bytes=24 * 1024 * 1024),
        cost_estimate=pl.CostEstimate(flops=0, bytes_accessed=1024, transcendentals=0),
    )(swap_flags.reshape(-1, 1), routes.T, probs.T, tokens, out_grad)


def expert_kernel(
    steps,
    inv_model,
    inv_hidden,
    mine_ref,
    other_ref,
    mine_scaled_ref,
    other_scaled_ref,
    weight_ref,
    pair_ref,
    pair_other_ref,
    left_ref,
    pre_ref,
    back_ref,
    delta_ref,
):
    step = pl.program_id(0)
    chips, both, _ = weight_ref.shape
    local = both // 2
    rows = mine_ref.shape[0]
    contract_last = (((1,), (1,)), ((), ()))
    up = jnp.concatenate([weight_ref[i, :local] for i in range(chips)], axis=0)

    @pl.when(step == 0)
    def _():
        pre_ref[...] = jnp.zeros_like(pre_ref)
        back_ref[...] = jnp.zeros_like(back_ref)

    @pl.when(step < steps)
    def _():
        down = jnp.concatenate([weight_ref[i, local:] for i in range(chips)], axis=0)
        token = jnp.concatenate((mine_ref[...], other_ref[...]), axis=0)
        pre_ref[...] += lax.dot_general(
            up, token, contract_last, preferred_element_type=jnp.float32
        )
        scaled = jnp.concatenate((mine_scaled_ref[...], other_scaled_ref[...]), axis=0)
        back_ref[...] += lax.dot_general(
            down, scaled, contract_last, preferred_element_type=jnp.float32
        )

    @pl.when(step == steps - 1)
    def _():
        pre_act = pre_ref[...] * inv_model
        sigmoid_act = 1.0 / (1.0 + jnp.exp(-pre_act))
        delta = (
            back_ref[...] * inv_hidden * sigmoid_act * (1.0 + pre_act * (1.0 - sigmoid_act))
        ).astype(jnp.bfloat16)
        left_ref[0] = delta
        left_ref[1] = (pre_act * sigmoid_act).astype(jnp.bfloat16)
        delta_ref[...] = delta.T

    @pl.when(step >= steps)
    def _():
        pair = jnp.dot(delta_ref[...], up, preferred_element_type=jnp.float32) * inv_model
        pair_ref[...] = pair[:rows]
        pair_other_ref[...] = pair[rows:].astype(jnp.bfloat16)


def expert_stage(mine, other, mine_scaled, other_scaled, weights, inv_model, inv_hidden):
    rows, width = mine.shape
    chips, both, _ = weights.shape
    hidden = chips * both // 2
    block = 1792
    steps = width // block

    def early(i):
        return jnp.minimum(i, steps - 1)

    def late(i):
        return jnp.maximum(i - steps, 0)

    row_spec = pl.BlockSpec((rows, block), lambda i: (0, early(i)))
    late_spec = pl.BlockSpec((rows, block), lambda i: (0, late(i)))
    return pl.pallas_call(
        functools.partial(expert_kernel, steps, inv_model, inv_hidden),
        grid=(2 * steps,),
        in_specs=[row_spec] * 4 + [pl.BlockSpec((chips, both, block), lambda i: (0, 0, i % steps))],
        out_specs=[
            late_spec,
            late_spec,
            pl.BlockSpec((2, hidden, 2 * rows), lambda i: (0, 0, 0)),
        ],
        out_shape=[
            jax.ShapeDtypeStruct((rows, width), jnp.float32),
            jax.ShapeDtypeStruct((rows, width), jnp.bfloat16),
            jax.ShapeDtypeStruct((2, hidden, 2 * rows), jnp.bfloat16),
        ],
        scratch_shapes=[
            pltpu.VMEM((hidden, 2 * rows), jnp.float32),
            pltpu.VMEM((hidden, 2 * rows), jnp.float32),
            pltpu.VMEM((2 * rows, hidden), jnp.bfloat16),
        ],
        compiler_params=pltpu.CompilerParams(
            dimension_semantics=("arbitrary",), vmem_limit_bytes=60 * 1024 * 1024
        ),
        cost_estimate=pl.CostEstimate(
            flops=12 * rows * hidden * width, bytes_accessed=32 * rows * width, transcendentals=0
        ),
    )(mine, other, mine_scaled, other_scaled, weights)


def weight_kernel(
    inv_model,
    inv_hidden,
    left_ref,
    mine_ref,
    other_ref,
    mine_scaled_ref,
    other_scaled_ref,
    part_ref,
):
    chips, both, _ = part_ref.shape
    local = both // 2
    for kind, mine, other, scale in (
        (0, mine_ref, other_ref, inv_model),
        (1, mine_scaled_ref, other_scaled_ref, inv_hidden),
    ):
        right = jnp.concatenate((mine[...], other[...]), axis=0)
        part = jnp.dot(left_ref[kind], right, preferred_element_type=jnp.float32) * scale
        part = part.astype(jnp.bfloat16)
        for i in range(chips):
            part_ref[i, kind * local : (kind + 1) * local] = part[i * local : (i + 1) * local]


def weight_stage(left, mine, other, mine_scaled, other_scaled, chips, inv_model, inv_hidden):
    rows, width = mine.shape
    both = 2 * left.shape[1] // chips
    block = 896
    row_spec = pl.BlockSpec((rows, block), lambda i: (0, i))
    return pl.pallas_call(
        functools.partial(weight_kernel, inv_model, inv_hidden),
        grid=(width // block,),
        in_specs=[pl.BlockSpec(left.shape, lambda i: (0, 0, 0))] + [row_spec] * 4,
        out_specs=pl.BlockSpec((chips, both, block), lambda i: (0, 0, i)),
        out_shape=jax.ShapeDtypeStruct((chips, both, width), jnp.bfloat16),
        compiler_params=pltpu.CompilerParams(
            dimension_semantics=("arbitrary",), vmem_limit_bytes=60 * 1024 * 1024
        ),
        cost_estimate=pl.CostEstimate(flops=0, bytes_accessed=1024, transcendentals=0),
    )(left, mine, other, mine_scaled, other_scaled)


def on_device(
    tokens,
    out_grad,
    routes,
    probs,
    swap_flags,
    up_weight,
    down_weight,
    up_first,
    up_second,
    down_first,
    down_second,
):
    model_width = tokens.shape[1]
    high = lax.axis_size(HIGH)
    side = lax.axis_size(SIDE)
    experts = high * side
    ring = lax.axis_size(RING)
    near = lax.axis_size(NEAR)
    chips = ring * near
    half_axis = experts // 2
    capacity = max(2, routes.size * 5 // (4 * experts))
    side_rows = high * capacity
    high_rows = side * capacity
    buffer_rows = experts * capacity
    local_hidden = up_weight.shape[1]
    hidden_units = local_hidden * chips * lax.axis_size(CORE)
    inv_model = model_width ** (-0.5)
    inv_hidden = hidden_units ** (-0.5)
    my_high = lax.axis_index(HIGH)
    my_index = my_high * side + lax.axis_index(SIDE)
    expert_ids = jnp.arange(experts, dtype=jnp.int32)
    flag_mine = jnp.sum(jnp.where(expert_ids == my_index, swap_flags, 0))
    swapped = flag_mine == 1

    weights = jnp.concatenate((up_weight[0], down_weight[0]), axis=0)
    weights_partner = partner(weights, FAR, 1)

    send_tokens, send_scaled, token_select = dispatch(
        swap_flags, routes, probs, tokens, out_grad, capacity
    )
    buffer_ids = jnp.arange(buffer_rows, dtype=jnp.int32)
    other_order = (
        (buffer_ids // capacity % high) * side_rows
        + (buffer_ids // side_rows) * capacity
        + buffer_ids % capacity
    )
    regroup = (buffer_ids[None, :] == other_order[:, None]).astype(jnp.bfloat16)

    def along_side(rows):
        return lax.all_to_all(
            rows.reshape(side, side_rows, model_width),
            SIDE,
            split_axis=0,
            concat_axis=0,
            tiled=True,
        ).reshape(buffer_rows, model_width)

    def pick(matrix, rows):
        return jnp.dot(matrix, rows, preferred_element_type=jnp.float32).astype(jnp.bfloat16)

    ways = z_routes()

    def along_high(rows, back):
        blocks = [rows[i * high_rows : (i + 1) * high_rows] for i in range(high)]
        moved = [
            lax.ppermute(
                array, (NEAR, *HIGH), [(b, a) for a, b in way] if back else way
            )
            for array, way in zip(blocks[1:], ways)
        ]
        return jnp.concatenate(blocks[:1] + moved, axis=0), moved[1]

    token_rows = pick(regroup, along_side(send_tokens))
    side_scaled = along_side(send_scaled)
    scaled_rows = pick(regroup, side_scaled)

    rows_mine, nearest = along_high(token_rows, False)

    weights = jnp.where(swapped, weights_partner, weights)
    weights, _ = lax.optimization_barrier((weights, token_rows))
    both = jnp.stack((weights, partner(weights, NEAR, 1)), axis=0)
    both, _, _ = lax.optimization_barrier((both, side_scaled, nearest))
    gathered = lax.all_gather(both, RING, axis=0).reshape(
        chips, 2 * local_hidden, model_width
    )

    scaled_mine, _ = along_high(scaled_rows, False)
    rows_other = partner(rows_mine, CORE, 1)
    scaled_other = partner(scaled_mine, CORE, 1)
    moments = (up_first[0], up_second[0], down_first[0], down_second[0])

    rounded = tuple(array.astype(jnp.bfloat16) for array in moments)
    up_held, _ = lax.optimization_barrier((rounded[:2], scaled_mine))
    up_arrived = tuple(partner(array, FAR, 1) for array in up_held)
    pair_mine, for_other, left = expert_stage(
        rows_mine, rows_other, scaled_mine, scaled_other, gathered, inv_model, inv_hidden
    )
    parts = weight_stage(
        left, rows_mine, rows_other, scaled_mine, scaled_other, chips, inv_model, inv_hidden
    )
    from_other = partner(for_other, CORE, 1)
    pair_grad = (pair_mine + from_other.astype(jnp.float32)).astype(jnp.bfloat16)
    up_arrived, parts = lax.optimization_barrier((up_arrived, parts))
    down_held, _ = lax.optimization_barrier((rounded[2], parts))
    down_arrived = partner(down_held, FAR, 1)
    down_arrived, pair_grad = lax.optimization_barrier((down_arrived, pair_grad))
    back_rows, _ = along_high(pair_grad, True)
    late_held, back_rows = lax.optimization_barrier((rounded[3], back_rows))
    late_arrived = partner(late_held, FAR, 1)
    returned = along_side(pick(regroup, back_rows))
    late_arrived, returned = lax.optimization_barrier((late_arrived, returned))
    token_grad = lax.dot_general(
        token_select, returned, (((0,), (0,)), ((), ())), preferred_element_type=jnp.float32
    ).astype(jnp.bfloat16)

    own, beside = lax.psum_scatter(
        parts.reshape(ring, near, 2 * local_hidden, model_width),
        RING,
        scatter_dimension=0,
        tiled=False,
    )
    arrived = (*up_arrived, down_arrived, late_arrived)
    summed = own.astype(jnp.float32) + partner(beside, NEAR, 1).astype(jnp.float32)
    moments = tuple(
        jnp.where(swapped, new.astype(jnp.float32), old) for new, old in zip(arrived, moments)
    )
    new_up, up_first_new, up_second_new = adam_update(
        weights[:local_hidden], moments[0], moments[1], summed[:local_hidden]
    )
    new_down, down_first_new, down_second_new = adam_update(
        weights[local_hidden:], moments[2], moments[3], summed[local_hidden:]
    )
    return (
        token_grad,
        new_up[None],
        new_down[None],
        up_first_new[None],
        up_second_new[None],
        down_first_new[None],
        down_second_new[None],
    )


def solution(mesh):
    dp, expert = (mesh.shape[name] for name in ("dp", "expert"))
    fine = Mesh(
        mesh.devices.reshape(2, dp // 4, 2, 2, HIGHS // 2, expert // HIGHS),
        (NEAR, RING, CORE, *HIGH, SIDE),
    )
    rows = P((NEAR, RING, CORE, *HIGH, SIDE), None)
    slots = P((*HIGH, SIDE), (NEAR, RING, CORE), None)
    return jax.shard_map(
        on_device,
        mesh=fine,
        in_specs=(rows, rows, rows, rows, P()) + (slots,) * 6,
        out_specs=(rows,) + (slots,) * 6,
        check_vma=False,
    )
```

```python
import functools

import jax
import jax.numpy as jnp
from jax import lax
from jax.experimental import pallas as pl
from jax.experimental.pallas import tpu as pltpu
from jax.sharding import Mesh
from jax.sharding import PartitionSpec as P

ADAM_STEP = 20


beta_first = 0.9
beta_second = 0.95
step_size = 0.05
adam_epsilon = 1e-08

NEAR = "near"
RING = "ring"
CORE = "core"
FAR = "far"
STEP = "step"
HIGH = (FAR, STEP)
SIDE = "side"
HIGHS = 4


def partner(array, axis, flip):
    return lax.ppermute(array, axis, [(i, i ^ flip) for i in range(lax.axis_size(axis))])


def z_routes():
    routes = []
    for step, crosses in ((1, False), (-1, True), (2, True)):
        pairs = []
        for near in range(2):
            sign = 1 if near == 0 else -1
            for high in range(HIGHS):
                other = (1 - near) if crosses else near
                pairs.append((near * HIGHS + high, other * HIGHS + (high + sign * step) % HIGHS))
        routes.append(pairs)
    return routes


def adam_update(weight, first, second, gradient):
    first_new = beta_first * first + (1.0 - beta_first) * gradient
    second_new = beta_second * second + (1.0 - beta_second) * gradient * gradient
    corr_first = 1.0 - beta_first**ADAM_STEP
    corr_second = 1.0 - beta_second**ADAM_STEP
    stepped = weight.astype(jnp.float32) - step_size * (first_new / corr_first) / (
        jnp.sqrt(second_new / corr_second) + adam_epsilon
    )
    return (stepped.astype(jnp.bfloat16), first_new, second_new)


def dispatch_kernel(
    capacity,
    flags_ref,
    routes_ref,
    probs_ref,
    tokens_ref,
    out_grad_ref,
    token_rows_ref,
    scaled_rows_ref,
    select_ref,
):
    tops, count = routes_ref.shape
    experts = flags_ref.shape[0]
    rows, width = token_rows_ref.shape
    side = experts // HIGHS
    half_axis = experts // 2
    my_high = lax.axis_index(FAR) * (HIGHS // 2) + lax.axis_index(STEP)
    my_near = lax.axis_index(NEAR)
    ids = lax.broadcasted_iota(jnp.int32, (experts, 1), 0)
    slot = jnp.where(flags_ref[...] == 1, jnp.bitwise_xor(ids, half_axis), ids)
    away = lax.shift_right_logical(slot, side.bit_length() - 1) - my_high
    away = jnp.bitwise_and(jnp.where(my_near == 0, away, -away), HIGHS - 1)
    block = jnp.where(away >= 2, 5 - away, away)
    base = jnp.bitwise_and(slot, side - 1) * (HIGHS * capacity) + block * capacity
    base = base.astype(jnp.float32)
    expert_ids = lax.broadcasted_iota(jnp.int32, (experts, count), 0)
    before = (
        lax.broadcasted_iota(jnp.int32, (count, count), 0)
        < lax.broadcasted_iota(jnp.int32, (count, count), 1)
    )
    before = jnp.where(before, 1.0, 0.0).astype(jnp.bfloat16)
    row_ids = lax.broadcasted_iota(jnp.int32, (rows, count), 0)
    token_pick = jnp.zeros((rows, count), jnp.float32)
    prob_pick = jnp.zeros((rows, count), jnp.float32)
    for k in range(tops):
        onehot = jnp.where(routes_ref[k : k + 1] == expert_ids, 1.0, 0.0)
        earlier = jnp.dot(onehot.astype(jnp.bfloat16), before, preferred_element_type=jnp.float32)
        row = jnp.sum(onehot * (base + earlier), axis=0, keepdims=True).astype(jnp.int32)
        hit = row_ids == row
        token_pick = token_pick + jnp.where(hit, 1.0, 0.0)
        prob_pick = prob_pick + jnp.where(hit, probs_ref[k : k + 1].astype(jnp.float32), 0.0)
        base = base + jnp.sum(onehot, axis=1, keepdims=True)
    token_pick = token_pick.astype(jnp.bfloat16)
    prob_pick = prob_pick.astype(jnp.bfloat16)
    select_ref[...] = token_pick
    piece = 512
    for at in range(0, width, piece):
        cut = slice(at, min(at + piece, width))
        for pick, source, target in (
            (token_pick, tokens_ref, token_rows_ref),
            (prob_pick, out_grad_ref, scaled_rows_ref),
        ):
            target[:, cut] = jnp.dot(
                pick, source[:, cut], preferred_element_type=jnp.float32
            ).astype(jnp.bfloat16)


def dispatch(swap_flags, routes, probs, tokens, out_grad, capacity):
    count, width = tokens.shape
    rows = swap_flags.shape[0] * capacity
    whole = pl.BlockSpec(memory_space=pltpu.VMEM)
    return pl.pallas_call(
        functools.partial(dispatch_kernel, capacity),
        in_specs=[whole] * 5,
        out_specs=[whole] * 3,
        out_shape=[
            jax.ShapeDtypeStruct((rows, width), jnp.bfloat16),
            jax.ShapeDtypeStruct((rows, width), jnp.bfloat16),
            jax.ShapeDtypeStruct((rows, count), jnp.bfloat16),
        ],
        compiler_params=pltpu.CompilerParams(vmem_limit_bytes=24 * 1024 * 1024),
        cost_estimate=pl.CostEstimate(flops=0, bytes_accessed=1024, transcendentals=0),
    )(swap_flags.reshape(-1, 1), routes.T, probs.T, tokens, out_grad)


def expert_kernel(
    steps,
    inv_model,
    inv_hidden,
    mine_ref,
    other_ref,
    mine_scaled_ref,
    other_scaled_ref,
    weight_ref,
    pair_ref,
    pair_other_ref,
    left_ref,
    pre_ref,
    back_ref,
    delta_ref,
):
    step = pl.program_id(0)
    chips, both, _ = weight_ref.shape
    local = both // 2
    rows = mine_ref.shape[0]
    contract_last = (((1,), (1,)), ((), ()))
    up = jnp.concatenate([weight_ref[i, :local] for i in range(chips)], axis=0)

    @pl.when(step == 0)
    def _():
        pre_ref[...] = jnp.zeros_like(pre_ref)
        back_ref[...] = jnp.zeros_like(back_ref)

    @pl.when(step < steps)
    def _():
        down = jnp.concatenate([weight_ref[i, local:] for i in range(chips)], axis=0)
        token = jnp.concatenate((mine_ref[...], other_ref[...]), axis=0)
        pre_ref[...] += lax.dot_general(
            up, token, contract_last, preferred_element_type=jnp.float32
        )
        scaled = jnp.concatenate((mine_scaled_ref[...], other_scaled_ref[...]), axis=0)
        back_ref[...] += lax.dot_general(
            down, scaled, contract_last, preferred_element_type=jnp.float32
        )

    @pl.when(step == steps - 1)
    def _():
        pre_act = pre_ref[...] * inv_model
        sigmoid_act = 1.0 / (1.0 + jnp.exp(-pre_act))
        delta = (
            back_ref[...] * inv_hidden * sigmoid_act * (1.0 + pre_act * (1.0 - sigmoid_act))
        ).astype(jnp.bfloat16)
        left_ref[0] = delta
        left_ref[1] = (pre_act * sigmoid_act).astype(jnp.bfloat16)
        delta_ref[...] = delta.T

    @pl.when(step >= steps)
    def _():
        pair = jnp.dot(delta_ref[...], up, preferred_element_type=jnp.float32) * inv_model
        pair_ref[...] = pair[:rows]
        pair_other_ref[...] = pair[rows:].astype(jnp.bfloat16)


def expert_stage(mine, other, mine_scaled, other_scaled, weights, inv_model, inv_hidden):
    rows, width = mine.shape
    chips, both, _ = weights.shape
    hidden = chips * both // 2
    block = 512
    steps = width // block

    def early(i):
        return jnp.minimum(i, steps - 1)

    def late(i):
        return jnp.maximum(i - steps, 0)

    row_spec = pl.BlockSpec((rows, block), lambda i: (0, early(i)))
    late_spec = pl.BlockSpec((rows, block), lambda i: (0, late(i)))
    return pl.pallas_call(
        functools.partial(expert_kernel, steps, inv_model, inv_hidden),
        grid=(2 * steps,),
        in_specs=[row_spec] * 4 + [pl.BlockSpec((chips, both, block), lambda i: (0, 0, i % steps))],
        out_specs=[
            late_spec,
            late_spec,
            pl.BlockSpec((2, hidden, 2 * rows), lambda i: (0, 0, 0)),
        ],
        out_shape=[
            jax.ShapeDtypeStruct((rows, width), jnp.float32),
            jax.ShapeDtypeStruct((rows, width), jnp.bfloat16),
            jax.ShapeDtypeStruct((2, hidden, 2 * rows), jnp.bfloat16),
        ],
        scratch_shapes=[
            pltpu.VMEM((hidden, 2 * rows), jnp.float32),
            pltpu.VMEM((hidden, 2 * rows), jnp.float32),
            pltpu.VMEM((2 * rows, hidden), jnp.bfloat16),
        ],
        compiler_params=pltpu.CompilerParams(
            dimension_semantics=("arbitrary",), vmem_limit_bytes=60 * 1024 * 1024
        ),
        cost_estimate=pl.CostEstimate(
            flops=12 * rows * hidden * width, bytes_accessed=32 * rows * width, transcendentals=0
        ),
    )(mine, other, mine_scaled, other_scaled, weights)


def weight_kernel(
    inv_model,
    inv_hidden,
    left_ref,
    mine_ref,
    other_ref,
    mine_scaled_ref,
    other_scaled_ref,
    part_ref,
):
    chips, both, _ = part_ref.shape
    local = both // 2
    for kind, mine, other, scale in (
        (0, mine_ref, other_ref, inv_model),
        (1, mine_scaled_ref, other_scaled_ref, inv_hidden),
    ):
        right = jnp.concatenate((mine[...], other[...]), axis=0)
        part = jnp.dot(left_ref[kind], right, preferred_element_type=jnp.float32) * scale
        part = part.astype(jnp.bfloat16)
        for i in range(chips):
            part_ref[i, kind * local : (kind + 1) * local] = part[i * local : (i + 1) * local]


def weight_stage(left, mine, other, mine_scaled, other_scaled, chips, inv_model, inv_hidden):
    rows, width = mine.shape
    both = 2 * left.shape[1] // chips
    block = 512
    row_spec = pl.BlockSpec((rows, block), lambda i: (0, i))
    return pl.pallas_call(
        functools.partial(weight_kernel, inv_model, inv_hidden),
        grid=(width // block,),
        in_specs=[pl.BlockSpec(left.shape, lambda i: (0, 0, 0))] + [row_spec] * 4,
        out_specs=pl.BlockSpec((chips, both, block), lambda i: (0, 0, i)),
        out_shape=jax.ShapeDtypeStruct((chips, both, width), jnp.bfloat16),
        compiler_params=pltpu.CompilerParams(
            dimension_semantics=("arbitrary",), vmem_limit_bytes=60 * 1024 * 1024
        ),
        cost_estimate=pl.CostEstimate(flops=0, bytes_accessed=1024, transcendentals=0),
    )(left, mine, other, mine_scaled, other_scaled)


def on_device(
    tokens,
    out_grad,
    routes,
    probs,
    swap_flags,
    up_weight,
    down_weight,
    up_first,
    up_second,
    down_first,
    down_second,
):
    model_width = tokens.shape[1]
    high = lax.axis_size(HIGH)
    side = lax.axis_size(SIDE)
    experts = high * side
    ring = lax.axis_size(RING)
    near = lax.axis_size(NEAR)
    chips = ring * near
    half_axis = experts // 2
    capacity = max(2, routes.size * 5 // (4 * experts))
    side_rows = high * capacity
    high_rows = side * capacity
    buffer_rows = experts * capacity
    local_hidden = up_weight.shape[1]
    hidden_units = local_hidden * chips * lax.axis_size(CORE)
    inv_model = model_width ** (-0.5)
    inv_hidden = hidden_units ** (-0.5)
    my_high = lax.axis_index(HIGH)
    my_index = my_high * side + lax.axis_index(SIDE)
    expert_ids = jnp.arange(experts, dtype=jnp.int32)
    flag_mine = jnp.sum(jnp.where(expert_ids == my_index, swap_flags, 0))
    swapped = flag_mine == 1

    weights = jnp.concatenate((up_weight[0], down_weight[0]), axis=0)
    weights_partner = partner(weights, FAR, 1)

    send_tokens, send_scaled, token_select = dispatch(
        swap_flags, routes, probs, tokens, out_grad, capacity
    )
    buffer_ids = jnp.arange(buffer_rows, dtype=jnp.int32)
    other_order = (
        (buffer_ids // capacity % high) * side_rows
        + (buffer_ids // side_rows) * capacity
        + buffer_ids % capacity
    )
    regroup = (buffer_ids[None, :] == other_order[:, None]).astype(jnp.bfloat16)

    def along_side(rows):
        return lax.all_to_all(
            rows.reshape(side, side_rows, model_width),
            SIDE,
            split_axis=0,
            concat_axis=0,
            tiled=True,
        ).reshape(buffer_rows, model_width)

    def pick(matrix, rows):
        return jnp.dot(matrix, rows, preferred_element_type=jnp.float32).astype(jnp.bfloat16)

    ways = z_routes()

    def along_high(rows, back):
        blocks = [rows[i * high_rows : (i + 1) * high_rows] for i in range(high)]
        moved = [
            lax.ppermute(
                array, (NEAR, *HIGH), [(b, a) for a, b in way] if back else way
            )
            for array, way in zip(blocks[1:], ways)
        ]
        return jnp.concatenate(blocks[:1] + moved, axis=0), moved[-1]

    token_rows = pick(regroup, along_side(send_tokens))
    side_scaled = along_side(send_scaled)
    scaled_rows = pick(regroup, side_scaled)

    rows_mine, farthest = along_high(token_rows, False)

    weights = jnp.where(swapped, weights_partner, weights)
    weights, _ = lax.optimization_barrier((weights, token_rows))
    both = jnp.stack((weights, partner(weights, NEAR, 1)), axis=0)
    both, _, _ = lax.optimization_barrier((both, side_scaled, farthest))
    gathered = lax.all_gather(both, RING, axis=0).reshape(
        chips, 2 * local_hidden, model_width
    )

    scaled_mine, _ = along_high(scaled_rows, False)
    rows_other = partner(rows_mine, CORE, 1)
    scaled_other = partner(scaled_mine, CORE, 1)
    moments = (up_first[0], up_second[0], down_first[0], down_second[0])

    rounded = tuple(array.astype(jnp.bfloat16) for array in moments)
    up_held, _ = lax.optimization_barrier((rounded[:2], scaled_mine))
    up_arrived = tuple(partner(array, FAR, 1) for array in up_held)
    pair_mine, for_other, left = expert_stage(
        rows_mine, rows_other, scaled_mine, scaled_other, gathered, inv_model, inv_hidden
    )
    parts = weight_stage(
        left, rows_mine, rows_other, scaled_mine, scaled_other, chips, inv_model, inv_hidden
    )
    from_other = partner(for_other, CORE, 1)
    pair_grad = (pair_mine + from_other.astype(jnp.float32)).astype(jnp.bfloat16)
    up_arrived, parts = lax.optimization_barrier((up_arrived, parts))
    down_held, _ = lax.optimization_barrier((rounded[2], parts))
    down_arrived = partner(down_held, FAR, 1)
    back_rows, _ = along_high(pair_grad, True)
    down_arrived, back_rows = lax.optimization_barrier((down_arrived, back_rows))
    late_held, back_rows = lax.optimization_barrier((rounded[3], back_rows))
    late_arrived = partner(late_held, FAR, 1)
    returned = along_side(pick(regroup, back_rows))
    late_arrived, returned = lax.optimization_barrier((late_arrived, returned))
    token_grad = lax.dot_general(
        token_select, returned, (((0,), (0,)), ((), ())), preferred_element_type=jnp.float32
    ).astype(jnp.bfloat16)

    own, beside = lax.psum_scatter(
        parts.reshape(ring, near, 2 * local_hidden, model_width),
        RING,
        scatter_dimension=0,
        tiled=False,
    )
    arrived = (*up_arrived, down_arrived, late_arrived)
    summed = own.astype(jnp.float32) + partner(beside, NEAR, 1).astype(jnp.float32)
    moments = tuple(
        jnp.where(swapped, new.astype(jnp.float32), old) for new, old in zip(arrived, moments)
    )
    new_up, up_first_new, up_second_new = adam_update(
        weights[:local_hidden], moments[0], moments[1], summed[:local_hidden]
    )
    new_down, down_first_new, down_second_new = adam_update(
        weights[local_hidden:], moments[2], moments[3], summed[local_hidden:]
    )
    return (
        token_grad,
        new_up[None],
        new_down[None],
        up_first_new[None],
        up_second_new[None],
        down_first_new[None],
        down_second_new[None],
    )


def solution(mesh):
    dp, expert = (mesh.shape[name] for name in ("dp", "expert"))
    fine = Mesh(
        mesh.devices.reshape(2, dp // 4, 2, 2, HIGHS // 2, expert // HIGHS),
        (NEAR, RING, CORE, *HIGH, SIDE),
    )
    rows = P((NEAR, RING, CORE, *HIGH, SIDE), None)
    slots = P((*HIGH, SIDE), (NEAR, RING, CORE), None)
    return jax.shard_map(
        on_device,
        mesh=fine,
        in_specs=(rows, rows, rows, rows, P()) + (slots,) * 6,
        out_specs=(rows,) + (slots,) * 6,
        check_vma=False,
    )
```
